256 devices in a mesh: samp: 8 (over z_hi, core), seq: 32 (over x, y, z_lo).
Axes of the slice: x: 4, y: 4, z: 8 (z_hi: 4, z_lo: 2; z = z_hi * 2 + z_lo), core: 2. Of those that a mesh axis runs over, the one named last changes fastest.
Arguments:
- atom_act: bfloat16 [16, 12288, 128], P('samp', 'seq'), may hold values from -6 to 6
- atom_gain: float32 [128], replicated, may hold values from 0.25 to 1.75
- atom_query: bfloat16 [128, 128], replicated, may hold values from -0.5 to 0.5
- atom_keyval: bfloat16 [128, 256], replicated, may hold values from -0.5 to 0.5
- atom_output: bfloat16 [128, 128], replicated, may hold values from -0.5 to 0.5
- atom_bias: bfloat16 [4, 384, 32, 128], P(None, 'seq'), may hold values from -4 to 298
- key_range: int32 [384, 2], P('seq'), may hold values from 0 to 12288, as said below
- atom_token: int32 [12288], P('seq'), may hold values from 0 to 1535, as said below
- token_counts: int32 [1536], P('seq'), may hold values from 1 to 15, as said below
- gather_weight: bfloat16 [128, 768], replicated, may hold values from -0.5 to 0.5
- token_gain: float32 [768], replicated, may hold values from 0.25 to 1.75
- token_query: bfloat16 [768, 768], replicated, may hold values from -0.21875 to 0.21875
- token_keyval: bfloat16 [768, 1536], replicated, may hold values from -0.21875 to 0.21875
- token_output: bfloat16 [768, 768], replicated, may hold values from -0.21875 to 0.21875
- pair_bias: bfloat16 [16, 1536, 1536], P('samp', 'seq'), may hold values from -4 to 298
- trans_gain: float32 [768], replicated, may hold values from 0.25 to 1.75
- trans_gate_up: bfloat16 [768, 3072], replicated, may hold values from -0.21875 to 0.21875
- trans_down: bfloat16 [1536, 768], replicated, may hold values from -0.15625 to 0.15625
- back_weight: bfloat16 [768, 128], replicated, may hold values from -0.21875 to 0.21875
Outputs:
- atom_out: bfloat16 [16, 12288, 128], P('samp', 'seq')
- token_out: bfloat16 [16, 1536, 768], P('samp', 'seq')
The draws below stay inside these ranges and needn't reach their ends.
Inputs may be any that keep to these rules, and one draw needn't show every extreme that they name: max(0, 32 * b - 48) <= key_range[b, 0] <= 32 * b and 32 * b + 32 <= key_range[b, 1] <= min(12288, 32 * b + 80). atom_token never falls along the atoms; atom a belongs to token a // 8 or a // 8 - 1. token_counts[t] is the number of atoms a with atom_token[a] = t.
All inputs are finite; a program needn't handle non-finite values.
Results may differ from the reference program's by a relative error of at most 0.025.
Values may be sent and summed in bfloat16 or wider, within the bound.
No kernel may reach another device: no remote copies, remote signals or barrier semaphores. Data moves between devices by JAX's collectives and lax.ppermute only.
A program may use at most 128 MiB of HBM per device.

```python
import math
import jax
import jax.numpy as jnp
from jax import lax

C = 128
AH = 4
D = 768
HEADS = 16
FF = 1536
WQ = 32
WK = 128
EDGE = 48
APT = 8
SAMPLES = 16
TOKENS = 1536
ATOMS = 12288
WINDOWS = 384


def spiked_bias(key, array_shape):
    key_base = jax.random.fold_in(key, 0)
    values = jnp.clip(jax.random.normal(key_base, array_shape, jnp.float32), -4.0, 4.0)
    return values


def draw_atom_bias(key, part):
    return spiked_bias(jax.random.fold_in(key, 3), (AH, WINDOWS, WQ, WK)).astype(jnp.bfloat16)


def draw_pair_bias(key, part):
    return spiked_bias(jax.random.fold_in(key, 4), (HEADS, TOKENS, TOKENS)).astype(jnp.bfloat16)


def draw_key_range(key, part):
    key_low, key_high = jax.random.split(jax.random.fold_in(key, 5))
    window = jnp.arange(WINDOWS, dtype=jnp.int32)
    window_low = jnp.maximum(0, WQ * window - EDGE + jax.random.randint(key_low, (WINDOWS,), 0, EDGE // 3 + 1, dtype=jnp.int32))
    window_high = jnp.minimum(ATOMS, WQ * window + WQ + EDGE - jax.random.randint(key_high, (WINDOWS,), 0, EDGE // 3 + 1, dtype=jnp.int32))
    return jnp.stack([window_low, window_high], axis=1).astype(jnp.int32)


def token_layout(key):
    own_key = jax.random.fold_in(key, 11)
    key_offsets, key_place = jax.random.split(own_key)
    token_index = jnp.arange(TOKENS, dtype=jnp.int32)
    offsets = jax.random.randint(key_offsets, (TOKENS,), 0, APT, dtype=jnp.int32)
    chosen_place = jax.random.randint(key_place, (), 1, TOKENS - 3, dtype=jnp.int32)
    offsets = jnp.where(token_index == chosen_place - 1, 0, offsets)
    offsets = jnp.where((token_index == chosen_place) | (token_index == chosen_place + 1), APT - 1, offsets)
    offsets = jnp.where((token_index == chosen_place + 2) | (token_index == TOKENS - 1), 0, offsets)
    previous = jnp.concatenate([jnp.zeros((1,), jnp.int32), offsets[:-1]])
    counts = (APT + offsets - previous).astype(jnp.int32)
    starts = (APT * token_index + previous).astype(jnp.int32)
    atom_owner = jnp.searchsorted(starts, jnp.arange(ATOMS, dtype=jnp.int32), side='right').astype(jnp.int32) - 1
    return (atom_owner, counts)


def draw_atom_token(key, part):
    return token_layout(key)[0]


def draw_token_counts(key, part):
    return token_layout(key)[1]


def steps_of(key, dims, cuts, smallest, high):
    factor_of = 1.0
    for dim, blocks in cuts:
        draws = jax.random.uniform(jax.random.fold_in(jax.random.fold_in(key, 6), dim), (blocks,), jnp.float32, smallest / len(cuts), high / len(cuts))
        factor_of = factor_of * jnp.repeat(jnp.exp(draws), dims[dim] // blocks).reshape((-1,) + (1,) * (len(dims) - 1 - dim))
    return factor_of


def scatter_about(stream_key, extent, deviation, reach, pieces=(), kind=jnp.bfloat16):
    loudness = steps_of(stream_key, extent, pieces, -0.22, 0.18) if pieces else 1.0
    drawn = jax.random.normal(stream_key, extent, jnp.float32) * deviation * loudness
    return jnp.minimum(jnp.maximum(drawn, -reach), reach).astype(kind)


def setup_inputs(seed: int = 0) -> dict:
    streams_of = jax.random.split(jax.random.key(seed), 20)
    return {
        "atom_act": scatter_about(streams_of[0], (SAMPLES, ATOMS, C), 1.0, 6.0, ((0, 8), (1, 32))),
        "atom_gain": jnp.clip(1.0 + 0.15 * jax.random.normal(streams_of[1], (C,), jnp.float32), 0.25, 1.75),
        "atom_query": scatter_about(streams_of[2], (C, C), C ** -0.5, 0.5),
        "atom_keyval": scatter_about(streams_of[3], (C, 2 * C), C ** -0.5, 0.5),
        "atom_output": scatter_about(streams_of[4], (C, C), C ** -0.5, 0.5),
        "atom_bias": draw_atom_bias(jax.random.fold_in(streams_of[19], 71), 0),
        "key_range": draw_key_range(jax.random.fold_in(streams_of[19], 71), 0),
        "atom_token": draw_atom_token(jax.random.fold_in(streams_of[19], 71), 0),
        "token_counts": draw_token_counts(jax.random.fold_in(streams_of[19], 71), 0),
        "gather_weight": scatter_about(streams_of[9], (C, D), C ** -0.5, 0.5),
        "token_gain": jnp.clip(1.0 + 0.15 * jax.random.normal(streams_of[10], (D,), jnp.float32), 0.25, 1.75),
        "token_query": scatter_about(streams_of[11], (D, D), D ** -0.5, 0.21875),
        "token_keyval": scatter_about(streams_of[12], (D, 2 * D), D ** -0.5, 0.21875),
        "token_output": scatter_about(streams_of[13], (D, D), D ** -0.5, 0.21875),
        "pair_bias": draw_pair_bias(jax.random.fold_in(streams_of[19], 71), 0),
        "trans_gain": jnp.clip(1.0 + 0.15 * jax.random.normal(streams_of[15], (D,), jnp.float32), 0.25, 1.75),
        "trans_gate_up": scatter_about(streams_of[16], (D, 2 * FF), D ** -0.5, 0.21875),
        "trans_down": scatter_about(streams_of[17], (FF, D), FF ** -0.5, 0.15625),
        "back_weight": scatter_about(streams_of[18], (D, C), D ** -0.5, 0.21875),
    }


EPSILON = 1e-05
NEGATIVE = -1e+30

def layer_norm(values, gain_vector):
    widened = values.astype(jnp.float32)
    centred = widened - lax.optimization_barrier(jnp.mean(widened, axis=-1, keepdims=True))
    variance = lax.optimization_barrier(jnp.mean(centred * centred, axis=-1, keepdims=True))
    return (centred * lax.rsqrt(variance + EPSILON) * gain_vector).astype(jnp.bfloat16)

def softmax_rows(scores):
    maxima = lax.optimization_barrier(jnp.max(scores, axis=-1, keepdims=True))
    exponent = jnp.exp(scores - maxima)
    return exponent / lax.optimization_barrier(jnp.sum(exponent, axis=-1, keepdims=True))

def reference(atom_act, atom_gain, atom_query, atom_keyval, atom_output, atom_bias, key_range, atom_token, token_counts, gather_weight, token_gain, token_query, token_keyval, token_output, pair_bias, trans_gain, trans_gate_up, trans_down, back_weight):
    head_width = C // AH
    head_size = D // HEADS
    atom_scale = 1.0 / math.sqrt(head_width)
    token_scale = 1.0 / math.sqrt(head_size)
    window_number = jnp.arange(WINDOWS, dtype=jnp.int32)
    position = WQ * window_number[:, None] - EDGE + jnp.arange(WK, dtype=jnp.int32)[None, :]
    key_valid = (position >= key_range[:, 0:1]) & (position < key_range[:, 1:2])
    bias_atoms = atom_bias.astype(jnp.float32)
    count_column = token_counts.astype(jnp.float32)[:, None]

    def one_sample(sample_act):
        normed = layer_norm(sample_act, atom_gain)
        queries = jnp.dot(normed, atom_query, preferred_element_type=jnp.float32).astype(jnp.bfloat16)
        keyvals = jnp.dot(normed, atom_keyval, preferred_element_type=jnp.float32).astype(jnp.bfloat16)
        padded = jnp.pad(keyvals, ((EDGE, EDGE), (0, 0)))
        blocks = padded.reshape(WINDOWS + 2 * EDGE // WQ, WQ, 2 * C)
        window_keys = jnp.concatenate([blocks[offset:offset + WINDOWS] for offset in range(WK // WQ)], axis=1)
        key_part = window_keys[..., :C].reshape(WINDOWS, WK, AH, head_width).astype(jnp.float32)
        value_part = window_keys[..., C:].reshape(WINDOWS, WK, AH, head_width).astype(jnp.float32)
        query_part = queries.reshape(WINDOWS, WQ, AH, head_width).astype(jnp.float32)
        scores = jnp.einsum('wqhd,wkhd->hwqk', query_part, key_part) * atom_scale + bias_atoms
        scores = jnp.where(key_valid[None, :, None, :], scores, NEGATIVE)
        weights = softmax_rows(scores).astype(jnp.bfloat16).astype(jnp.float32)
        attended = jnp.einsum('hwqk,wkhd->wqhd', weights, value_part).astype(jnp.bfloat16).reshape(ATOMS, C)
        atom_mid = (sample_act.astype(jnp.float32) + jnp.dot(attended, atom_output, preferred_element_type=jnp.float32)).astype(jnp.bfloat16)
        hidden_atoms = jax.nn.relu(jnp.dot(atom_mid, gather_weight, preferred_element_type=jnp.float32)).astype(jnp.bfloat16)
        sums = jax.ops.segment_sum(hidden_atoms.astype(jnp.float32), atom_token, num_segments=TOKENS)
        token_act = (sums / count_column).astype(jnp.bfloat16)
        token_norm = layer_norm(token_act, token_gain)
        token_queries = jnp.dot(token_norm, token_query, preferred_element_type=jnp.float32).astype(jnp.bfloat16)
        token_keyvals = jnp.dot(token_norm, token_keyval, preferred_element_type=jnp.float32).astype(jnp.bfloat16)
        query_heads = token_queries.reshape(TOKENS, HEADS, head_size).transpose(1, 0, 2)
        key_heads = token_keyvals[:, :D].reshape(TOKENS, HEADS, head_size).transpose(1, 0, 2)
        value_heads = token_keyvals[:, D:].reshape(TOKENS, HEADS, head_size).transpose(1, 0, 2)

        def one_head(operands):
            query_one, key_one, value_one, bias_one = operands
            head_scores = jnp.dot(query_one, key_one.T, preferred_element_type=jnp.float32) * token_scale + bias_one.astype(jnp.float32)
            head_weights = softmax_rows(head_scores).astype(jnp.bfloat16)
            return jnp.dot(head_weights, value_one, preferred_element_type=jnp.float32)
        head_out = lax.map(one_head, (query_heads, key_heads, value_heads, pair_bias))
        merged = head_out.astype(jnp.bfloat16).transpose(1, 0, 2).reshape(TOKENS, D)
        token_mid = (token_act.astype(jnp.float32) + jnp.dot(merged, token_output, preferred_element_type=jnp.float32)).astype(jnp.bfloat16)
        trans_norm = layer_norm(token_mid, trans_gain)
        gate_up = jnp.dot(trans_norm, trans_gate_up, preferred_element_type=jnp.float32)
        hidden = (jax.nn.silu(gate_up[:, :FF]) * gate_up[:, FF:]).astype(jnp.bfloat16)
        token_out = (token_mid.astype(jnp.float32) + jnp.dot(hidden, trans_down, preferred_element_type=jnp.float32)).astype(jnp.bfloat16)
        back_rows = jnp.dot(token_out, back_weight, preferred_element_type=jnp.float32).astype(jnp.bfloat16)
        atom_out = (atom_mid.astype(jnp.float32) + back_rows[atom_token].astype(jnp.float32)).astype(jnp.bfloat16)
        return (atom_out, token_out)
    atom_out, token_out = lax.map(one_sample, atom_act)
    return (atom_out, token_out)
```

```python
import functools
import math

import jax
import jax.numpy as jnp
from jax import lax
from jax.experimental import pallas as pl
from jax.experimental.pallas import tpu as pltpu
from jax.sharding import PartitionSpec as P

AH = 4
HEADS = 16
WQ = 32
WK = 128
EDGE = 48
APT = 8
BEFORE = EDGE
AFTER = WQ + EDGE
META = 16
GROUP = 8

EPSILON = 1e-05
NEGATIVE = -1e30
F32 = jnp.float32
BF16 = jnp.bfloat16

NT = (((1,), (1,)), ((), ()))
TN = (((0,), (0,)), ((), ()))


def dot(a, b):
    return jnp.dot(a, b, preferred_element_type=F32)


def dot_nt(a, b):
    return lax.dot_general(a, b, NT, preferred_element_type=F32)


def dot_tn(a, b):
    return lax.dot_general(a, b, TN, preferred_element_type=F32)


def layer_norm(widened, gain):
    centred = widened - jnp.mean(widened, axis=-1, keepdims=True)
    variance = jnp.mean(centred * centred, axis=-1, keepdims=True)
    return (centred * lax.rsqrt(variance + EPSILON) * gain).astype(BF16)


def lane_group(rows, lanes, width):
    return lax.broadcasted_iota(jnp.int32, (rows, lanes), 1) // width


def atom_kernel(
    range_ref,
    act_ref,
    before_ref,
    after_ref,
    gain_ref,
    query_ref,
    keyval_ref,
    output_ref,
    bias_ref,
    token_ref,
    gather_ref,
    token_gain_ref,
    mid_ref,
    tokact_ref,
    norm_ref,
    att_ref,
):
    samples, atoms, channels = act_ref.shape
    windows = atoms // WQ
    tokens = norm_ref.shape[1]
    head_width = channels // AH
    scale = 1.0 / math.sqrt(head_width)
    device = lax.axis_index("seq")
    gain = gain_ref[...]
    bias_at = samples * AFTER
    meta_at = bias_at + AH * WQ

    head_of = lane_group(WQ, channels, head_width)
    masks = [(head_of == h).astype(BF16) for h in range(AH)]
    masks32 = [(head_of == h).astype(F32) for h in range(AH)]
    index = lax.broadcasted_iota(jnp.int32, (1, WK), 1)

    meta = after_ref[meta_at : meta_at + META, :].astype(F32)
    indexf = index.astype(F32)
    valid_after = (indexf >= meta[0:1, :]) & (indexf < meta[1:2, :])

    slot = token_ref[...] - device * tokens
    rows = lax.broadcasted_iota(jnp.int32, (tokens, atoms), 0)
    own_table = (rows == slot).astype(BF16)
    lane = lax.broadcasted_iota(jnp.int32, (tokens, WQ), 1)
    back_step = meta[2:3, :WQ] > 0.5
    after_table = (
        (lax.broadcasted_iota(jnp.int32, (tokens, WQ), 0) == tokens - 1) & (lane < APT) & back_step
    ).astype(BF16)
    counts = jnp.sum(own_table.astype(F32), axis=1, keepdims=True) + jnp.sum(
        after_table.astype(F32), axis=1, keepdims=True
    )
    counts = jnp.maximum(counts, 1.0)

    for s in range(samples):
        own = act_ref[s]
        extended = jnp.concatenate(
            [
                before_ref[s * BEFORE : (s + 1) * BEFORE, :],
                own,
                after_ref[s * AFTER : (s + 1) * AFTER, :],
            ],
            axis=0,
        ).astype(F32)
        normed = layer_norm(extended, gain)
        queries = dot(normed, query_ref[...]).astype(BF16)
        keyvals = dot(normed, keyval_ref[...]).astype(BF16)
        for w in range(windows + 1):
            q = queries[BEFORE + WQ * w : BEFORE + WQ * (w + 1), :]
            keys = keyvals[WQ * w : WQ * w + WK, :channels]
            values = keyvals[WQ * w : WQ * w + WK, channels:]
            stacked = jnp.concatenate([q * m for m in masks], axis=0)
            scores = dot_nt(stacked, keys) * scale
            if w < windows:
                bias = bias_ref[:, w].reshape(AH * WQ, WK)
                start = (device * windows + w) * WQ - EDGE
                valid = (index >= range_ref[w, 0] - start) & (index < range_ref[w, 1] - start)
            else:
                bias = after_ref[bias_at : bias_at + AH * WQ, :]
                valid = valid_after
            scores = jnp.where(valid, scores + bias.astype(F32), NEGATIVE)
            exponent = jnp.exp(scores - jnp.max(scores, axis=-1, keepdims=True))
            weights = exponent / jnp.sum(exponent, axis=-1, keepdims=True)
            mixed = dot(weights.astype(BF16), values)
            attended = mixed[:WQ] * masks32[0]
            for h in range(1, AH):
                attended = attended + mixed[WQ * h : WQ * (h + 1)] * masks32[h]
            att_ref[WQ * w : WQ * (w + 1), :] = attended.astype(BF16)
        merged = dot(att_ref[...], output_ref[...])
        mid = (extended[BEFORE : BEFORE + atoms + WQ, :] + merged).astype(BF16)
        mid_ref[s] = mid[:atoms]
        hidden = jnp.maximum(dot(mid, gather_ref[...]), 0.0).astype(BF16)
        sums = dot(own_table, hidden[:atoms]) + dot(after_table, hidden[atoms:])
        token_act = (sums / counts).astype(BF16)
        tokact_ref[s] = token_act
        norm_ref[s] = layer_norm(token_act.astype(F32), token_gain_ref[...])


def vmem():
    return pl.BlockSpec(memory_space=pltpu.VMEM)


def smem():
    return pl.BlockSpec(memory_space=pltpu.SMEM)


def anywhere():
    return pl.BlockSpec(memory_space=pl.ANY)


def run_atoms(key_range, act, before, after, *rest):
    samples, atoms, channels = act.shape
    width = rest[-2].shape[1]
    tokens = atoms // APT
    return pl.pallas_call(
        atom_kernel,
        out_shape=(
            jax.ShapeDtypeStruct((samples, atoms, channels), BF16),
            jax.ShapeDtypeStruct((samples, tokens, width), BF16),
            jax.ShapeDtypeStruct((samples, tokens, width), BF16),
        ),
        in_specs=[smem()] + [vmem()] * (3 + len(rest)),
        out_specs=(vmem(),) * 3,
        scratch_shapes=[pltpu.VMEM((atoms + WQ, channels), BF16)],
        compiler_params=pltpu.CompilerParams(vmem_limit_bytes=24 * 2**20),
        cost_estimate=pl.CostEstimate(
            flops=800_000_000, bytes_accessed=4_000_000, transcendentals=500_000
        ),
        name="atoms",
    )(key_range, act, before, after, *rest)


def block_rows(dx, dy, dz, rows):
    device = lax.axis_index("seq")
    x, y, z = device // 8, (device // 2) % 4, device % 2
    source = ((x + dx) % 4) * 8 + ((y + dy) % 4) * 2 + (z + dz) % 2
    return source * rows


def token_kernel(plan, pieces, *refs):
    parts = refs[:pieces]
    (
        bias_ref,
        norm_ref,
        tokact_ref,
        mid_ref,
        token_ref,
        gain_ref,
        query_hbm,
        keyval_hbm,
        output_hbm,
        gate_hbm,
        down_hbm,
        back_hbm,
        atom_out_ref,
        token_out_ref,
        back_rows_ref,
        all_ref,
        query_ref,
        keyval_ref,
        output_ref,
        gate_ref,
        down_ref,
        back_ref,
        att_ref,
        weight_sems,
        part_sems,
    ) = refs[pieces:]
    samples, tokens, width = norm_ref.shape
    head_size = width // HEADS
    scale = 1.0 / math.sqrt(head_size)
    device = lax.axis_index("seq")

    weight_copies = []
    for i, (source, target) in enumerate(
        (
            (query_hbm, query_ref),
            (keyval_hbm, keyval_ref),
            (output_hbm, output_ref),
            (gate_hbm, gate_ref),
            (down_hbm, down_ref),
            (back_hbm, back_ref),
        )
    ):
        copy = pltpu.make_async_copy(source, target, weight_sems.at[i])
        copy.start()
        weight_copies.append(copy)
    part_copies = []
    for i, (part, at, sample, offset) in enumerate(plan):
        target = pl.multiple_of(block_rows(*offset, tokens), 16)
        copy = pltpu.make_async_copy(
            parts[part].at[at : at + tokens],
            all_ref.at[sample, pl.ds(target, tokens)],
            part_sems.at[i],
        )
        copy.start()
        part_copies.append(copy)

    weight_copies[0].wait()
    norm = norm_ref[...].reshape(samples * tokens, width)
    queries = dot(norm, query_ref[...]).astype(BF16)
    weight_copies[1].wait()
    lanes = GROUP * head_size
    head_of = lane_group(tokens, lanes, head_size)
    masks = [(head_of == h).astype(BF16) for h in range(GROUP)]
    masks32 = [(head_of == h).astype(F32) for h in range(GROUP)]
    for copy in part_copies:
        copy.wait()
    for s in range(samples):
        for g in range(HEADS // GROUP):
            columns = slice(lanes * g, lanes * (g + 1))
            q = queries[tokens * s : tokens * (s + 1), columns]
            stacked = jnp.concatenate([q * m for m in masks], axis=0)
            absorbed = (dot_nt(stacked, keyval_ref[:, columns]) * scale).astype(BF16)
            scores = dot_nt(absorbed, all_ref[s])
            bias = bias_ref[GROUP * g : GROUP * (g + 1)].reshape(GROUP * tokens, -1)
            scores = scores + bias.astype(F32)
            exponent = jnp.exp(scores - jnp.max(scores, axis=-1, keepdims=True))
            total = jnp.sum(exponent, axis=-1, keepdims=True)
            mixed = dot(exponent.astype(BF16), all_ref[s]) / total
            value_at = slice(width + lanes * g, width + lanes * (g + 1))
            valued = dot(mixed.astype(BF16), keyval_ref[:, value_at])
            attended = valued[:tokens] * masks32[0]
            for h in range(1, GROUP):
                attended = attended + valued[tokens * h : tokens * (h + 1)] * masks32[h]
            att_ref[tokens * s : tokens * (s + 1), columns] = attended.astype(BF16)

    weight_copies[2].wait()
    merged = dot(att_ref[...], output_ref[...])
    token_act = tokact_ref[...].reshape(samples * tokens, width).astype(F32)
    token_mid = (token_act + merged).astype(BF16).astype(F32)
    trans = layer_norm(token_mid, gain_ref[...])
    weight_copies[3].wait()
    hidden_width = down_ref.shape[0]
    gate = dot(trans, gate_ref[:, :hidden_width])
    up = dot(trans, gate_ref[:, hidden_width:])
    hidden = (gate / (1.0 + jnp.exp(-gate)) * up).astype(BF16)
    weight_copies[4].wait()
    token_out = (token_mid + dot(hidden, down_ref[...])).astype(BF16)
    token_out_ref[...] = token_out.reshape(samples, tokens, width)
    weight_copies[5].wait()
    back_rows = dot(token_out, back_ref[...]).astype(BF16)
    back_rows_ref[...] = back_rows.reshape(samples, tokens, -1)
    atoms = mid_ref.shape[1]
    slot = token_ref[...] - device * tokens
    table = (lax.broadcasted_iota(jnp.int32, (tokens, atoms), 0) == slot).astype(BF16)
    for s in range(samples):
        gathered = dot_tn(table, back_rows[tokens * s : tokens * (s + 1)])
        atom_out_ref[s] = (mid_ref[s].astype(F32) + gathered).astype(BF16)


def run_tokens(plan, parts, bias, norm, tokact, mid, token, gain, weights):
    samples, tokens, width = norm.shape
    return pl.pallas_call(
        functools.partial(token_kernel, plan, len(parts)),
        out_shape=(
            jax.ShapeDtypeStruct(mid.shape, BF16),
            jax.ShapeDtypeStruct(norm.shape, BF16),
            jax.ShapeDtypeStruct((samples, tokens, mid.shape[2]), BF16),
        ),
        in_specs=[anywhere()] * len(parts) + [vmem()] * 6 + [anywhere()] * 6,
        out_specs=(vmem(),) * 3,
        scratch_shapes=[pltpu.VMEM((samples, bias.shape[2], width), BF16)]
        + [pltpu.VMEM(w.shape, w.dtype) for w in weights]
        + [
            pltpu.VMEM((samples * tokens, width), BF16),
            pltpu.SemaphoreType.DMA((len(weights),)),
            pltpu.SemaphoreType.DMA((len(plan),)),
        ],
        compiler_params=pltpu.CompilerParams(vmem_limit_bytes=52 * 2**20),
        cost_estimate=pl.CostEstimate(
            flops=10_000_000_000, bytes_accessed=20_000_000, transcendentals=3_000_000
        ),
        name="tokens",
    )(*parts, bias, norm, tokact, mid, token, gain, *weights)


def shifted(value, dx, dy, dz=0):
    pairs = []
    for t in range(32):
        x, y, z = t // 8, (t // 2) % 4, t % 2
        pairs.append((t, ((x + dx) % 4) * 8 + ((y + dy) % 4) * 2 + (z + dz) % 2))
    return lax.ppermute(value, "seq", pairs)


def ring(value, dx, dy):
    half = value.shape[0] // 2
    low = shifted(value, dx, dy)
    high = shifted(value, -dx, -dy)
    far_low = shifted(low[:half], dx, dy)
    far_high = shifted(high[half:], -dx, -dy)
    return [value, low, high, far_low, far_high]


def spread(norm):
    samples, tokens, _ = norm.shape
    other = shifted(norm, 0, 0, 1)
    parts, plan = [], []
    for s in range(samples):
        dx, dy = (1, 0) if s % 2 == 0 else (0, 1)
        first = jnp.concatenate([norm[s], other[s]], axis=0)
        line = ring(first, dx, dy)
        steps = (0, 0, -1, -1, 1, 1, 2, 2)
        plane = ring(jnp.concatenate(line, axis=0), dy, dx)
        base = len(parts)
        parts += plane
        for piece, (value, far) in enumerate(zip(plane, (0, -1, 1, 2, 2))):
            skip = 4 if piece == 4 else 0
            for k in range(value.shape[0] // tokens):
                near = steps[k + skip]
                offset = (near * dx + far * dy, near * dy + far * dx, (k + skip) % 2)
                plan.append((base + piece, k * tokens, s, offset))
    return parts, plan


def per_device(
    atom_act,
    atom_gain,
    atom_query,
    atom_keyval,
    atom_output,
    atom_bias,
    key_range,
    atom_token,
    token_counts,
    gather_weight,
    token_gain,
    token_query,
    token_keyval,
    token_output,
    pair_bias,
    trans_gain,
    trans_gate_up,
    trans_down,
    back_weight,
):
    samples, atoms, channels = atom_act.shape
    tokens = token_counts.shape[0]
    device = lax.axis_index("seq")
    count = lax.axis_size("seq")
    to_next = [(i, i + 1) for i in range(count - 1)]
    to_previous = [(i + 1, i) for i in range(count - 1)]

    first_start = device * atoms - EDGE
    meta = jnp.zeros((META, channels), F32)
    meta = meta.at[0].set((key_range[0, 0] - first_start).astype(F32))
    meta = meta.at[1].set((key_range[0, 1] - first_start).astype(F32))
    step = (device * atoms + jnp.arange(WQ, dtype=jnp.int32)) // APT - atom_token[:WQ]
    meta = meta.at[2, :WQ].set(step.astype(F32))
    packed = jnp.concatenate(
        [
            atom_act[:, :AFTER].reshape(samples * AFTER, channels),
            atom_bias[:, 0].reshape(AH * WQ, WK),
            meta.astype(BF16),
        ],
        axis=0,
    )
    after = lax.ppermute(packed, "seq", to_previous)
    before = lax.ppermute(
        atom_act[:, atoms - BEFORE :].reshape(samples * BEFORE, channels), "seq", to_next
    )
    all_bias = lax.all_gather(pair_bias, "samp", axis=0, tiled=True)
    token_row = atom_token.reshape(1, atoms)
    atom_mid, token_act, token_norm = run_atoms(
        key_range,
        atom_act,
        before,
        after,
        atom_gain.reshape(1, -1),
        atom_query,
        atom_keyval,
        atom_output,
        atom_bias,
        token_row,
        gather_weight,
        token_gain.reshape(1, -1),
    )
    parts, plan = spread(token_norm)
    atom_out, token_out, back_rows = run_tokens(
        plan,
        parts,
        all_bias,
        token_norm,
        token_act,
        atom_mid,
        token_row,
        trans_gain.reshape(1, -1),
        [token_query, token_keyval, token_output, trans_gate_up, trans_down, back_weight],
    )
    previous = lax.ppermute(back_rows[:, tokens - 1], "seq", to_next)
    earlier = (atom_token[:APT] < device * tokens)[None, :, None]
    extra = jnp.where(earlier, previous[:, None, :].astype(F32), 0.0)
    head = (atom_out[:, :APT].astype(F32) + extra).astype(BF16)
    atom_out = lax.dynamic_update_slice(atom_out, head, (0, 0, 0))
    return (atom_out, token_out)


def solution(mesh):
    placed = (
        P("samp", "seq", None),
        P(),
        P(),
        P(),
        P(),
        P(None, "seq", None, None),
        P("seq", None),
        P("seq"),
        P("seq"),
        P(),
        P(),
        P(),
        P(),
        P(),
        P("samp", "seq", None),
        P(),
        P(),
        P(),
        P(),
    )
    return jax.shard_map(
        per_device,
        mesh=mesh,
        in_specs=placed,
        out_specs=(P("samp", "seq", None), P("samp", "seq", None)),
        check_vma=False,
    )
```

```python
import functools
import math

import jax
import jax.numpy as jnp
from jax import lax
from jax.experimental import pallas as pl
from jax.experimental.pallas import tpu as pltpu
from jax.sharding import PartitionSpec as P

AH = 4
HEADS = 16
WQ = 32
WK = 128
EDGE = 48
APT = 8
BEFORE = EDGE
AFTER = WQ + EDGE
META = 16
GROUP = 8

EPSILON = 1e-05
NEGATIVE = -1e30
F32 = jnp.float32
BF16 = jnp.bfloat16

NT = (((1,), (1,)), ((), ()))
TN = (((0,), (0,)), ((), ()))


def dot(a, b):
    return jnp.dot(a, b, preferred_element_type=F32)


def dot_nt(a, b):
    return lax.dot_general(a, b, NT, preferred_element_type=F32)


def dot_tn(a, b):
    return lax.dot_general(a, b, TN, preferred_element_type=F32)


def layer_norm(widened, gain):
    centred = widened - jnp.mean(widened, axis=-1, keepdims=True)
    variance = jnp.mean(centred * centred, axis=-1, keepdims=True)
    return (centred * lax.rsqrt(variance + EPSILON) * gain).astype(BF16)


def lane_group(rows, lanes, width):
    return lax.broadcasted_iota(jnp.int32, (rows, lanes), 1) // width


def pack_kernel(range_ref, act_hbm, bias_hbm, first_ref, last_ref, sems):
    samples, atoms, _ = act_hbm.shape
    bias_at = samples * AFTER
    meta_at = bias_at + AH * WQ
    copies = []
    for s in range(samples):
        copies.append((act_hbm.at[s, :AFTER], first_ref.at[AFTER * s : AFTER * (s + 1)]))
        copies.append((act_hbm.at[s, atoms - BEFORE :], last_ref.at[BEFORE * s : BEFORE * (s + 1)]))
    for h in range(AH):
        copies.append((bias_hbm.at[h, 0], first_ref.at[bias_at + WQ * h : bias_at + WQ * (h + 1)]))
    started = []
    for i, (source, target) in enumerate(copies):
        copy = pltpu.make_async_copy(source, target, sems.at[i])
        copy.start()
        started.append(copy)
    start = lax.axis_index("seq") * atoms - EDGE
    row = lax.broadcasted_iota(jnp.int32, (META, WK), 0)
    meta = jnp.where(row == 0, range_ref[0, 0] - start, range_ref[0, 1] - start)
    first_ref[meta_at : meta_at + META, :] = meta.astype(F32).astype(BF16)
    for copy in started:
        copy.wait()


def run_pack(key_range, act, bias):
    samples, _, channels = act.shape
    return pl.pallas_call(
        pack_kernel,
        out_shape=(
            jax.ShapeDtypeStruct((samples * AFTER + AH * WQ + META, channels), BF16),
            jax.ShapeDtypeStruct((samples * BEFORE, channels), BF16),
        ),
        in_specs=[smem(), anywhere(), anywhere()],
        out_specs=(vmem(), vmem()),
        scratch_shapes=[pltpu.SemaphoreType.DMA((2 * samples + AH,))],
        compiler_params=pltpu.CompilerParams(vmem_limit_bytes=60 * 2**20),
        name="pack",
    )(key_range, act, bias)


def atom_kernel(
    range_ref,
    count_ref,
    before_ref,
    after_ref,
    gain_ref,
    token_ref,
    token_gain_ref,
    act_hbm,
    query_hbm,
    keyval_hbm,
    bias_hbm,
    output_hbm,
    gather_hbm,
    mid_ref,
    tokact_ref,
    norm_ref,
    act_ref,
    query_ref,
    keyval_ref,
    bias_ref,
    output_ref,
    gather_ref,
    att_ref,
    sems,
):
    copies = []
    for i, (source, target) in enumerate(
        (
            (act_hbm, act_ref),
            (query_hbm, query_ref),
            (keyval_hbm, keyval_ref),
            (bias_hbm, bias_ref),
            (output_hbm, output_ref),
            (gather_hbm, gather_ref),
        )
    ):
        copy = pltpu.make_async_copy(source, target, sems.at[i])
        copy.start()
        copies.append(copy)
    samples, atoms, channels = act_ref.shape
    windows = atoms // WQ
    tokens = norm_ref.shape[1]
    head_width = channels // AH
    scale = 1.0 / math.sqrt(head_width)
    device = lax.axis_index("seq")
    gain = gain_ref[...]
    bias_at = samples * AFTER
    meta_at = bias_at + AH * WQ

    head_of = lane_group(WQ, channels, head_width)
    masks = [(head_of == h).astype(BF16) for h in range(AH)]
    masks32 = [(head_of == h).astype(F32) for h in range(AH)]
    index = lax.broadcasted_iota(jnp.int32, (1, WK), 1)

    meta = after_ref[meta_at : meta_at + META, :].astype(F32)
    indexf = index.astype(F32)
    valid_after = (indexf >= meta[0:1, :]) & (indexf < meta[1:2, :])

    slot = token_ref[...] - device * tokens
    own_table = (lax.broadcasted_iota(jnp.int32, (tokens, atoms), 0) == slot).astype(F32)
    own_counts = jnp.sum(own_table, axis=1, keepdims=True)
    own_table = own_table.astype(BF16)
    row = lax.broadcasted_iota(jnp.int32, (tokens, 1), 0)
    remaining = jnp.where(
        row == tokens - 1, count_ref[tokens - 1].astype(F32) - own_counts, jnp.zeros_like(own_counts)
    )
    lane = lax.broadcasted_iota(jnp.int32, (tokens, WQ), 1).astype(F32)
    after_table = (lane < remaining).astype(BF16)
    counts = jnp.maximum(own_counts + remaining, 1.0)

    for copy in copies[:4]:
        copy.wait()
    for s in range(samples):
        extended = jnp.concatenate(
            [
                before_ref[s * BEFORE : (s + 1) * BEFORE, :],
                act_ref[s],
                after_ref[s * AFTER : (s + 1) * AFTER, :],
            ],
            axis=0,
        ).astype(F32)
        normed = layer_norm(extended, gain)
        queries = dot(normed, query_ref[...]).astype(BF16)
        keyvals = dot(normed, keyval_ref[...]).astype(BF16)
        for w in range(windows + 1):
            q = queries[BEFORE + WQ * w : BEFORE + WQ * (w + 1), :]
            keys = keyvals[WQ * w : WQ * w + WK, :channels]
            values = keyvals[WQ * w : WQ * w + WK, channels:]
            stacked = jnp.concatenate([q * m for m in masks], axis=0)
            scores = dot_nt(stacked, keys) * scale
            if w < windows:
                bias = bias_ref[:, w].reshape(AH * WQ, WK)
                start = (device * windows + w) * WQ - EDGE
                valid = (index >= range_ref[w, 0] - start) & (index < range_ref[w, 1] - start)
            else:
                bias = after_ref[bias_at : bias_at + AH * WQ, :]
                valid = valid_after
            scores = jnp.where(valid, scores + bias.astype(F32), NEGATIVE)
            exponent = jnp.exp(scores - jnp.max(scores, axis=-1, keepdims=True))
            total = jnp.sum(exponent, axis=-1, keepdims=True)
            mixed = dot(exponent.astype(BF16), values) / total
            attended = mixed[:WQ] * masks32[0]
            for h in range(1, AH):
                attended = attended + mixed[WQ * h : WQ * (h + 1)] * masks32[h]
            att_ref[s, WQ * w : WQ * (w + 1), :] = attended.astype(BF16)
        if s == 0:
            copies[4].wait()
            copies[5].wait()
        merged = dot(att_ref[s], output_ref[...])
        mid = (extended[BEFORE : BEFORE + atoms + WQ, :] + merged).astype(BF16)
        mid_ref[s] = mid[:atoms]
        hidden = jnp.maximum(dot(mid, gather_ref[...]), 0.0).astype(BF16)
        sums = dot(own_table, hidden[:atoms]) + dot(after_table, hidden[atoms:])
        token_act = (sums / counts).astype(BF16)
        tokact_ref[s] = token_act
        norm_ref[s] = layer_norm(token_act.astype(F32), token_gain_ref[...])


def vmem():
    return pl.BlockSpec(memory_space=pltpu.VMEM)


def smem():
    return pl.BlockSpec(memory_space=pltpu.SMEM)


def anywhere():
    return pl.BlockSpec(memory_space=pl.ANY)


def run_atoms(key_range, counts, before, after, gain, token, token_gain, *arrays):
    samples, atoms, channels = arrays[0].shape
    width = arrays[-1].shape[1]
    tokens = atoms // APT
    return pl.pallas_call(
        atom_kernel,
        out_shape=(
            jax.ShapeDtypeStruct((samples, atoms, channels), BF16),
            jax.ShapeDtypeStruct((samples, tokens, width), BF16),
            jax.ShapeDtypeStruct((samples, tokens, width), BF16),
        ),
        in_specs=[smem()] * 2 + [vmem()] * 5 + [anywhere()] * len(arrays),
        out_specs=(vmem(),) * 3,
        scratch_shapes=[pltpu.VMEM(a.shape, a.dtype) for a in arrays]
        + [
            pltpu.VMEM((samples, atoms + WQ, channels), BF16),
            pltpu.SemaphoreType.DMA((len(arrays),)),
        ],
        compiler_params=pltpu.CompilerParams(vmem_limit_bytes=60 * 2**20),
        cost_estimate=pl.CostEstimate(
            flops=800_000_000, bytes_accessed=4_000_000, transcendentals=500_000
        ),
        name="atoms",
    )(key_range, counts, before, after, gain, token, token_gain, *arrays)


def block_rows(dx, dy, dz, rows):
    device = lax.axis_index("seq")
    x, y, z = device // 8, (device // 2) % 4, device % 2
    source = ((x + dx) % 4) * 8 + ((y + dy) % 4) * 2 + (z + dz) % 2
    return source * rows


def query_kernel(norm_ref, query_hbm, keyval_hbm, absorbed_ref, query_ref, key_ref, sems):
    samples, tokens, width = norm_ref.shape
    first = pltpu.make_async_copy(query_hbm, query_ref, sems.at[0])
    second = pltpu.make_async_copy(keyval_hbm.at[:, :width], key_ref, sems.at[1])
    first.start()
    second.start()
    head_size = width // HEADS
    scale = 1.0 / math.sqrt(head_size)
    lanes = GROUP * head_size
    head_of = lane_group(tokens, lanes, head_size)
    masks = [(head_of == h).astype(BF16) for h in range(GROUP)]
    first.wait()
    queries = dot(norm_ref[...].reshape(samples * tokens, width), query_ref[...]).astype(BF16)
    second.wait()
    for s in range(samples):
        for g in range(HEADS // GROUP):
            columns = slice(lanes * g, lanes * (g + 1))
            q = queries[tokens * s : tokens * (s + 1), columns]
            stacked = jnp.concatenate([q * m for m in masks], axis=0)
            absorbed = dot_nt(stacked, key_ref[:, columns]) * scale
            absorbed_ref[s, lanes * g : lanes * (g + 1)] = absorbed.astype(BF16)


def run_queries(norm, token_query, token_keyval):
    samples, tokens, width = norm.shape
    return pl.pallas_call(
        query_kernel,
        out_shape=jax.ShapeDtypeStruct((samples, HEADS * tokens, width), BF16),
        in_specs=[vmem(), anywhere(), anywhere()],
        out_specs=vmem(),
        scratch_shapes=[
            pltpu.VMEM((width, width), BF16),
            pltpu.VMEM((width, width), BF16),
            pltpu.SemaphoreType.DMA((2,)),
        ],
        compiler_params=pltpu.CompilerParams(vmem_limit_bytes=30 * 2**20),
        cost_estimate=pl.CostEstimate(
            flops=2_000_000_000, bytes_accessed=5_000_000, transcendentals=0
        ),
        name="queries",
    )(norm, token_query, token_keyval)


def token_kernel(plan, bias_plan, pieces, *refs):
    parts = refs[:pieces]
    (
        bias_near_hbm,
        bias_far_hbm,
        absorbed_ref,
        tokact_ref,
        mid_ref,
        token_ref,
        gain_ref,
        keyval_hbm,
        output_hbm,
        gate_hbm,
        down_hbm,
        back_hbm,
        atom_out_ref,
        token_out_ref,
        back_rows_ref,
        all_ref,
        bias_ref,
        value_ref,
        output_ref,
        gate_ref,
        down_ref,
        back_ref,
        att_ref,
        weight_sems,
        part_sems,
        bias_sems,
    ) = refs[pieces:]
    samples, tokens, width = tokact_ref.shape
    head_size = width // HEADS
    device = lax.axis_index("seq")
    mine = lax.axis_index("samp")

    part_copies = []
    for i, (part, at, sample, offset) in enumerate(plan):
        target = pl.multiple_of(block_rows(*offset, tokens), 16)
        copy = pltpu.make_async_copy(
            parts[part].at[at : at + tokens],
            all_ref.at[sample, pl.ds(target, tokens)],
            part_sems.at[i],
        )
        copy.start()
        part_copies.append(copy)
    bias_copies = []
    for i, (near, at, hop) in enumerate(bias_plan):
        source = (mine // 2 + hop) % 4 * 2 + (mine % 2 if near else 1 - mine % 2)
        heads = bias_ref.shape[0] // len(bias_plan)
        copy = pltpu.make_async_copy(
            (bias_near_hbm if near else bias_far_hbm).at[at],
            bias_ref.at[pl.ds(source * heads, heads)],
            bias_sems.at[i],
        )
        copy.start()
        bias_copies.append(copy)
    weight_copies = []
    for i, (source, target) in enumerate(
        (
            (keyval_hbm.at[:, width:], value_ref),
            (output_hbm, output_ref),
            (gate_hbm, gate_ref),
            (down_hbm, down_ref),
            (back_hbm, back_ref),
        )
    ):
        copy = pltpu.make_async_copy(source, target, weight_sems.at[i])
        copy.start()
        weight_copies.append(copy)

    lanes = GROUP * head_size
    head_of = lane_group(tokens, lanes, head_size)
    masks32 = [(head_of == h).astype(F32) for h in range(GROUP)]
    for copy in part_copies:
        copy.wait()
    for copy in bias_copies:
        copy.wait()
    for s in range(samples):
        for g in range(HEADS // GROUP):
            columns = slice(lanes * g, lanes * (g + 1))
            scores = dot_nt(absorbed_ref[s, columns], all_ref[s])
            bias = bias_ref[GROUP * g : GROUP * (g + 1)].reshape(GROUP * tokens, -1)
            scores = scores + bias.astype(F32)
            exponent = jnp.exp(scores - jnp.max(scores, axis=-1, keepdims=True))
            total = jnp.sum(exponent, axis=-1, keepdims=True)
            mixed = dot(exponent.astype(BF16), all_ref[s]) / total
            if s == 0 and g == 0:
                weight_copies[0].wait()
            valued = dot(mixed.astype(BF16), value_ref[:, columns])
            attended = valued[:tokens] * masks32[0]
            for h in range(1, GROUP):
                attended = attended + valued[tokens * h : tokens * (h + 1)] * masks32[h]
            att_ref[tokens * s : tokens * (s + 1), columns] = attended.astype(BF16)

    weight_copies[1].wait()
    merged = dot(att_ref[...], output_ref[...])
    token_act = tokact_ref[...].reshape(samples * tokens, width).astype(F32)
    token_mid = (token_act + merged).astype(BF16).astype(F32)
    trans = layer_norm(token_mid, gain_ref[...])
    weight_copies[2].wait()
    hidden_width = down_ref.shape[0]
    gate = dot(trans, gate_ref[:, :hidden_width])
    up = dot(trans, gate_ref[:, hidden_width:])
    hidden = (gate / (1.0 + jnp.exp(-gate)) * up).astype(BF16)
    weight_copies[3].wait()
    token_out = (token_mid + dot(hidden, down_ref[...])).astype(BF16)
    token_out_ref[...] = token_out.reshape(samples, tokens, width)
    weight_copies[4].wait()
    back_rows = dot(token_out, back_ref[...]).astype(BF16)
    back_rows_ref[...] = back_rows.reshape(samples, tokens, -1)
    atoms = mid_ref.shape[1]
    slot = token_ref[...] - device * tokens
    table = (lax.broadcasted_iota(jnp.int32, (tokens, atoms), 0) == slot).astype(BF16)
    for s in range(samples):
        gathered = dot_tn(table, back_rows[tokens * s : tokens * (s + 1)])
        atom_out_ref[s] = (mid_ref[s].astype(F32) + gathered).astype(BF16)


def run_tokens(plan, parts, bias_plan, bias_near, bias_far, absorbed, tokact, mid, token, gain, weights):
    samples, tokens, width = tokact.shape
    keys = bias_near.shape[-1]
    return pl.pallas_call(
        functools.partial(token_kernel, plan, bias_plan, len(parts)),
        out_shape=(
            jax.ShapeDtypeStruct(mid.shape, BF16),
            jax.ShapeDtypeStruct(tokact.shape, BF16),
            jax.ShapeDtypeStruct((samples, tokens, mid.shape[2]), BF16),
        ),
        in_specs=[anywhere()] * (len(parts) + 2) + [vmem()] * 5 + [anywhere()] * 5,
        out_specs=(vmem(),) * 3,
        scratch_shapes=[
            pltpu.VMEM((samples, keys, width), BF16),
            pltpu.VMEM((HEADS, tokens, keys), BF16),
            pltpu.VMEM((width, width), BF16),
        ]
        + [pltpu.VMEM(w.shape, w.dtype) for w in weights[1:]]
        + [
            pltpu.VMEM((samples * tokens, width), BF16),
            pltpu.SemaphoreType.DMA((len(weights),)),
            pltpu.SemaphoreType.DMA((len(plan),)),
            pltpu.SemaphoreType.DMA((len(bias_plan),)),
        ],
        compiler_params=pltpu.CompilerParams(vmem_limit_bytes=44 * 2**20),
        cost_estimate=pl.CostEstimate(
            flops=10_000_000_000, bytes_accessed=20_000_000, transcendentals=3_000_000
        ),
        name="tokens",
    )(*parts, bias_near, bias_far, absorbed, tokact, mid, token, gain, *weights)


def shifted(value, dx, dy, dz=0):
    pairs = []
    for t in range(32):
        x, y, z = t // 8, (t // 2) % 4, t % 2
        pairs.append((t, ((x + dx) % 4) * 8 + ((y + dy) % 4) * 2 + (z + dz) % 2))
    return lax.ppermute(value, "seq", pairs)


def line_of(value, dx, dy):
    return [
        value,
        shifted(value, dx, dy),
        shifted(value, -dx, -dy),
        shifted(value, 2 * dx, 2 * dy),
    ]


def spread(norm):
    samples, tokens, _ = norm.shape
    other = shifted(norm, 0, 0, 1)
    parts, plan = [], []
    for s in range(samples):
        dx, dy = (0, 1) if s % 2 == 0 else (1, 0)
        first = jnp.concatenate([norm[s], other[s]], axis=0)
        line = line_of(first, dx, dy)
        plane = line_of(jnp.concatenate(line, axis=0), dy, dx)
        steps = (0, -1, 1, 2)
        base = len(parts)
        parts += plane
        for piece, far in enumerate(steps):
            for k in range(2 * len(steps)):
                near = steps[k // 2]
                offset = (near * dx + far * dy, near * dy + far * dx, k % 2)
                plan.append((base + piece, k * tokens, s, offset))
    return parts, plan, parts[1]


def stack_kernel(count, *refs):
    pieces, stacked, sems = refs[:count], refs[-2], refs[-1]
    copies = []
    for i, piece in enumerate(pieces):
        copy = pltpu.make_async_copy(piece, stacked.at[i], sems.at[i])
        copy.start()
        copies.append(copy)
    for copy in copies:
        copy.wait()


def run_stack(pieces, after):
    count = len(pieces)
    return pl.pallas_call(
        functools.partial(stack_kernel, count),
        out_shape=jax.ShapeDtypeStruct((count,) + pieces[0].shape, pieces[0].dtype),
        in_specs=[anywhere()] * (count + 1),
        out_specs=anywhere(),
        scratch_shapes=[pltpu.SemaphoreType.DMA((count,))],
        compiler_params=pltpu.CompilerParams(vmem_limit_bytes=60 * 2**20),
        name="stack",
    )(*pieces, after)


BIAS_STEPS = (0, -1, 1, 2)


def column_of(bias):
    count = lax.axis_size("samp")

    def hop(by):
        return lax.ppermute(bias, "samp", [(i, (i + 2 * by) % count) for i in range(count)])

    return [bias, hop(1), hop(-1), hop(2)]


def other_core(value):
    return lax.ppermute(value, "samp", [(i, i ^ 1) for i in range(lax.axis_size("samp"))])


def per_device(
    atom_act,
    atom_gain,
    atom_query,
    atom_keyval,
    atom_output,
    atom_bias,
    key_range,
    atom_token,
    token_counts,
    gather_weight,
    token_gain,
    token_query,
    token_keyval,
    token_output,
    pair_bias,
    trans_gain,
    trans_gate_up,
    trans_down,
    back_weight,
):
    samples, atoms, channels = atom_act.shape
    tokens = token_counts.shape[0]
    device = lax.axis_index("seq")
    count = lax.axis_size("seq")
    to_next = [(i, i + 1) for i in range(count - 1)]
    to_previous = [(i + 1, i) for i in range(count - 1)]

    first, last = run_pack(key_range, atom_act, atom_bias)
    after = lax.ppermute(first, "seq", to_previous)
    before = lax.ppermute(last, "seq", to_next)
    column = column_of(pair_bias)
    token_row = atom_token.reshape(1, atoms)
    atom_mid, token_act, token_norm = run_atoms(
        key_range,
        token_counts,
        before,
        after,
        atom_gain.reshape(1, -1),
        token_row,
        token_gain.reshape(1, -1),
        atom_act,
        atom_query,
        atom_keyval,
        atom_bias,
        atom_output,
        gather_weight,
    )
    absorbed = run_queries(token_norm, token_query, token_keyval)
    parts, plan, ready = spread(token_norm)
    bias_near = run_stack(column, ready)
    bias_far = other_core(bias_near)
    bias_plan = [(side == 0, at, step) for side in range(2) for at, step in enumerate(BIAS_STEPS)]
    atom_out, token_out, back_rows = run_tokens(
        plan,
        parts,
        bias_plan,
        bias_near,
        bias_far,
        absorbed,
        token_act,
        atom_mid,
        token_row,
        trans_gain.reshape(1, -1),
        [token_keyval, token_output, trans_gate_up, trans_down, back_weight],
    )
    previous = lax.ppermute(back_rows[:, tokens - 1], "seq", to_next)
    earlier = (atom_token[:APT] < device * tokens)[None, :, None]
    extra = jnp.where(earlier, previous[:, None, :].astype(F32), 0.0)
    head = (atom_out[:, :APT].astype(F32) + extra).astype(BF16)
    atom_out = lax.dynamic_update_slice(atom_out, head, (0, 0, 0))
    return (atom_out, token_out)


def solution(mesh):
    placed = (
        P("samp", "seq", None),
        P(),
        P(),
        P(),
        P(),
        P(None, "seq", None, None),
        P("seq", None),
        P("seq"),
        P("seq"),
        P(),
        P(),
        P(),
        P(),
        P(),
        P("samp", "seq", None),
        P(),
        P(),
        P(),
        P(),
    )
    return jax.shard_map(
        per_device,
        mesh=mesh,
        in_specs=placed,
        out_specs=(P("samp", "seq", None), P("samp", "seq", None)),
        check_vma=False,
    )
```

```python
import functools
import math

import jax
import jax.numpy as jnp
from jax import lax
from jax.experimental import pallas as pl
from jax.experimental.pallas import tpu as pltpu
from jax.sharding import PartitionSpec as P

AH = 4
HEADS = 16
WQ = 32
WK = 128
EDGE = 48
APT = 8
BEFORE = EDGE
AFTER = WQ + EDGE
META = 16
GROUP = 8

EPSILON = 1e-05
NEGATIVE = -1e30
F32 = jnp.float32
BF16 = jnp.bfloat16


def cost(flops):
    return pl.CostEstimate(flops=flops, bytes_accessed=1000, transcendentals=0)


NT = (((1,), (1,)), ((), ()))
TN = (((0,), (0,)), ((), ()))


def dot(a, b):
    return jnp.dot(a, b, preferred_element_type=F32)


def dot_nt(a, b):
    return lax.dot_general(a, b, NT, preferred_element_type=F32)


def dot_tn(a, b):
    return lax.dot_general(a, b, TN, preferred_element_type=F32)


def layer_norm(widened, gain):
    centred = widened - jnp.mean(widened, axis=-1, keepdims=True)
    variance = jnp.mean(centred * centred, axis=-1, keepdims=True)
    return (centred * lax.rsqrt(variance + EPSILON) * gain).astype(BF16)


def lane_group(rows, lanes, width):
    return lax.broadcasted_iota(jnp.int32, (rows, lanes), 1) // width


def pack_kernel(range_ref, act_hbm, bias_hbm, first_ref, last_ref, sems):
    samples, atoms, _ = act_hbm.shape
    bias_at = samples * AFTER
    meta_at = bias_at + AH * WQ
    copies = []
    for s in range(samples):
        copies.append((act_hbm.at[s, :AFTER], first_ref.at[AFTER * s : AFTER * (s + 1)]))
        copies.append((act_hbm.at[s, atoms - BEFORE :], last_ref.at[BEFORE * s : BEFORE * (s + 1)]))
    for h in range(AH):
        copies.append((bias_hbm.at[h, 0], first_ref.at[bias_at + WQ * h : bias_at + WQ * (h + 1)]))
    started = []
    for i, (source, target) in enumerate(copies):
        copy = pltpu.make_async_copy(source, target, sems.at[i])
        copy.start()
        started.append(copy)
    start = lax.axis_index("seq") * atoms - EDGE
    row = lax.broadcasted_iota(jnp.int32, (META, WK), 0)
    meta = jnp.where(row == 0, range_ref[0, 0] - start, range_ref[1, 0] - start)
    first_ref[meta_at : meta_at + META, :] = meta.astype(F32).astype(BF16)
    for copy in started:
        copy.wait()


def run_pack(key_range, act, bias):
    samples, _, channels = act.shape
    return pl.pallas_call(
        pack_kernel,
        out_shape=(
            jax.ShapeDtypeStruct((samples * AFTER + AH * WQ + META, channels), BF16),
            jax.ShapeDtypeStruct((samples * BEFORE, channels), BF16),
        ),
        in_specs=[smem(), anywhere(), anywhere()],
        out_specs=(vmem(), vmem()),
        scratch_shapes=[pltpu.SemaphoreType.DMA((2 * samples + AH,))],
        compiler_params=pltpu.CompilerParams(vmem_limit_bytes=60 * 2**20),
        name="pack",
    )(key_range, act, bias)


def atom_kernel(
    range_ref,
    count_ref,
    before_ref,
    after_ref,
    gain_ref,
    token_ref,
    token_gain_ref,
    act_hbm,
    query_hbm,
    keyval_hbm,
    bias_hbm,
    output_hbm,
    gather_hbm,
    mid_ref,
    tokact_ref,
    norm_ref,
    act_ref,
    query_ref,
    keyval_ref,
    bias_ref,
    output_ref,
    gather_ref,
    att_ref,
    sems,
):
    copies = []
    for i, (source, target) in enumerate(
        (
            (act_hbm, act_ref),
            (query_hbm, query_ref),
            (keyval_hbm, keyval_ref),
            (bias_hbm, bias_ref),
            (output_hbm, output_ref),
            (gather_hbm, gather_ref),
        )
    ):
        copy = pltpu.make_async_copy(source, target, sems.at[i])
        copy.start()
        copies.append(copy)
    samples, atoms, channels = act_ref.shape
    windows = atoms // WQ
    tokens = norm_ref.shape[1]
    head_width = channels // AH
    scale = 1.0 / math.sqrt(head_width)
    device = lax.axis_index("seq")
    gain = gain_ref[...]
    bias_at = samples * AFTER
    meta_at = bias_at + AH * WQ

    head_of = lane_group(WQ, channels, head_width)
    masks = [(head_of == h).astype(BF16) for h in range(AH)]
    masks32 = [(head_of == h).astype(F32) for h in range(AH)]
    index = lax.broadcasted_iota(jnp.int32, (1, WK), 1)

    meta = after_ref[meta_at : meta_at + META, :].astype(F32)
    indexf = index.astype(F32)
    valid_after = (indexf >= meta[0:1, :]) & (indexf < meta[1:2, :])

    slot = token_ref[...] - device * tokens
    own_table = (lax.broadcasted_iota(jnp.int32, (tokens, atoms), 0) == slot).astype(F32)
    own_counts = jnp.sum(own_table, axis=1, keepdims=True)
    own_table = own_table.astype(BF16)
    row = lax.broadcasted_iota(jnp.int32, (tokens, 1), 0)
    remaining = jnp.where(
        row == tokens - 1, count_ref[tokens - 1].astype(F32) - own_counts, jnp.zeros_like(own_counts)
    )
    lane = lax.broadcasted_iota(jnp.int32, (tokens, WQ), 1).astype(F32)
    after_table = (lane < remaining).astype(BF16)
    counts = jnp.maximum(own_counts + remaining, 1.0)

    for copy in copies[:4]:
        copy.wait()
    for s in range(samples):
        extended = jnp.concatenate(
            [
                before_ref[s * BEFORE : (s + 1) * BEFORE, :],
                act_ref[s],
                after_ref[s * AFTER : (s + 1) * AFTER, :],
            ],
            axis=0,
        ).astype(F32)
        normed = layer_norm(extended, gain)
        queries = dot(normed, query_ref[...]).astype(BF16)
        keyvals = dot(normed, keyval_ref[...]).astype(BF16)
        for w in range(windows + 1):
            q = queries[BEFORE + WQ * w : BEFORE + WQ * (w + 1), :]
            keys = keyvals[WQ * w : WQ * w + WK, :channels]
            values = keyvals[WQ * w : WQ * w + WK, channels:]
            stacked = jnp.concatenate([q * m for m in masks], axis=0)
            scores = dot_nt(stacked, keys) * scale
            if w < windows:
                bias = bias_ref[:, w].reshape(AH * WQ, WK)
                start = (device * windows + w) * WQ - EDGE
                valid = (index >= range_ref[0, w] - start) & (index < range_ref[1, w] - start)
            else:
                bias = after_ref[bias_at : bias_at + AH * WQ, :]
                valid = valid_after
            scores = jnp.where(valid, scores + bias.astype(F32), NEGATIVE)
            exponent = jnp.exp(scores - jnp.max(scores, axis=-1, keepdims=True))
            total = jnp.sum(exponent, axis=-1, keepdims=True)
            mixed = dot(exponent.astype(BF16), values) / total
            attended = mixed[:WQ] * masks32[0]
            for h in range(1, AH):
                attended = attended + mixed[WQ * h : WQ * (h + 1)] * masks32[h]
            att_ref[s, WQ * w : WQ * (w + 1), :] = attended.astype(BF16)
        if s == 0:
            copies[4].wait()
            copies[5].wait()
        merged = dot(att_ref[s], output_ref[...])
        mid = (extended[BEFORE : BEFORE + atoms + WQ, :] + merged).astype(BF16)
        mid_ref[s] = mid[:atoms]
        hidden = jnp.maximum(dot(mid, gather_ref[...]), 0.0).astype(BF16)
        sums = dot(own_table, hidden[:atoms]) + dot(after_table, hidden[atoms:])
        token_act = (sums / counts).astype(BF16)
        tokact_ref[s] = token_act
        norm_ref[s] = layer_norm(token_act.astype(F32), token_gain_ref[...])


def vmem():
    return pl.BlockSpec(memory_space=pltpu.VMEM)


def smem():
    return pl.BlockSpec(memory_space=pltpu.SMEM)


def anywhere():
    return pl.BlockSpec(memory_space=pl.ANY)


def run_atoms(key_range, counts, before, after, gain, token, token_gain, *arrays):
    samples, atoms, channels = arrays[0].shape
    width = arrays[-1].shape[1]
    tokens = atoms // APT
    return pl.pallas_call(
        atom_kernel,
        out_shape=(
            jax.ShapeDtypeStruct((samples, atoms, channels), BF16),
            jax.ShapeDtypeStruct((samples, tokens, width), BF16),
            jax.ShapeDtypeStruct((samples, tokens, width), BF16),
        ),
        in_specs=[smem()] * 2 + [vmem()] * 5 + [anywhere()] * len(arrays),
        out_specs=(vmem(),) * 3,
        scratch_shapes=[pltpu.VMEM(a.shape, a.dtype) for a in arrays]
        + [
            pltpu.VMEM((samples, atoms + WQ, channels), BF16),
            pltpu.SemaphoreType.DMA((len(arrays),)),
        ],
        compiler_params=pltpu.CompilerParams(vmem_limit_bytes=60 * 2**20),
        cost_estimate=cost(5_000_000_000),
        name="atoms",
    )(key_range, counts, before, after, gain, token, token_gain, *arrays)


def query_kernel(norm_ref, query_hbm, keyval_hbm, absorbed_ref, query_ref, key_ref, sems):
    samples, tokens, width = norm_ref.shape
    first = pltpu.make_async_copy(query_hbm, query_ref, sems.at[0])
    second = pltpu.make_async_copy(keyval_hbm.at[:, :width], key_ref, sems.at[1])
    first.start()
    second.start()
    head_size = width // HEADS
    scale = 1.0 / math.sqrt(head_size)
    lanes = GROUP * head_size
    head_of = lane_group(tokens, lanes, head_size)
    masks = [(head_of == h).astype(BF16) for h in range(GROUP)]
    first.wait()
    queries = dot(norm_ref[...].reshape(samples * tokens, width), query_ref[...]).astype(BF16)
    second.wait()
    for s in range(samples):
        for g in range(HEADS // GROUP):
            columns = slice(lanes * g, lanes * (g + 1))
            q = queries[tokens * s : tokens * (s + 1), columns]
            stacked = jnp.concatenate([q * m for m in masks], axis=0)
            absorbed = dot_nt(stacked, key_ref[:, columns]) * scale
            absorbed_ref[s, lanes * g : lanes * (g + 1)] = absorbed.astype(BF16)


def run_queries(norm, token_query, token_keyval):
    samples, tokens, width = norm.shape
    return pl.pallas_call(
        query_kernel,
        out_shape=jax.ShapeDtypeStruct((samples, HEADS * tokens, width), BF16),
        in_specs=[vmem(), anywhere(), anywhere()],
        out_specs=vmem(),
        scratch_shapes=[
            pltpu.VMEM((width, width), BF16),
            pltpu.VMEM((width, width), BF16),
            pltpu.SemaphoreType.DMA((2,)),
        ],
        compiler_params=pltpu.CompilerParams(vmem_limit_bytes=30 * 2**20),
        cost_estimate=cost(2_000_000_000),
        name="queries",
    )(norm, token_query, token_keyval)


def reorder_kernel(bias_ref, after_hbm, out_ref):
    heads, tokens, keys = bias_ref.shape
    line = keys // 4
    part = line // 4
    for h in range(heads):
        rows = bias_ref[h]
        blocks = [
            rows[:, line * x + part * y : line * x + part * (y + 1)] for y in range(4) for x in range(4)
        ]
        out_ref[h] = jnp.concatenate(blocks, axis=1)


def run_reorder(bias, after):
    return pl.pallas_call(
        reorder_kernel,
        out_shape=jax.ShapeDtypeStruct(bias.shape, BF16),
        in_specs=[vmem(), anywhere()],
        out_specs=vmem(),
        compiler_params=pltpu.CompilerParams(vmem_limit_bytes=24 * 2**20),
        cost_estimate=cost(2_000_000_000),
        name="reorder",
    )(bias, after)


def place(device, sample):
    x, y = device // 8, (device // 2) % 4
    return x if sample % 2 == 0 else y


def piece_scores(q, piece, bias_ref, group, chunk):
    size = piece.shape[0]
    start = pl.multiple_of(chunk * size, 128)
    bias = bias_ref[GROUP * group : GROUP * (group + 1), :, pl.ds(start, size)]
    return dot_nt(q, piece) + bias.reshape(q.shape[0], size).astype(F32)


def early_kernel(
    absorbed_ref,
    bias0_ref,
    bias1_ref,
    own0_ref,
    low0_ref,
    high0_ref,
    own1_ref,
    low1_ref,
    high1_ref,
    mixed_ref,
    best_ref,
    total_ref,
):
    device = lax.axis_index("seq")
    samples = absorbed_ref.shape[0]
    rows_of = absorbed_ref.shape[1] * GROUP // HEADS
    pieces = ((own0_ref, low0_ref, high0_ref), (own1_ref, low1_ref, high1_ref))
    for s in range(samples):
        here = place(device, s)
        for g in range(HEADS // GROUP):
            rows = slice(rows_of * g, rows_of * (g + 1))
            q = absorbed_ref[s, rows]
            scores = [
                piece_scores(q, piece[...], (bias0_ref, bias1_ref)[s], g, (here + step) % 4)
                for piece, step in zip(pieces[s], (0, 3, 1))
            ]
            best = functools.reduce(
                jnp.maximum, [jnp.max(c, axis=-1, keepdims=True) for c in scores]
            )
            total, mixed = 0.0, 0.0
            for piece, c in zip(pieces[s], scores):
                exponent = jnp.exp(c - best)
                total = total + jnp.sum(exponent, axis=-1, keepdims=True)
                mixed = mixed + dot(exponent.astype(BF16), piece[...])
            mixed_ref[s, rows] = mixed
            best_ref[s, rows] = jnp.broadcast_to(best, (rows_of, 128))
            total_ref[s, rows] = jnp.broadcast_to(total, (rows_of, 128))


def run_early(absorbed, bias0, bias1, pieces):
    samples, rows, width = absorbed.shape
    return pl.pallas_call(
        early_kernel,
        out_shape=(
            jax.ShapeDtypeStruct((samples, rows, width), F32),
            jax.ShapeDtypeStruct((samples, rows, 128), F32),
            jax.ShapeDtypeStruct((samples, rows, 128), F32),
        ),
        in_specs=[vmem()] * (3 + len(pieces)),
        out_specs=(vmem(),) * 3,
        compiler_params=pltpu.CompilerParams(vmem_limit_bytes=26 * 2**20),
        cost_estimate=cost(8_000_000_000),
        name="early",
    )(absorbed, bias0, bias1, *pieces)


def late_kernel(
    absorbed_ref,
    bias0_ref,
    bias1_ref,
    far0_low_ref,
    far0_high_ref,
    far1_low_ref,
    far1_high_ref,
    mixed_ref,
    best_ref,
    total_ref,
    tokact_ref,
    mid_ref,
    token_ref,
    gain_ref,
    keyval_hbm,
    output_hbm,
    gate_hbm,
    down_hbm,
    back_hbm,
    atom_out_ref,
    token_out_ref,
    back_rows_ref,
    value_ref,
    output_ref,
    gate_ref,
    down_ref,
    back_ref,
    att_ref,
    weight_sems,
):
    samples, tokens, width = tokact_ref.shape
    head_size = width // HEADS
    device = lax.axis_index("seq")
    weight_copies = []
    for i, (source, target) in enumerate(
        (
            (keyval_hbm.at[:, width:], value_ref),
            (output_hbm, output_ref),
            (gate_hbm, gate_ref),
            (down_hbm, down_ref),
            (back_hbm, back_ref),
        )
    ):
        copy = pltpu.make_async_copy(source, target, weight_sems.at[i])
        copy.start()
        weight_copies.append(copy)

    lanes = GROUP * head_size
    head_of = lane_group(tokens, lanes, head_size)
    masks32 = [(head_of == h).astype(F32) for h in range(GROUP)]
    halves = ((far0_low_ref, far0_high_ref), (far1_low_ref, far1_high_ref))
    for s in range(samples):
        far = (place(device, s) + 2) % 4
        piece = jnp.concatenate([halves[s][0][...], halves[s][1][...]], axis=0)
        for g in range(HEADS // GROUP):
            columns = slice(lanes * g, lanes * (g + 1))
            scores = piece_scores(absorbed_ref[s, columns], piece, (bias0_ref, bias1_ref)[s], g, far)
            before = best_ref[s, columns][:, :1]
            best = jnp.maximum(before, jnp.max(scores, axis=-1, keepdims=True))
            exponent = jnp.exp(scores - best)
            shrink = jnp.exp(before - best)
            total = total_ref[s, columns][:, :1] * shrink + jnp.sum(
                exponent, axis=-1, keepdims=True
            )
            mixed = mixed_ref[s, columns] * shrink + dot(exponent.astype(BF16), piece)
            mixed = mixed / total
            if s == 0 and g == 0:
                weight_copies[0].wait()
            valued = dot(mixed.astype(BF16), value_ref[:, columns])
            attended = valued[:tokens] * masks32[0]
            for h in range(1, GROUP):
                attended = attended + valued[tokens * h : tokens * (h + 1)] * masks32[h]
            att_ref[tokens * s : tokens * (s + 1), columns] = attended.astype(BF16)

    weight_copies[1].wait()
    merged = dot(att_ref[...], output_ref[...])
    token_act = tokact_ref[...].reshape(samples * tokens, width).astype(F32)
    token_mid = (token_act + merged).astype(BF16).astype(F32)
    trans = layer_norm(token_mid, gain_ref[...])
    weight_copies[2].wait()
    hidden_width = down_ref.shape[0]
    gate = dot(trans, gate_ref[:, :hidden_width])
    up = dot(trans, gate_ref[:, hidden_width:])
    hidden = (gate / (1.0 + jnp.exp(-gate)) * up).astype(BF16)
    weight_copies[3].wait()
    token_out = (token_mid + dot(hidden, down_ref[...])).astype(BF16)
    token_out_ref[...] = token_out.reshape(samples, tokens, width)
    weight_copies[4].wait()
    back_rows = dot(token_out, back_ref[...]).astype(BF16)
    back_rows_ref[...] = back_rows.reshape(samples, tokens, -1)
    atoms = mid_ref.shape[1]
    slot = token_ref[...] - device * tokens
    table = (lax.broadcasted_iota(jnp.int32, (tokens, atoms), 0) == slot).astype(BF16)
    for s in range(samples):
        gathered = dot_tn(table, back_rows[tokens * s : tokens * (s + 1)])
        atom_out_ref[s] = (mid_ref[s].astype(F32) + gathered).astype(BF16)


def run_late(absorbed, bias0, bias1, far, early, tokact, mid, token, gain, weights):
    samples, tokens, width = tokact.shape
    return pl.pallas_call(
        late_kernel,
        out_shape=(
            jax.ShapeDtypeStruct(mid.shape, BF16),
            jax.ShapeDtypeStruct(tokact.shape, BF16),
            jax.ShapeDtypeStruct((samples, tokens, mid.shape[2]), BF16),
        ),
        in_specs=[vmem()] * 14 + [anywhere()] * 5,
        out_specs=(vmem(),) * 3,
        scratch_shapes=[pltpu.VMEM((width, width), BF16)]
        + [pltpu.VMEM(w.shape, w.dtype) for w in weights[1:]]
        + [
            pltpu.VMEM((samples * tokens, width), BF16),
            pltpu.SemaphoreType.DMA((len(weights),)),
        ],
        compiler_params=pltpu.CompilerParams(vmem_limit_bytes=28 * 2**20),
        cost_estimate=cost(5_000_000_000),
        name="late",
    )(absorbed, bias0, bias1, *far, *early, tokact, mid, token, gain, *weights)


def shifted(value, dx, dy):
    pairs = []
    for t in range(32):
        x, y, z = t // 8, (t // 2) % 4, t % 2
        pairs.append((t, ((x + dx) % 4) * 8 + ((y + dy) % 4) * 2 + z))
    return lax.ppermute(value, "seq", pairs)


def exchanged(value, bit):
    return lax.ppermute(value, "seq", [(t, t ^ (1 << bit)) for t in range(32)])


def join_kernel(bits, *refs):
    count = len(bits)
    device = lax.axis_index("seq")
    for i, bit in enumerate(bits):
        own, other, joined = refs[i], refs[count + i], refs[2 * count + i]
        rows = joined.shape[0] // 2
        where = (device // (1 << bit)) % 2
        joined[pl.ds(pl.multiple_of(where * rows, 16), rows)] = own[...].reshape(rows, -1)
        joined[pl.ds(pl.multiple_of((1 - where) * rows, 16), rows)] = other[...].reshape(rows, -1)


def joined(own, other, bits):
    rows, width = own[0].shape
    shape = jax.ShapeDtypeStruct((2 * rows, width), BF16)
    return pl.pallas_call(
        functools.partial(join_kernel, bits),
        out_shape=(shape,) * len(bits),
        in_specs=[vmem()] * (2 * len(bits)),
        out_specs=(vmem(),) * len(bits),
        compiler_params=pltpu.CompilerParams(vmem_limit_bytes=16 * 2**20),
        cost_estimate=cost(1_000_000),
        name="join",
    )(*own, *other)


def spread(norm):
    other = exchanged(norm, 0)
    lines = joined([norm[0], norm[1]], [other[0], other[1]], (0, 0))
    for bits in ((1, 3), (2, 4)):
        lines = joined(lines, [exchanged(v, b) for v, b in zip(lines, bits)], bits)
    near, far = [], []
    for value, dx, dy in ((lines[0], 1, 0), (lines[1], 0, 1)):
        near.append((value, shifted(value, dx, dy), shifted(value, -dx, -dy)))
    for (value, low, high), dx, dy in ((near[0], 1, 0), (near[1], 0, 1)):
        half = value.shape[0] // 2
        far += [shifted(low[:half], dx, dy), shifted(high[half:], -dx, -dy)]
    return near, far


def per_device(
    atom_act,
    atom_gain,
    atom_query,
    atom_keyval,
    atom_output,
    atom_bias,
    key_range,
    atom_token,
    token_counts,
    gather_weight,
    token_gain,
    token_query,
    token_keyval,
    token_output,
    pair_bias,
    trans_gain,
    trans_gate_up,
    trans_down,
    back_weight,
):
    samples, atoms, channels = atom_act.shape
    tokens = token_counts.shape[0]
    device = lax.axis_index("seq")
    count = lax.axis_size("seq")
    to_next = [(i, i + 1) for i in range(count - 1)]
    to_previous = [(i + 1, i) for i in range(count - 1)]

    ranges = key_range.T
    first, last = run_pack(ranges, atom_act, atom_bias)
    after = lax.ppermute(first, "seq", to_previous)
    before = lax.ppermute(last, "seq", to_next)
    bias = lax.all_gather(pair_bias, "samp", axis=0, tiled=True)
    token_row = atom_token.reshape(1, atoms)
    atom_mid, token_act, token_norm = run_atoms(
        ranges,
        token_counts,
        before,
        after,
        atom_gain.reshape(1, -1),
        token_row,
        token_gain.reshape(1, -1),
        atom_act,
        atom_query,
        atom_keyval,
        atom_bias,
        atom_output,
        gather_weight,
    )
    absorbed = run_queries(token_norm, token_query, token_keyval)
    near, far = spread(token_norm)
    turned = run_reorder(bias, near[1][0])
    early = run_early(absorbed, bias, turned, near[0] + near[1])
    atom_out, token_out, back_rows = run_late(
        absorbed,
        bias,
        turned,
        far,
        early,
        token_act,
        atom_mid,
        token_row,
        trans_gain.reshape(1, -1),
        [token_keyval, token_output, trans_gate_up, trans_down, back_weight],
    )
    previous = lax.ppermute(back_rows[:, tokens - 1], "seq", to_next)
    earlier = (atom_token[:APT] < device * tokens)[None, :, None]
    extra = jnp.where(earlier, previous[:, None, :].astype(F32), 0.0)
    head = (atom_out[:, :APT].astype(F32) + extra).astype(BF16)
    atom_out = lax.dynamic_update_slice(atom_out, head, (0, 0, 0))
    return (atom_out, token_out)


def solution(mesh):
    placed = (
        P("samp", "seq", None),
        P(),
        P(),
        P(),
        P(),
        P(None, "seq", None, None),
        P("seq", None),
        P("seq"),
        P("seq"),
        P(),
        P(),
        P(),
        P(),
        P(),
        P("samp", "seq", None),
        P(),
        P(),
        P(),
        P(),
    )
    return jax.shard_map(
        per_device,
        mesh=mesh,
        in_specs=placed,
        out_specs=(P("samp", "seq", None), P("samp", "seq", None)),
        check_vma=False,
    )
```

```python
import functools
import math

import jax
import jax.numpy as jnp
from jax import lax
from jax.experimental import pallas as pl
from jax.experimental.pallas import tpu as pltpu
from jax.sharding import PartitionSpec as P

AH = 4
HEADS = 16
WQ = 32
WK = 128
EDGE = 48
APT = 8
BEFORE = EDGE
AFTER = WQ + EDGE
META = 16
GROUP = 8

EPSILON = 1e-05
NEGATIVE = -1e30
F32 = jnp.float32
BF16 = jnp.bfloat16


def cost(flops):
    return pl.CostEstimate(flops=flops, bytes_accessed=1000, transcendentals=0)


NT = (((1,), (1,)), ((), ()))
TN = (((0,), (0,)), ((), ()))


def dot(a, b):
    return jnp.dot(a, b, preferred_element_type=F32)


def dot_nt(a, b):
    return lax.dot_general(a, b, NT, preferred_element_type=F32)


def dot_tn(a, b):
    return lax.dot_general(a, b, TN, preferred_element_type=F32)


def layer_norm(widened, gain):
    centred = widened - jnp.mean(widened, axis=-1, keepdims=True)
    variance = jnp.mean(centred * centred, axis=-1, keepdims=True)
    return (centred * lax.rsqrt(variance + EPSILON) * gain).astype(BF16)


def lane_group(rows, lanes, width):
    return lax.broadcasted_iota(jnp.int32, (rows, lanes), 1) // width


def pack_kernel(range_ref, act_hbm, bias_hbm, first_ref, last_ref, sems):
    samples, atoms, _ = act_hbm.shape
    bias_at = samples * AFTER
    meta_at = bias_at + AH * WQ
    copies = []
    for s in range(samples):
        copies.append((act_hbm.at[s, :AFTER], first_ref.at[AFTER * s : AFTER * (s + 1)]))
        copies.append((act_hbm.at[s, atoms - BEFORE :], last_ref.at[BEFORE * s : BEFORE * (s + 1)]))
    for h in range(AH):
        copies.append((bias_hbm.at[h, 0], first_ref.at[bias_at + WQ * h : bias_at + WQ * (h + 1)]))
    started = []
    for i, (source, target) in enumerate(copies):
        copy = pltpu.make_async_copy(source, target, sems.at[i])
        copy.start()
        started.append(copy)
    start = lax.axis_index("seq") * atoms - EDGE
    row = lax.broadcasted_iota(jnp.int32, (META, WK), 0)
    meta = jnp.where(row == 0, range_ref[0, 0] - start, range_ref[1, 0] - start)
    first_ref[meta_at : meta_at + META, :] = meta.astype(F32).astype(BF16)
    for copy in started:
        copy.wait()


def run_pack(key_range, act, bias):
    samples, _, channels = act.shape
    return pl.pallas_call(
        pack_kernel,
        out_shape=(
            jax.ShapeDtypeStruct((samples * AFTER + AH * WQ + META, channels), BF16),
            jax.ShapeDtypeStruct((samples * BEFORE, channels), BF16),
        ),
        in_specs=[smem(), anywhere(), anywhere()],
        out_specs=(vmem(), vmem()),
        scratch_shapes=[pltpu.SemaphoreType.DMA((2 * samples + AH,))],
        compiler_params=pltpu.CompilerParams(vmem_limit_bytes=60 * 2**20),
        name="pack",
    )(key_range, act, bias)


def atom_kernel(
    range_ref,
    count_ref,
    before_ref,
    after_ref,
    gain_ref,
    token_ref,
    token_gain_ref,
    act_hbm,
    query_hbm,
    keyval_hbm,
    bias_hbm,
    output_hbm,
    gather_hbm,
    mid_ref,
    tokact_ref,
    norm_ref,
    act_ref,
    query_ref,
    keyval_ref,
    bias_ref,
    output_ref,
    gather_ref,
    att_ref,
    sems,
):
    copies = []
    for i, (source, target) in enumerate(
        (
            (act_hbm, act_ref),
            (query_hbm, query_ref),
            (keyval_hbm, keyval_ref),
            (bias_hbm, bias_ref),
            (output_hbm, output_ref),
            (gather_hbm, gather_ref),
        )
    ):
        copy = pltpu.make_async_copy(source, target, sems.at[i])
        copy.start()
        copies.append(copy)
    samples, atoms, channels = act_ref.shape
    windows = atoms // WQ
    tokens = norm_ref.shape[1]
    head_width = channels // AH
    scale = 1.0 / math.sqrt(head_width)
    device = lax.axis_index("seq")
    gain = gain_ref[...]
    bias_at = samples * AFTER
    meta_at = bias_at + AH * WQ

    head_of = lane_group(WQ, channels, head_width)
    masks = [(head_of == h).astype(BF16) for h in range(AH)]
    masks32 = [(head_of == h).astype(F32) for h in range(AH)]
    index = lax.broadcasted_iota(jnp.int32, (1, WK), 1)

    meta = after_ref[meta_at : meta_at + META, :].astype(F32)
    indexf = index.astype(F32)
    valid_after = (indexf >= meta[0:1, :]) & (indexf < meta[1:2, :])

    slot = token_ref[...] - device * tokens
    own_table = (lax.broadcasted_iota(jnp.int32, (tokens, atoms), 0) == slot).astype(F32)
    own_counts = jnp.sum(own_table, axis=1, keepdims=True)
    own_table = own_table.astype(BF16)
    row = lax.broadcasted_iota(jnp.int32, (tokens, 1), 0)
    remaining = jnp.where(
        row == tokens - 1, count_ref[tokens - 1].astype(F32) - own_counts, jnp.zeros_like(own_counts)
    )
    lane = lax.broadcasted_iota(jnp.int32, (tokens, WQ), 1).astype(F32)
    after_table = (lane < remaining).astype(BF16)
    counts = jnp.maximum(own_counts + remaining, 1.0)

    for copy in copies[:4]:
        copy.wait()
    for s in range(samples):
        extended = jnp.concatenate(
            [
                before_ref[s * BEFORE : (s + 1) * BEFORE, :],
                act_ref[s],
                after_ref[s * AFTER : (s + 1) * AFTER, :],
            ],
            axis=0,
        ).astype(F32)
        normed = layer_norm(extended, gain)
        queries = dot(normed, query_ref[...]).astype(BF16)
        keyvals = dot(normed, keyval_ref[...]).astype(BF16)
        for w in range(windows + 1):
            q = queries[BEFORE + WQ * w : BEFORE + WQ * (w + 1), :]
            keys = keyvals[WQ * w : WQ * w + WK, :channels]
            values = keyvals[WQ * w : WQ * w + WK, channels:]
            stacked = jnp.concatenate([q * m for m in masks], axis=0)
            scores = dot_nt(stacked, keys) * scale
            if w < windows:
                bias = bias_ref[:, w].reshape(AH * WQ, WK)
                start = (device * windows + w) * WQ - EDGE
                valid = (index >= range_ref[0, w] - start) & (index < range_ref[1, w] - start)
            else:
                bias = after_ref[bias_at : bias_at + AH * WQ, :]
                valid = valid_after
            scores = jnp.where(valid, scores + bias.astype(F32), NEGATIVE)
            exponent = jnp.exp(scores - jnp.max(scores, axis=-1, keepdims=True))
            total = jnp.sum(exponent, axis=-1, keepdims=True)
            mixed = dot(exponent.astype(BF16), values) / total
            attended = mixed[:WQ] * masks32[0]
            for h in range(1, AH):
                attended = attended + mixed[WQ * h : WQ * (h + 1)] * masks32[h]
            att_ref[s, WQ * w : WQ * (w + 1), :] = attended.astype(BF16)
        if s == 0:
            copies[4].wait()
            copies[5].wait()
        merged = dot(att_ref[s], output_ref[...])
        mid = (extended[BEFORE : BEFORE + atoms + WQ, :] + merged).astype(BF16)
        mid_ref[s] = mid[:atoms]
        hidden = jnp.maximum(dot(mid, gather_ref[...]), 0.0).astype(BF16)
        sums = dot(own_table, hidden[:atoms]) + dot(after_table, hidden[atoms:])
        token_act = (sums / counts).astype(BF16)
        tokact_ref[s] = token_act
        norm_ref[s] = layer_norm(token_act.astype(F32), token_gain_ref[...])


def vmem():
    return pl.BlockSpec(memory_space=pltpu.VMEM)


def smem():
    return pl.BlockSpec(memory_space=pltpu.SMEM)


def anywhere():
    return pl.BlockSpec(memory_space=pl.ANY)


def run_atoms(key_range, counts, before, after, gain, token, token_gain, *arrays):
    samples, atoms, channels = arrays[0].shape
    width = arrays[-1].shape[1]
    tokens = atoms // APT
    return pl.pallas_call(
        atom_kernel,
        out_shape=(
            jax.ShapeDtypeStruct((samples, atoms, channels), BF16),
            jax.ShapeDtypeStruct((samples, tokens, width), BF16),
            jax.ShapeDtypeStruct((samples, tokens, width), BF16),
        ),
        in_specs=[smem()] * 2 + [vmem()] * 5 + [anywhere()] * len(arrays),
        out_specs=(vmem(),) * 3,
        scratch_shapes=[pltpu.VMEM(a.shape, a.dtype) for a in arrays]
        + [
            pltpu.VMEM((samples, atoms + WQ, channels), BF16),
            pltpu.SemaphoreType.DMA((len(arrays),)),
        ],
        compiler_params=pltpu.CompilerParams(vmem_limit_bytes=60 * 2**20),
        cost_estimate=cost(1_000_000),
        name="atoms",
    )(key_range, counts, before, after, gain, token, token_gain, *arrays)


def query_kernel(norm_ref, query_hbm, keyval_hbm, absorbed_ref, query_ref, key_ref, sems):
    samples, tokens, width = norm_ref.shape
    first = pltpu.make_async_copy(query_hbm, query_ref, sems.at[0])
    second = pltpu.make_async_copy(keyval_hbm.at[:, :width], key_ref, sems.at[1])
    first.start()
    second.start()
    head_size = width // HEADS
    scale = 1.0 / math.sqrt(head_size)
    lanes = GROUP * head_size
    head_of = lane_group(tokens, lanes, head_size)
    masks = [(head_of == h).astype(BF16) for h in range(GROUP)]
    first.wait()
    queries = dot(norm_ref[...].reshape(samples * tokens, width), query_ref[...]).astype(BF16)
    second.wait()
    for s in range(samples):
        for g in range(HEADS // GROUP):
            columns = slice(lanes * g, lanes * (g + 1))
            q = queries[tokens * s : tokens * (s + 1), columns]
            stacked = jnp.concatenate([q * m for m in masks], axis=0)
            absorbed = dot_nt(stacked, key_ref[:, columns]) * scale
            absorbed_ref[s, lanes * g : lanes * (g + 1)] = absorbed.astype(BF16)


def run_queries(norm, token_query, token_keyval):
    samples, tokens, width = norm.shape
    return pl.pallas_call(
        query_kernel,
        out_shape=jax.ShapeDtypeStruct((samples, HEADS * tokens, width), BF16),
        in_specs=[vmem(), anywhere(), anywhere()],
        out_specs=vmem(),
        scratch_shapes=[
            pltpu.VMEM((width, width), BF16),
            pltpu.VMEM((width, width), BF16),
            pltpu.SemaphoreType.DMA((2,)),
        ],
        compiler_params=pltpu.CompilerParams(vmem_limit_bytes=30 * 2**20),
        cost_estimate=cost(1_000_000),
        name="queries",
    )(norm, token_query, token_keyval)


def stack_kernel(steps, *refs):
    column = lax.axis_index("samp") // 2
    stacked = refs[-1]
    for step, piece in zip(steps, refs):
        stacked[(column + step) % len(steps)] = piece[...]


def run_stack(pieces, steps, after):
    count = len(pieces)
    return pl.pallas_call(
        functools.partial(stack_kernel, steps),
        out_shape=jax.ShapeDtypeStruct((count,) + pieces[0].shape, pieces[0].dtype),
        in_specs=[vmem()] * count + [anywhere()],
        out_specs=vmem(),
        compiler_params=pltpu.CompilerParams(vmem_limit_bytes=16 * 2**20),
        cost_estimate=cost(1_000_000),
        name="stack",
    )(*pieces, after)


def reorder_kernel(near_ref, far_ref, bias_ref, turned_ref):
    columns, heads, _, keys = near_ref.shape
    line = keys // 4
    part = line // 4
    core = lax.axis_index("samp") % 2
    for source, which in ((near_ref, core), (far_ref, 1 - core)):
        for column in range(columns):
            for head in range(heads):
                at = (2 * column + which) * heads + head
                rows = source[column, head]
                bias_ref[at] = rows
                blocks = [
                    rows[:, line * x + part * y : line * x + part * (y + 1)]
                    for y in range(4)
                    for x in range(4)
                ]
                turned_ref[at] = jnp.concatenate(blocks, axis=1)


def run_reorder(near, far):
    columns, heads, tokens, keys = near.shape
    shape = jax.ShapeDtypeStruct((2 * columns * heads, tokens, keys), BF16)
    return pl.pallas_call(
        reorder_kernel,
        out_shape=(shape, shape),
        in_specs=[vmem(), vmem()],
        out_specs=(vmem(), vmem()),
        compiler_params=pltpu.CompilerParams(vmem_limit_bytes=24 * 2**20),
        cost_estimate=cost(2_000_000_000),
        name="reorder",
    )(near, far)


def place(device, sample):
    x, y = device // 8, (device // 2) % 4
    return x if sample % 2 == 0 else y


def piece_scores(q, piece, bias_ref, group, chunk):
    size = piece.shape[0]
    start = pl.multiple_of(chunk * size, 128)
    bias = bias_ref[GROUP * group : GROUP * (group + 1), :, pl.ds(start, size)]
    return dot_nt(q, piece) + bias.reshape(q.shape[0], size).astype(F32)


def early_kernel(
    absorbed_ref,
    bias0_ref,
    bias1_ref,
    own0_ref,
    low0_ref,
    high0_ref,
    own1_ref,
    low1_ref,
    high1_ref,
    mixed_ref,
    best_ref,
    total_ref,
):
    device = lax.axis_index("seq")
    samples = absorbed_ref.shape[0]
    rows_of = absorbed_ref.shape[1] * GROUP // HEADS
    pieces = ((own0_ref, low0_ref, high0_ref), (own1_ref, low1_ref, high1_ref))
    for s in range(samples):
        here = place(device, s)
        for g in range(HEADS // GROUP):
            rows = slice(rows_of * g, rows_of * (g + 1))
            q = absorbed_ref[s, rows]
            scores = [
                piece_scores(q, piece[...], (bias0_ref, bias1_ref)[s], g, (here + step) % 4)
                for piece, step in zip(pieces[s], (0, 3, 1))
            ]
            best = functools.reduce(
                jnp.maximum, [jnp.max(c, axis=-1, keepdims=True) for c in scores]
            )
            total, mixed = 0.0, 0.0
            for piece, c in zip(pieces[s], scores):
                exponent = jnp.exp(c - best)
                total = total + jnp.sum(exponent, axis=-1, keepdims=True)
                mixed = mixed + dot(exponent.astype(BF16), piece[...])
            mixed_ref[s, rows] = mixed
            best_ref[s, rows] = jnp.broadcast_to(best, (rows_of, 128))
            total_ref[s, rows] = jnp.broadcast_to(total, (rows_of, 128))


def run_early(absorbed, bias0, bias1, pieces):
    samples, rows, width = absorbed.shape
    return pl.pallas_call(
        early_kernel,
        out_shape=(
            jax.ShapeDtypeStruct((samples, rows, width), F32),
            jax.ShapeDtypeStruct((samples, rows, 128), F32),
            jax.ShapeDtypeStruct((samples, rows, 128), F32),
        ),
        in_specs=[vmem()] * (3 + len(pieces)),
        out_specs=(vmem(),) * 3,
        compiler_params=pltpu.CompilerParams(vmem_limit_bytes=26 * 2**20),
        cost_estimate=cost(8_000_000_000),
        name="early",
    )(absorbed, bias0, bias1, *pieces)


def late_kernel(
    absorbed_ref,
    bias0_ref,
    bias1_ref,
    far0_ref,
    far1_ref,
    mixed_ref,
    best_ref,
    total_ref,
    tokact_ref,
    mid_ref,
    token_ref,
    gain_ref,
    keyval_hbm,
    output_hbm,
    gate_hbm,
    down_hbm,
    back_hbm,
    atom_out_ref,
    token_out_ref,
    back_rows_ref,
    value_ref,
    output_ref,
    gate_ref,
    down_ref,
    back_ref,
    att_ref,
    weight_sems,
):
    samples, tokens, width = tokact_ref.shape
    head_size = width // HEADS
    device = lax.axis_index("seq")
    weight_copies = []
    for i, (source, target) in enumerate(
        (
            (keyval_hbm.at[:, width:], value_ref),
            (output_hbm, output_ref),
            (gate_hbm, gate_ref),
            (down_hbm, down_ref),
            (back_hbm, back_ref),
        )
    ):
        copy = pltpu.make_async_copy(source, target, weight_sems.at[i])
        copy.start()
        weight_copies.append(copy)

    lanes = GROUP * head_size
    head_of = lane_group(tokens, lanes, head_size)
    masks32 = [(head_of == h).astype(F32) for h in range(GROUP)]
    for s in range(samples):
        far = (place(device, s) + 2) % 4
        piece = (far0_ref, far1_ref)[s][...]
        for g in range(HEADS // GROUP):
            columns = slice(lanes * g, lanes * (g + 1))
            scores = piece_scores(absorbed_ref[s, columns], piece, (bias0_ref, bias1_ref)[s], g, far)
            before = best_ref[s, columns][:, :1]
            best = jnp.maximum(before, jnp.max(scores, axis=-1, keepdims=True))
            exponent = jnp.exp(scores - best)
            shrink = jnp.exp(before - best)
            total = total_ref[s, columns][:, :1] * shrink + jnp.sum(
                exponent, axis=-1, keepdims=True
            )
            mixed = mixed_ref[s, columns] * shrink + dot(exponent.astype(BF16), piece)
            mixed = mixed / total
            if s == 0 and g == 0:
                weight_copies[0].wait()
            valued = dot(mixed.astype(BF16), value_ref[:, columns])
            attended = valued[:tokens] * masks32[0]
            for h in range(1, GROUP):
                attended = attended + valued[tokens * h : tokens * (h + 1)] * masks32[h]
            att_ref[tokens * s : tokens * (s + 1), columns] = attended.astype(BF16)

    weight_copies[1].wait()
    merged = dot(att_ref[...], output_ref[...])
    token_act = tokact_ref[...].reshape(samples * tokens, width).astype(F32)
    token_mid = (token_act + merged).astype(BF16).astype(F32)
    trans = layer_norm(token_mid, gain_ref[...])
    weight_copies[2].wait()
    hidden_width = down_ref.shape[0]
    gate = dot(trans, gate_ref[:, :hidden_width])
    up = dot(trans, gate_ref[:, hidden_width:])
    hidden = (gate / (1.0 + jnp.exp(-gate)) * up).astype(BF16)
    weight_copies[3].wait()
    token_out = (token_mid + dot(hidden, down_ref[...])).astype(BF16)
    token_out_ref[...] = token_out.reshape(samples, tokens, width)
    weight_copies[4].wait()
    back_rows = dot(token_out, back_ref[...]).astype(BF16)
    back_rows_ref[...] = back_rows.reshape(samples, tokens, -1)
    atoms = mid_ref.shape[1]
    slot = token_ref[...] - device * tokens
    table = (lax.broadcasted_iota(jnp.int32, (tokens, atoms), 0) == slot).astype(BF16)
    for s in range(samples):
        gathered = dot_tn(table, back_rows[tokens * s : tokens * (s + 1)])
        atom_out_ref[s] = (mid_ref[s].astype(F32) + gathered).astype(BF16)


def run_late(absorbed, bias0, bias1, far, early, tokact, mid, token, gain, weights):
    samples, tokens, width = tokact.shape
    return pl.pallas_call(
        late_kernel,
        out_shape=(
            jax.ShapeDtypeStruct(mid.shape, BF16),
            jax.ShapeDtypeStruct(tokact.shape, BF16),
            jax.ShapeDtypeStruct((samples, tokens, mid.shape[2]), BF16),
        ),
        in_specs=[vmem()] * 12 + [anywhere()] * 5,
        out_specs=(vmem(),) * 3,
        scratch_shapes=[pltpu.VMEM((width, width), BF16)]
        + [pltpu.VMEM(w.shape, w.dtype) for w in weights[1:]]
        + [
            pltpu.VMEM((samples * tokens, width), BF16),
            pltpu.SemaphoreType.DMA((len(weights),)),
        ],
        compiler_params=pltpu.CompilerParams(vmem_limit_bytes=28 * 2**20),
        cost_estimate=cost(5_000_000_000),
        name="late",
    )(absorbed, bias0, bias1, *far, *early, tokact, mid, token, gain, *weights)


def shifted(value, dx, dy):
    pairs = []
    for t in range(32):
        x, y, z = t // 8, (t // 2) % 4, t % 2
        pairs.append((t, ((x + dx) % 4) * 8 + ((y + dy) % 4) * 2 + z))
    return lax.ppermute(value, "seq", pairs)


def exchanged(value, bit):
    return lax.ppermute(value, "seq", [(t, t ^ (1 << bit)) for t in range(32)])


def join_kernel(bits, *refs):
    count = len(bits)
    device = lax.axis_index("seq")
    for i, bit in enumerate(bits):
        own, other, joined = refs[i], refs[count + i], refs[2 * count + i]
        rows = joined.shape[0] // 2
        where = (device // (1 << bit)) % 2
        joined[pl.ds(pl.multiple_of(where * rows, 16), rows)] = own[...].reshape(rows, -1)
        joined[pl.ds(pl.multiple_of((1 - where) * rows, 16), rows)] = other[...].reshape(rows, -1)


def joined(own, other, bits):
    rows, width = own[0].shape
    shape = jax.ShapeDtypeStruct((2 * rows, width), BF16)
    return pl.pallas_call(
        functools.partial(join_kernel, bits),
        out_shape=(shape,) * len(bits),
        in_specs=[vmem()] * (2 * len(bits)),
        out_specs=(vmem(),) * len(bits),
        compiler_params=pltpu.CompilerParams(vmem_limit_bytes=16 * 2**20),
        cost_estimate=cost(1_000_000),
        name="join",
    )(*own, *other)


def spread(norm):
    other = exchanged(norm, 0)
    lines = joined([norm[0], norm[1]], [other[0], other[1]], (0, 0))
    for bits in ((1, 3), (2, 4)):
        earlier = lines
        lines = joined(lines, [exchanged(v, b) for v, b in zip(lines, bits)], bits)
    near, far = [], []
    for value, dx, dy in ((lines[0], 1, 0), (lines[1], 0, 1)):
        near.append((value, shifted(value, dx, dy), shifted(value, -dx, -dy)))
        far.append(shifted(value, 2 * dx, 2 * dy))
    return near, far, earlier[1]


BIAS_STEPS = (0, 3, 1, 2)


def column_of(bias):
    count = lax.axis_size("samp")

    def hop(by):
        return lax.ppermute(bias, "samp", [((i + 2 * by) % count, i) for i in range(count)])

    return [bias] + [hop(step) for step in BIAS_STEPS[1:]]


def other_core(value):
    return lax.ppermute(value, "samp", [(i, i ^ 1) for i in range(lax.axis_size("samp"))])


def per_device(
    atom_act,
    atom_gain,
    atom_query,
    atom_keyval,
    atom_output,
    atom_bias,
    key_range,
    atom_token,
    token_counts,
    gather_weight,
    token_gain,
    token_query,
    token_keyval,
    token_output,
    pair_bias,
    trans_gain,
    trans_gate_up,
    trans_down,
    back_weight,
):
    samples, atoms, channels = atom_act.shape
    tokens = token_counts.shape[0]
    device = lax.axis_index("seq")
    count = lax.axis_size("seq")
    to_next = [(i, i + 1) for i in range(count - 1)]
    to_previous = [(i + 1, i) for i in range(count - 1)]

    ranges = key_range.T
    first, last = run_pack(ranges, atom_act, atom_bias)
    after = lax.ppermute(first, "seq", to_previous)
    before = lax.ppermute(last, "seq", to_next)
    pieces = column_of(lax.optimization_barrier((pair_bias, first))[0])
    token_row = atom_token.reshape(1, atoms)
    atom_mid, token_act, token_norm = run_atoms(
        ranges,
        token_counts,
        before,
        after,
        atom_gain.reshape(1, -1),
        token_row,
        token_gain.reshape(1, -1),
        atom_act,
        atom_query,
        atom_keyval,
        atom_bias,
        atom_output,
        gather_weight,
    )
    absorbed = run_queries(token_norm, token_query, token_keyval)
    near, far, ready = spread(token_norm)
    bias_near = run_stack(pieces, BIAS_STEPS, ready)
    bias, turned = run_reorder(bias_near, other_core(bias_near))
    early = run_early(absorbed, bias, turned, near[0] + near[1])
    atom_out, token_out, back_rows = run_late(
        absorbed,
        bias,
        turned,
        far,
        early,
        token_act,
        atom_mid,
        token_row,
        trans_gain.reshape(1, -1),
        [token_keyval, token_output, trans_gate_up, trans_down, back_weight],
    )
    previous = lax.ppermute(back_rows[:, tokens - 1], "seq", to_next)
    earlier = (atom_token[:APT] < device * tokens)[None, :, None]
    extra = jnp.where(earlier, previous[:, None, :].astype(F32), 0.0)
    head = (atom_out[:, :APT].astype(F32) + extra).astype(BF16)
    atom_out = lax.dynamic_update_slice(atom_out, head, (0, 0, 0))
    return (atom_out, token_out)


def solution(mesh):
    placed = (
        P("samp", "seq", None),
        P(),
        P(),
        P(),
        P(),
        P(None, "seq", None, None),
        P("seq", None),
        P("seq"),
        P("seq"),
        P(),
        P(),
        P(),
        P(),
        P(),
        P("samp", "seq", None),
        P(),
        P(),
        P(),
        P(),
    )
    return jax.shard_map(
        per_device,
        mesh=mesh,
        in_specs=placed,
        out_specs=(P("samp", "seq", None), P("samp", "seq", None)),
        check_vma=False,
    )
```

```python
import functools
import math

import jax
import jax.numpy as jnp
from jax import lax
from jax.experimental import pallas as pl
from jax.experimental.pallas import tpu as pltpu
from jax.sharding import PartitionSpec as P

AH = 4
HEADS = 16
WQ = 32
WK = 128
EDGE = 48
APT = 8
BEFORE = EDGE
AFTER = WQ + EDGE
META = 16
GROUP = 8

EPSILON = 1e-05
NEGATIVE = -1e30
F32 = jnp.float32
BF16 = jnp.bfloat16


def cost(flops):
    return pl.CostEstimate(flops=flops, bytes_accessed=1000, transcendentals=0)


NT = (((1,), (1,)), ((), ()))
TN = (((0,), (0,)), ((), ()))


def dot(a, b):
    return jnp.dot(a, b, preferred_element_type=F32)


def dot_nt(a, b):
    return lax.dot_general(a, b, NT, preferred_element_type=F32)


def dot_tn(a, b):
    return lax.dot_general(a, b, TN, preferred_element_type=F32)


def layer_norm(widened, gain):
    centred = widened - jnp.mean(widened, axis=-1, keepdims=True)
    variance = jnp.mean(centred * centred, axis=-1, keepdims=True)
    return (centred * lax.rsqrt(variance + EPSILON) * gain).astype(BF16)


def one_row(flat):
    return jnp.concatenate([flat[i : i + 1] for i in range(flat.shape[0])], axis=1)


def lane_group(rows, lanes, width):
    return lax.broadcasted_iota(jnp.int32, (rows, lanes), 1) // width


def pack_kernel(range_ref, act_hbm, bias_hbm, first_ref, last_ref, sems):
    samples, atoms, _ = act_hbm.shape
    bias_at = samples * AFTER
    meta_at = bias_at + AH * WQ
    copies = []
    for s in range(samples):
        copies.append((act_hbm.at[s, :AFTER], first_ref.at[AFTER * s : AFTER * (s + 1)]))
        copies.append((act_hbm.at[s, atoms - BEFORE :], last_ref.at[BEFORE * s : BEFORE * (s + 1)]))
    for h in range(AH):
        copies.append((bias_hbm.at[h, 0], first_ref.at[bias_at + WQ * h : bias_at + WQ * (h + 1)]))
    started = []
    for i, (source, target) in enumerate(copies):
        copy = pltpu.make_async_copy(source, target, sems.at[i])
        copy.start()
        started.append(copy)
    start = lax.axis_index("seq") * atoms - EDGE
    row = lax.broadcasted_iota(jnp.int32, (META, WK), 0)
    meta = jnp.where(row == 0, range_ref[0, 0] - start, range_ref[1, 0] - start)
    first_ref[meta_at : meta_at + META, :] = meta.astype(F32).astype(BF16)
    for copy in started:
        copy.wait()


def run_pack(key_range, act, bias):
    samples, _, channels = act.shape
    return pl.pallas_call(
        pack_kernel,
        out_shape=(
            jax.ShapeDtypeStruct((samples * AFTER + AH * WQ + META, channels), BF16),
            jax.ShapeDtypeStruct((samples * BEFORE, channels), BF16),
        ),
        in_specs=[smem(), anywhere(), anywhere()],
        out_specs=(vmem(), vmem()),
        scratch_shapes=[pltpu.SemaphoreType.DMA((2 * samples + AH,))],
        compiler_params=pltpu.CompilerParams(vmem_limit_bytes=60 * 2**20),
        name="pack",
    )(key_range, act, bias)


def atom_kernel(
    range_ref,
    count_ref,
    before_ref,
    after_ref,
    gain_ref,
    token_ref,
    token_gain_ref,
    act_hbm,
    query_hbm,
    keyval_hbm,
    bias_hbm,
    output_hbm,
    gather_hbm,
    mid_ref,
    tokact_ref,
    norm_ref,
    act_ref,
    query_ref,
    keyval_ref,
    bias_ref,
    output_ref,
    gather_ref,
    att_ref,
    sems,
):
    copies = []
    for i, (source, target) in enumerate(
        (
            (act_hbm, act_ref),
            (query_hbm, query_ref),
            (keyval_hbm, keyval_ref),
            (bias_hbm, bias_ref),
            (output_hbm, output_ref),
            (gather_hbm, gather_ref),
        )
    ):
        copy = pltpu.make_async_copy(source, target, sems.at[i])
        copy.start()
        copies.append(copy)
    samples, atoms, channels = act_ref.shape
    windows = atoms // WQ
    tokens = norm_ref.shape[1]
    head_width = channels // AH
    scale = 1.0 / math.sqrt(head_width)
    device = lax.axis_index("seq")
    gain = gain_ref[...]
    token_gain = one_row(token_gain_ref[...])
    bias_at = samples * AFTER
    meta_at = bias_at + AH * WQ

    head_of = lane_group(WQ, channels, head_width)
    masks = [(head_of == h).astype(BF16) for h in range(AH)]
    masks32 = [(head_of == h).astype(F32) for h in range(AH)]
    index = lax.broadcasted_iota(jnp.int32, (1, WK), 1)

    meta = after_ref[meta_at : meta_at + META, :].astype(F32)
    indexf = index.astype(F32)
    valid_after = (indexf >= meta[0:1, :]) & (indexf < meta[1:2, :])

    slot = one_row(token_ref[...]) - device * tokens
    own_table = (lax.broadcasted_iota(jnp.int32, (tokens, atoms), 0) == slot).astype(F32)
    own_counts = jnp.sum(own_table, axis=1, keepdims=True)
    own_table = own_table.astype(BF16)
    row = lax.broadcasted_iota(jnp.int32, (tokens, 1), 0)
    remaining = jnp.where(
        row == tokens - 1, count_ref[tokens - 1].astype(F32) - own_counts, jnp.zeros_like(own_counts)
    )
    lane = lax.broadcasted_iota(jnp.int32, (tokens, WQ), 1).astype(F32)
    after_table = (lane < remaining).astype(BF16)
    counts = jnp.maximum(own_counts + remaining, 1.0)

    for copy in copies[:4]:
        copy.wait()
    for s in range(samples):
        extended = jnp.concatenate(
            [
                before_ref[s * BEFORE : (s + 1) * BEFORE, :],
                act_ref[s],
                after_ref[s * AFTER : (s + 1) * AFTER, :],
            ],
            axis=0,
        ).astype(F32)
        normed = layer_norm(extended, gain)
        queries = dot(normed, query_ref[...]).astype(BF16)
        keyvals = dot(normed, keyval_ref[...]).astype(BF16)
        values_ones = jnp.concatenate(
            [keyvals[:, channels:], jnp.ones((keyvals.shape[0], channels), BF16)], axis=1
        )
        for w in range(windows + 1):
            q = queries[BEFORE + WQ * w : BEFORE + WQ * (w + 1), :]
            keys = keyvals[WQ * w : WQ * w + WK, :channels]
            stacked = jnp.concatenate([q * m for m in masks], axis=0)
            scores = dot_nt(stacked, keys) * scale
            if w < windows:
                bias = bias_ref[:, w].reshape(AH * WQ, WK)
                start = (device * windows + w) * WQ - EDGE
                valid = (index >= range_ref[0, w] - start) & (index < range_ref[1, w] - start)
            else:
                bias = after_ref[bias_at : bias_at + AH * WQ, :]
                valid = valid_after
            scores = jnp.where(valid, scores + bias.astype(F32), NEGATIVE)
            exponent = jnp.exp(scores - jnp.max(scores, axis=-1, keepdims=True))
            sums = dot(exponent.astype(BF16), values_ones[WQ * w : WQ * w + WK])
            mixed = sums[:, :channels] / sums[:, channels:]
            attended = mixed[:WQ] * masks32[0]
            for h in range(1, AH):
                attended = attended + mixed[WQ * h : WQ * (h + 1)] * masks32[h]
            att_ref[s, WQ * w : WQ * (w + 1), :] = attended.astype(BF16)
        if s == 0:
            copies[4].wait()
            copies[5].wait()
        merged = dot(att_ref[s], output_ref[...])
        mid = (extended[BEFORE : BEFORE + atoms + WQ, :] + merged).astype(BF16)
        mid_ref[s] = mid[:atoms]
        hidden = jnp.maximum(dot(mid, gather_ref[...]), 0.0).astype(BF16)
        sums = dot(own_table, hidden[:atoms]) + dot(after_table, hidden[atoms:])
        token_act = (sums / counts).astype(BF16)
        tokact_ref[s] = token_act
        norm_ref[s] = layer_norm(token_act.astype(F32), token_gain)


def vmem():
    return pl.BlockSpec(memory_space=pltpu.VMEM)


def smem():
    return pl.BlockSpec(memory_space=pltpu.SMEM)


def anywhere():
    return pl.BlockSpec(memory_space=pl.ANY)


def run_atoms(key_range, counts, before, after, gain, token, token_gain, *arrays):
    samples, atoms, channels = arrays[0].shape
    width = arrays[-1].shape[1]
    tokens = atoms // APT
    return pl.pallas_call(
        atom_kernel,
        out_shape=(
            jax.ShapeDtypeStruct((samples, atoms, channels), BF16),
            jax.ShapeDtypeStruct((samples, tokens, width), BF16),
            jax.ShapeDtypeStruct((samples, tokens, width), BF16),
        ),
        in_specs=[smem()] * 2 + [vmem()] * 5 + [anywhere()] * len(arrays),
        out_specs=(vmem(),) * 3,
        scratch_shapes=[pltpu.VMEM(a.shape, a.dtype) for a in arrays]
        + [
            pltpu.VMEM((samples, atoms + WQ, channels), BF16),
            pltpu.SemaphoreType.DMA((len(arrays),)),
        ],
        compiler_params=pltpu.CompilerParams(vmem_limit_bytes=60 * 2**20),
        cost_estimate=cost(1_000_000),
        name="atoms",
    )(key_range, counts, before, after, gain, token, token_gain, *arrays)


def query_kernel(norm_ref, query_hbm, keyval_hbm, absorbed_ref, query_ref, key_ref, sems):
    samples, tokens, width = norm_ref.shape
    first = pltpu.make_async_copy(query_hbm, query_ref, sems.at[0])
    second = pltpu.make_async_copy(keyval_hbm.at[:, :width], key_ref, sems.at[1])
    first.start()
    second.start()
    head_size = width // HEADS
    scale = 1.0 / math.sqrt(head_size)
    lanes = GROUP * head_size
    head_of = lane_group(tokens, lanes, head_size)
    masks = [(head_of == h).astype(BF16) for h in range(GROUP)]
    first.wait()
    queries = dot(norm_ref[...].reshape(samples * tokens, width), query_ref[...]).astype(BF16)
    second.wait()
    for s in range(samples):
        for g in range(HEADS // GROUP):
            columns = slice(lanes * g, lanes * (g + 1))
            q = queries[tokens * s : tokens * (s + 1), columns]
            stacked = jnp.concatenate([q * m for m in masks], axis=0)
            absorbed = dot_nt(stacked, key_ref[:, columns]) * scale
            absorbed_ref[s, lanes * g : lanes * (g + 1)] = absorbed.astype(BF16)


def run_queries(norm, token_query, token_keyval):
    samples, tokens, width = norm.shape
    return pl.pallas_call(
        query_kernel,
        out_shape=jax.ShapeDtypeStruct((samples, HEADS * tokens, width), BF16),
        in_specs=[vmem(), anywhere(), anywhere()],
        out_specs=vmem(),
        scratch_shapes=[
            pltpu.VMEM((width, width), BF16),
            pltpu.VMEM((width, width), BF16),
            pltpu.SemaphoreType.DMA((2,)),
        ],
        compiler_params=pltpu.CompilerParams(vmem_limit_bytes=30 * 2**20),
        cost_estimate=cost(1_000_000),
        name="queries",
    )(norm, token_query, token_keyval)


def reorder_kernel(near_ref, far_ref, bias_ref, turned_ref):
    columns, heads, _, keys = near_ref.shape
    line = keys // 4
    part = line // 4
    core = lax.axis_index("samp") % 2
    for source, which in ((near_ref, core), (far_ref, 1 - core)):
        for column in range(columns):
            for head in range(heads):
                at = (2 * column + which) * heads + head
                rows = source[column, head]
                bias_ref[at] = rows
                blocks = [
                    rows[:, line * x + part * y : line * x + part * (y + 1)]
                    for y in range(4)
                    for x in range(4)
                ]
                turned_ref[at] = jnp.concatenate(blocks, axis=1)


def run_reorder(near, far):
    columns, heads, tokens, keys = near.shape
    shape = jax.ShapeDtypeStruct((2 * columns * heads, tokens, keys), BF16)
    return pl.pallas_call(
        reorder_kernel,
        out_shape=(shape, shape),
        in_specs=[vmem(), vmem()],
        out_specs=(vmem(), vmem()),
        compiler_params=pltpu.CompilerParams(vmem_limit_bytes=24 * 2**20),
        cost_estimate=cost(2_000_000_000),
        name="reorder",
    )(near, far)


def place(device, sample):
    x, y = device // 8, (device // 2) % 4
    return x if sample % 2 == 0 else y


def piece_scores(q, piece, bias_ref, group, chunk):
    size = piece.shape[0]
    start = pl.multiple_of(chunk * size, 128)
    bias = bias_ref[GROUP * group : GROUP * (group + 1), :, pl.ds(start, size)]
    return dot_nt(q, piece) + bias.reshape(q.shape[0], size).astype(F32)


def early_kernel(
    absorbed_ref,
    bias0_ref,
    bias1_ref,
    own0_ref,
    low0_ref,
    high0_ref,
    own1_ref,
    low1_ref,
    high1_ref,
    mixed_ref,
    best_ref,
    total_ref,
):
    device = lax.axis_index("seq")
    samples = absorbed_ref.shape[0]
    rows_of = absorbed_ref.shape[1] * GROUP // HEADS
    pieces = ((own0_ref, low0_ref, high0_ref), (own1_ref, low1_ref, high1_ref))
    for s in range(samples):
        here = place(device, s)
        for g in range(HEADS // GROUP):
            rows = slice(rows_of * g, rows_of * (g + 1))
            q = absorbed_ref[s, rows]
            scores = [
                piece_scores(q, piece[...], (bias0_ref, bias1_ref)[s], g, (here + step) % 4)
                for piece, step in zip(pieces[s], (0, 3, 1))
            ]
            best = functools.reduce(
                jnp.maximum, [jnp.max(c, axis=-1, keepdims=True) for c in scores]
            )
            total, mixed = 0.0, 0.0
            for piece, c in zip(pieces[s], scores):
                exponent = jnp.exp(c - best)
                total = total + jnp.sum(exponent, axis=-1, keepdims=True)
                mixed = mixed + dot(exponent.astype(BF16), piece[...])
            mixed_ref[s, rows] = mixed
            best_ref[s, rows] = jnp.broadcast_to(best, (rows_of, 128))
            total_ref[s, rows] = jnp.broadcast_to(total, (rows_of, 128))


def run_early(absorbed, bias0, bias1, pieces):
    samples, rows, width = absorbed.shape
    return pl.pallas_call(
        early_kernel,
        out_shape=(
            jax.ShapeDtypeStruct((samples, rows, width), F32),
            jax.ShapeDtypeStruct((samples, rows, 128), F32),
            jax.ShapeDtypeStruct((samples, rows, 128), F32),
        ),
        in_specs=[vmem()] * (3 + len(pieces)),
        out_specs=(vmem(),) * 3,
        compiler_params=pltpu.CompilerParams(vmem_limit_bytes=26 * 2**20),
        cost_estimate=cost(8_000_000_000),
        name="early",
    )(absorbed, bias0, bias1, *pieces)


def late_kernel(
    absorbed_ref,
    bias0_ref,
    bias1_ref,
    far0_ref,
    far1_ref,
    mixed_ref,
    best_ref,
    total_ref,
    tokact_ref,
    mid_ref,
    token_ref,
    gain_ref,
    keyval_hbm,
    output_hbm,
    gate_hbm,
    down_hbm,
    back_hbm,
    atom_out_ref,
    token_out_ref,
    back_rows_ref,
    value_ref,
    output_ref,
    gate_ref,
    down_ref,
    back_ref,
    att_ref,
    weight_sems,
):
    samples, tokens, width = tokact_ref.shape
    head_size = width // HEADS
    device = lax.axis_index("seq")
    weight_copies = []
    for i, (source, target) in enumerate(
        (
            (keyval_hbm.at[:, width:], value_ref),
            (output_hbm, output_ref),
            (gate_hbm, gate_ref),
            (down_hbm, down_ref),
            (back_hbm, back_ref),
        )
    ):
        copy = pltpu.make_async_copy(source, target, weight_sems.at[i])
        copy.start()
        weight_copies.append(copy)

    lanes = GROUP * head_size
    head_of = lane_group(tokens, lanes, head_size)
    masks32 = [(head_of == h).astype(F32) for h in range(GROUP)]
    for s in range(samples):
        far = (place(device, s) + 2) % 4
        piece = (far0_ref, far1_ref)[s][...]
        for g in range(HEADS // GROUP):
            columns = slice(lanes * g, lanes * (g + 1))
            scores = piece_scores(absorbed_ref[s, columns], piece, (bias0_ref, bias1_ref)[s], g, far)
            before = best_ref[s, columns][:, :1]
            best = jnp.maximum(before, jnp.max(scores, axis=-1, keepdims=True))
            exponent = jnp.exp(scores - best)
            shrink = jnp.exp(before - best)
            total = total_ref[s, columns][:, :1] * shrink + jnp.sum(
                exponent, axis=-1, keepdims=True
            )
            mixed = mixed_ref[s, columns] * shrink + dot(exponent.astype(BF16), piece)
            mixed = mixed / total
            if s == 0 and g == 0:
                weight_copies[0].wait()
            valued = dot(mixed.astype(BF16), value_ref[:, columns])
            attended = valued[:tokens] * masks32[0]
            for h in range(1, GROUP):
                attended = attended + valued[tokens * h : tokens * (h + 1)] * masks32[h]
            att_ref[tokens * s : tokens * (s + 1), columns] = attended.astype(BF16)

    weight_copies[1].wait()
    merged = dot(att_ref[...], output_ref[...])
    token_act = tokact_ref[...].reshape(samples * tokens, width).astype(F32)
    token_mid = (token_act + merged).astype(BF16).astype(F32)
    trans = layer_norm(token_mid, one_row(gain_ref[...]))
    weight_copies[2].wait()
    hidden_width = down_ref.shape[0]
    gate = dot(trans, gate_ref[:, :hidden_width])
    up = dot(trans, gate_ref[:, hidden_width:])
    hidden = (gate / (1.0 + jnp.exp(-gate)) * up).astype(BF16)
    weight_copies[3].wait()
    token_out = (token_mid + dot(hidden, down_ref[...])).astype(BF16)
    token_out_ref[...] = token_out.reshape(samples, tokens, width)
    weight_copies[4].wait()
    back_rows = dot(token_out, back_ref[...]).astype(BF16)
    back_rows_ref[...] = back_rows.reshape(samples, tokens, -1)
    atoms = mid_ref.shape[1]
    slot = one_row(token_ref[...]) - device * tokens
    table = (lax.broadcasted_iota(jnp.int32, (tokens, atoms), 0) == slot).astype(BF16)
    for s in range(samples):
        gathered = dot_tn(table, back_rows[tokens * s : tokens * (s + 1)])
        atom_out_ref[s] = (mid_ref[s].astype(F32) + gathered).astype(BF16)


def run_late(absorbed, bias0, bias1, far, early, tokact, mid, token, gain, weights):
    samples, tokens, width = tokact.shape
    return pl.pallas_call(
        late_kernel,
        out_shape=(
            jax.ShapeDtypeStruct(mid.shape, BF16),
            jax.ShapeDtypeStruct(tokact.shape, BF16),
            jax.ShapeDtypeStruct((samples, tokens, mid.shape[2]), BF16),
        ),
        in_specs=[vmem()] * 12 + [anywhere()] * 5,
        out_specs=(vmem(),) * 3,
        scratch_shapes=[pltpu.VMEM((width, width), BF16)]
        + [pltpu.VMEM(w.shape, w.dtype) for w in weights[1:]]
        + [
            pltpu.VMEM((samples * tokens, width), BF16),
            pltpu.SemaphoreType.DMA((len(weights),)),
        ],
        compiler_params=pltpu.CompilerParams(vmem_limit_bytes=28 * 2**20),
        cost_estimate=cost(5_000_000_000),
        name="late",
    )(absorbed, bias0, bias1, *far, *early, tokact, mid, token, gain, *weights)


def shifted(value, dx, dy):
    pairs = []
    for t in range(32):
        x, y, z = t // 8, (t // 2) % 4, t % 2
        pairs.append((t, ((x + dx) % 4) * 8 + ((y + dy) % 4) * 2 + z))
    return lax.ppermute(value, "seq", pairs)


def exchanged(value, axis, bit):
    return lax.ppermute(value, axis, [(t, t ^ (1 << bit)) for t in range(lax.axis_size(axis))])


def join_kernel(axis, bits, *refs):
    count = len(bits)
    device = lax.axis_index(axis)
    for own, other, joined, bit in zip(refs, refs[count:], refs[-count:], bits):
        rows = joined.shape[0] // 2
        where = (device // (1 << bit)) % 2
        joined[pl.ds(pl.multiple_of(where * rows, 16), rows)] = own[...]
        joined[pl.ds(pl.multiple_of((1 - where) * rows, 16), rows)] = other[...]


def joined(own, other, axis, bits, after=()):
    rows, width = own[0].shape
    shape = jax.ShapeDtypeStruct((2 * rows, width), BF16)
    return pl.pallas_call(
        functools.partial(join_kernel, axis, bits),
        out_shape=(shape,) * len(bits),
        in_specs=[vmem()] * (2 * len(bits)) + [anywhere()] * len(after),
        out_specs=(vmem(),) * len(bits),
        compiler_params=pltpu.CompilerParams(vmem_limit_bytes=16 * 2**20),
        cost_estimate=cost(1_000_000),
        name="join",
    )(*own, *other, *after)


def spread(norm):
    other = exchanged(norm, "seq", 0)
    lines = joined([norm[0], norm[1]], [other[0], other[1]], "seq", (0, 0))
    steps = [other]
    for bits in ((1, 3), (2, 4)):
        lines = joined(lines, [exchanged(v, "seq", b) for v, b in zip(lines, bits)], "seq", bits)
        steps.append(lines[1])
    near, far = [], []
    for value, dx, dy in ((lines[0], 1, 0), (lines[1], 0, 1)):
        low = shifted(value, dx, dy)
        near.append((value, low, shifted(value, -dx, -dy)))
        far.append(shifted(low, dx, dy))
    return near, far, steps


def all_heads(bias, steps):
    heads, tokens, keys = bias.shape
    rows = bias.reshape(heads * tokens, keys)
    for bit, after in zip((1, 2), (steps[0], steps[-1])):
        (rows,) = joined([rows], [exchanged(rows, "samp", bit)], "samp", (bit,), (after,))
    shape = (lax.axis_size("samp") // 2, heads, tokens, keys)
    return rows.reshape(shape), exchanged(rows, "samp", 0).reshape(shape)


def per_device(
    atom_act,
    atom_gain,
    atom_query,
    atom_keyval,
    atom_output,
    atom_bias,
    key_range,
    atom_token,
    token_counts,
    gather_weight,
    token_gain,
    token_query,
    token_keyval,
    token_output,
    pair_bias,
    trans_gain,
    trans_gate_up,
    trans_down,
    back_weight,
):
    samples, atoms, channels = atom_act.shape
    tokens = token_counts.shape[0]
    device = lax.axis_index("seq")
    count = lax.axis_size("seq")
    to_next = [(i, i + 1) for i in range(count - 1)]
    to_previous = [(i + 1, i) for i in range(count - 1)]

    ranges = key_range.T
    first, last = run_pack(ranges, atom_act, atom_bias)
    after = lax.ppermute(first, "seq", to_previous)
    before = lax.ppermute(last, "seq", to_next)
    token_row = atom_token.reshape(-1, 128)
    atom_mid, token_act, token_norm = run_atoms(
        ranges,
        token_counts,
        before,
        after,
        atom_gain.reshape(1, -1),
        token_row,
        token_gain.reshape(-1, 128),
        atom_act,
        atom_query,
        atom_keyval,
        atom_bias,
        atom_output,
        gather_weight,
    )
    absorbed = run_queries(token_norm, token_query, token_keyval)
    near, far, steps = spread(token_norm)
    bias, turned = run_reorder(*all_heads(pair_bias, steps))
    early = run_early(absorbed, bias, turned, near[0] + near[1])
    atom_out, token_out, back_rows = run_late(
        absorbed,
        bias,
        turned,
        far,
        early,
        token_act,
        atom_mid,
        token_row,
        trans_gain.reshape(-1, 128),
        [token_keyval, token_output, trans_gate_up, trans_down, back_weight],
    )
    previous = lax.ppermute(back_rows[:, tokens - 1], "seq", to_next)
    earlier = (atom_token[:APT] < device * tokens)[None, :, None]
    extra = jnp.where(earlier, previous[:, None, :].astype(F32), 0.0)
    head = (atom_out[:, :APT].astype(F32) + extra).astype(BF16)
    atom_out = lax.dynamic_update_slice(atom_out, head, (0, 0, 0))
    return (atom_out, token_out)


def solution(mesh):
    placed = (
        P("samp", "seq", None),
        P(),
        P(),
        P(),
        P(),
        P(None, "seq", None, None),
        P("seq", None),
        P("seq"),
        P("seq"),
        P(),
        P(),
        P(),
        P(),
        P(),
        P("samp", "seq", None),
        P(),
        P(),
        P(),
        P(),
    )
    return jax.shard_map(
        per_device,
        mesh=mesh,
        in_specs=placed,
        out_specs=(P("samp", "seq", None), P("samp", "seq", None)),
        check_vma=False,
    )
```

```python
import functools
import math

import jax
import jax.numpy as jnp
from jax import lax
from jax.experimental import pallas as pl
from jax.experimental.pallas import tpu as pltpu
from jax.sharding import PartitionSpec as P

AH = 4
HEADS = 16
WQ = 32
WK = 128
EDGE = 48
APT = 8
BEFORE = EDGE
AFTER = WQ + EDGE
META = 16
GROUP = 8

EPSILON = 1e-05
NEGATIVE = -1e30
F32 = jnp.float32
BF16 = jnp.bfloat16


def cost(flops):
    return pl.CostEstimate(flops=flops, bytes_accessed=1000, transcendentals=0)


NT = (((1,), (1,)), ((), ()))
TN = (((0,), (0,)), ((), ()))


def dot(a, b):
    return jnp.dot(a, b, preferred_element_type=F32)


def dot_nt(a, b):
    return lax.dot_general(a, b, NT, preferred_element_type=F32)


def dot_tn(a, b):
    return lax.dot_general(a, b, TN, preferred_element_type=F32)


def layer_norm(widened, gain):
    centred = widened - jnp.mean(widened, axis=-1, keepdims=True)
    variance = jnp.mean(centred * centred, axis=-1, keepdims=True)
    return (centred * lax.rsqrt(variance + EPSILON) * gain).astype(BF16)


def one_row(flat):
    return jnp.concatenate([flat[i : i + 1] for i in range(flat.shape[0])], axis=1)


def lane_group(rows, lanes, width):
    return lax.broadcasted_iota(jnp.int32, (rows, lanes), 1) // width


def pack_kernel(range_ref, act_hbm, bias_hbm, first_ref, last_ref, sems):
    samples, atoms, _ = act_hbm.shape
    bias_at = samples * AFTER
    meta_at = bias_at + AH * WQ
    copies = []
    for s in range(samples):
        copies.append((act_hbm.at[s, :AFTER], first_ref.at[AFTER * s : AFTER * (s + 1)]))
        copies.append((act_hbm.at[s, atoms - BEFORE :], last_ref.at[BEFORE * s : BEFORE * (s + 1)]))
    for h in range(AH):
        copies.append((bias_hbm.at[h, 0], first_ref.at[bias_at + WQ * h : bias_at + WQ * (h + 1)]))
    started = []
    for i, (source, target) in enumerate(copies):
        copy = pltpu.make_async_copy(source, target, sems.at[i])
        copy.start()
        started.append(copy)
    start = lax.axis_index("seq") * atoms - EDGE
    row = lax.broadcasted_iota(jnp.int32, (META, WK), 0)
    meta = jnp.where(row == 0, range_ref[0, 0] - start, range_ref[1, 0] - start)
    first_ref[meta_at : meta_at + META, :] = meta.astype(F32).astype(BF16)
    for copy in started:
        copy.wait()


def run_pack(key_range, act, bias):
    samples, _, channels = act.shape
    return pl.pallas_call(
        pack_kernel,
        out_shape=(
            jax.ShapeDtypeStruct((samples * AFTER + AH * WQ + META, channels), BF16),
            jax.ShapeDtypeStruct((samples * BEFORE, channels), BF16),
        ),
        in_specs=[smem(), anywhere(), anywhere()],
        out_specs=(vmem(), vmem()),
        scratch_shapes=[pltpu.SemaphoreType.DMA((2 * samples + AH,))],
        compiler_params=pltpu.CompilerParams(vmem_limit_bytes=60 * 2**20),
        name="pack",
    )(key_range, act, bias)


def atom_kernel(
    range_ref,
    count_ref,
    before_ref,
    after_ref,
    gain_ref,
    token_ref,
    token_gain_ref,
    act_hbm,
    query_hbm,
    keyval_hbm,
    bias_hbm,
    output_hbm,
    gather_hbm,
    mid_ref,
    tokact_ref,
    norm_ref,
    act_ref,
    query_ref,
    keyval_ref,
    bias_ref,
    output_ref,
    gather_ref,
    att_ref,
    sems,
):
    copies = []
    for i, (source, target) in enumerate(
        (
            (act_hbm, act_ref),
            (query_hbm, query_ref),
            (keyval_hbm, keyval_ref),
            (bias_hbm, bias_ref),
            (output_hbm, output_ref),
            (gather_hbm, gather_ref),
        )
    ):
        copy = pltpu.make_async_copy(source, target, sems.at[i])
        copy.start()
        copies.append(copy)
    samples, atoms, channels = act_ref.shape
    windows = atoms // WQ
    tokens = norm_ref.shape[1]
    head_width = channels // AH
    scale = 1.0 / math.sqrt(head_width)
    device = lax.axis_index("seq")
    gain = gain_ref[...]
    token_gain = one_row(token_gain_ref[...])
    bias_at = samples * AFTER
    meta_at = bias_at + AH * WQ

    head_of = lane_group(WQ, channels, head_width)
    masks = [(head_of == h).astype(BF16) for h in range(AH)]
    masks32 = [(head_of == h).astype(F32) for h in range(AH)]
    index = lax.broadcasted_iota(jnp.int32, (1, WK), 1)

    meta = after_ref[meta_at : meta_at + META, :].astype(F32)
    indexf = index.astype(F32)
    valid_after = (indexf >= meta[0:1, :]) & (indexf < meta[1:2, :])

    slot = one_row(token_ref[...]) - device * tokens
    own_table = (lax.broadcasted_iota(jnp.int32, (tokens, atoms), 0) == slot).astype(F32)
    own_counts = jnp.sum(own_table, axis=1, keepdims=True)
    own_table = own_table.astype(BF16)
    row = lax.broadcasted_iota(jnp.int32, (tokens, 1), 0)
    remaining = jnp.where(
        row == tokens - 1, count_ref[tokens - 1].astype(F32) - own_counts, jnp.zeros_like(own_counts)
    )
    lane = lax.broadcasted_iota(jnp.int32, (tokens, WQ), 1).astype(F32)
    after_table = (lane < remaining).astype(BF16)
    counts = jnp.maximum(own_counts + remaining, 1.0)

    for copy in copies[:4]:
        copy.wait()
    for s in range(samples):
        extended = jnp.concatenate(
            [
                before_ref[s * BEFORE : (s + 1) * BEFORE, :],
                act_ref[s],
                after_ref[s * AFTER : (s + 1) * AFTER, :],
            ],
            axis=0,
        ).astype(F32)
        normed = layer_norm(extended, gain)
        queries = dot(normed, query_ref[...]).astype(BF16)
        keyvals = dot(normed, keyval_ref[...]).astype(BF16)
        values_ones = jnp.concatenate(
            [keyvals[:, channels:], jnp.ones((keyvals.shape[0], channels), BF16)], axis=1
        )
        for w in range(windows + 1):
            q = queries[BEFORE + WQ * w : BEFORE + WQ * (w + 1), :]
            keys = keyvals[WQ * w : WQ * w + WK, :channels]
            stacked = jnp.concatenate([q * m for m in masks], axis=0)
            scores = dot_nt(stacked, keys) * scale
            if w < windows:
                bias = bias_ref[:, w].reshape(AH * WQ, WK)
                start = (device * windows + w) * WQ - EDGE
                valid = (index >= range_ref[0, w] - start) & (index < range_ref[1, w] - start)
            else:
                bias = after_ref[bias_at : bias_at + AH * WQ, :]
                valid = valid_after
            scores = jnp.where(valid, scores + bias.astype(F32), NEGATIVE)
            exponent = jnp.exp(scores - jnp.max(scores, axis=-1, keepdims=True))
            sums = dot(exponent.astype(BF16), values_ones[WQ * w : WQ * w + WK])
            mixed = sums[:, :channels] / sums[:, channels:]
            attended = mixed[:WQ] * masks32[0]
            for h in range(1, AH):
                attended = attended + mixed[WQ * h : WQ * (h + 1)] * masks32[h]
            att_ref[s, WQ * w : WQ * (w + 1), :] = attended.astype(BF16)
        if s == 0:
            copies[4].wait()
            copies[5].wait()
        merged = dot(att_ref[s], output_ref[...])
        mid = (extended[BEFORE : BEFORE + atoms + WQ, :] + merged).astype(BF16)
        mid_ref[s] = mid[:atoms]
        hidden = jnp.maximum(dot(mid, gather_ref[...]), 0.0).astype(BF16)
        sums = dot(own_table, hidden[:atoms]) + dot(after_table, hidden[atoms:])
        token_act = (sums / counts).astype(BF16)
        tokact_ref[s] = token_act
        norm_ref[s] = layer_norm(token_act.astype(F32), token_gain)


def vmem():
    return pl.BlockSpec(memory_space=pltpu.VMEM)


def smem():
    return pl.BlockSpec(memory_space=pltpu.SMEM)


def anywhere():
    return pl.BlockSpec(memory_space=pl.ANY)


def run_atoms(key_range, counts, before, after, gain, token, token_gain, *arrays):
    samples, atoms, channels = arrays[0].shape
    width = arrays[-1].shape[1]
    tokens = atoms // APT
    return pl.pallas_call(
        atom_kernel,
        out_shape=(
            jax.ShapeDtypeStruct((samples, atoms, channels), BF16),
            jax.ShapeDtypeStruct((samples, tokens, width), BF16),
            jax.ShapeDtypeStruct((samples, tokens, width), BF16),
        ),
        in_specs=[smem()] * 2 + [vmem()] * 5 + [anywhere()] * len(arrays),
        out_specs=(vmem(),) * 3,
        scratch_shapes=[pltpu.VMEM(a.shape, a.dtype) for a in arrays]
        + [
            pltpu.VMEM((samples, atoms + WQ, channels), BF16),
            pltpu.SemaphoreType.DMA((len(arrays),)),
        ],
        compiler_params=pltpu.CompilerParams(vmem_limit_bytes=60 * 2**20),
        cost_estimate=cost(1_000_000),
        name="atoms",
    )(key_range, counts, before, after, gain, token, token_gain, *arrays)


def query_kernel(norm_ref, query_ref, keyval_ref, absorbed_ref):
    samples, tokens, width = norm_ref.shape
    head_size = width // HEADS
    scale = 1.0 / math.sqrt(head_size)
    lanes = GROUP * head_size
    head_of = lane_group(tokens, lanes, head_size)
    masks = [(head_of == h).astype(BF16) for h in range(GROUP)]
    queries = dot(norm_ref[...].reshape(samples * tokens, width), query_ref[...]).astype(BF16)
    for s in range(samples):
        for g in range(HEADS // GROUP):
            columns = slice(lanes * g, lanes * (g + 1))
            q = queries[tokens * s : tokens * (s + 1), columns]
            stacked = jnp.concatenate([q * m for m in masks], axis=0)
            absorbed = dot_nt(stacked, keyval_ref[:, columns]) * scale
            absorbed_ref[s, lanes * g : lanes * (g + 1)] = absorbed.astype(BF16)


def run_queries(norm, token_query, token_keyval):
    samples, tokens, width = norm.shape
    return pl.pallas_call(
        query_kernel,
        out_shape=jax.ShapeDtypeStruct((samples, HEADS * tokens, width), BF16),
        in_specs=[vmem()] * 3,
        out_specs=vmem(),
        compiler_params=pltpu.CompilerParams(vmem_limit_bytes=16 * 2**20),
        cost_estimate=cost(1_000_000),
        name="queries",
    )(norm, token_query, token_keyval)


def reorder_kernel(near_ref, far_ref, bias_ref, turned_ref):
    columns, heads, _, keys = near_ref.shape
    line = keys // 4
    part = line // 4
    core = lax.axis_index("samp") % 2
    for source, which in ((near_ref, core), (far_ref, 1 - core)):
        for column in range(columns):
            for head in range(heads):
                at = (2 * column + which) * heads + head
                rows = source[column, head]
                bias_ref[at] = rows
                blocks = [
                    rows[:, line * x + part * y : line * x + part * (y + 1)]
                    for y in range(4)
                    for x in range(4)
                ]
                turned_ref[at] = jnp.concatenate(blocks, axis=1)


def run_reorder(near, far):
    columns, heads, tokens, keys = near.shape
    shape = jax.ShapeDtypeStruct((2 * columns * heads, tokens, keys), BF16)
    return pl.pallas_call(
        reorder_kernel,
        out_shape=(shape, shape),
        in_specs=[vmem(), vmem()],
        out_specs=(vmem(), vmem()),
        compiler_params=pltpu.CompilerParams(vmem_limit_bytes=24 * 2**20),
        cost_estimate=cost(2_000_000_000),
        name="reorder",
    )(near, far)


def place(device, sample):
    x, y = device // 8, (device // 2) % 4
    return x if sample % 2 == 0 else y


def piece_scores(q, piece, bias_ref, group, chunk):
    size = piece.shape[0]
    start = pl.multiple_of(chunk * size, 128)
    bias = bias_ref[GROUP * group : GROUP * (group + 1), :, pl.ds(start, size)]
    return dot_nt(q, piece) + bias.reshape(q.shape[0], size).astype(F32)


def early_kernel(
    absorbed_ref,
    bias0_ref,
    bias1_ref,
    own0_ref,
    low0_ref,
    high0_ref,
    own1_ref,
    low1_ref,
    high1_ref,
    mixed_ref,
    best_ref,
    total_ref,
):
    device = lax.axis_index("seq")
    samples = absorbed_ref.shape[0]
    rows_of = absorbed_ref.shape[1] * GROUP // HEADS
    pieces = ((own0_ref, low0_ref, high0_ref), (own1_ref, low1_ref, high1_ref))
    for s in range(samples):
        here = place(device, s)
        for g in range(HEADS // GROUP):
            rows = slice(rows_of * g, rows_of * (g + 1))
            q = absorbed_ref[s, rows]
            scores = [
                piece_scores(q, piece[...], (bias0_ref, bias1_ref)[s], g, (here + step) % 4)
                for piece, step in zip(pieces[s], (0, 3, 1))
            ]
            best = functools.reduce(
                jnp.maximum, [jnp.max(c, axis=-1, keepdims=True) for c in scores]
            )
            total, mixed = 0.0, 0.0
            for piece, c in zip(pieces[s], scores):
                exponent = jnp.exp(c - best)
                total = total + jnp.sum(exponent, axis=-1, keepdims=True)
                mixed = mixed + dot(exponent.astype(BF16), piece[...])
            mixed_ref[s, rows] = mixed
            best_ref[s, rows] = jnp.broadcast_to(best, (rows_of, 128))
            total_ref[s, rows] = jnp.broadcast_to(total, (rows_of, 128))


def run_early(absorbed, bias0, bias1, pieces):
    samples, rows, width = absorbed.shape
    return pl.pallas_call(
        early_kernel,
        out_shape=(
            jax.ShapeDtypeStruct((samples, rows, width), F32),
            jax.ShapeDtypeStruct((samples, rows, 128), F32),
            jax.ShapeDtypeStruct((samples, rows, 128), F32),
        ),
        in_specs=[vmem()] * (3 + len(pieces)),
        out_specs=(vmem(),) * 3,
        compiler_params=pltpu.CompilerParams(vmem_limit_bytes=18 * 2**20),
        cost_estimate=cost(8_000_000_000),
        name="early",
    )(absorbed, bias0, bias1, *pieces)


def late_kernel(
    absorbed_ref,
    bias0_ref,
    bias1_ref,
    far0_ref,
    far1_ref,
    mixed_ref,
    best_ref,
    total_ref,
    tokact_ref,
    mid_ref,
    token_ref,
    gain_ref,
    keyval_ref,
    output_ref,
    gate_ref,
    down_ref,
    back_ref,
    atom_out_ref,
    token_out_ref,
    back_rows_ref,
    att_ref,
):
    samples, tokens, width = tokact_ref.shape
    head_size = width // HEADS
    device = lax.axis_index("seq")
    lanes = GROUP * head_size
    head_of = lane_group(tokens, lanes, head_size)
    masks32 = [(head_of == h).astype(F32) for h in range(GROUP)]
    for s in range(samples):
        far = (place(device, s) + 2) % 4
        piece = (far0_ref, far1_ref)[s][...]
        for g in range(HEADS // GROUP):
            columns = slice(lanes * g, lanes * (g + 1))
            scores = piece_scores(absorbed_ref[s, columns], piece, (bias0_ref, bias1_ref)[s], g, far)
            before = best_ref[s, columns][:, :1]
            best = jnp.maximum(before, jnp.max(scores, axis=-1, keepdims=True))
            exponent = jnp.exp(scores - best)
            shrink = jnp.exp(before - best)
            total = total_ref[s, columns][:, :1] * shrink + jnp.sum(
                exponent, axis=-1, keepdims=True
            )
            mixed = mixed_ref[s, columns] * shrink + dot(exponent.astype(BF16), piece)
            mixed = mixed / total
            value_at = slice(width + lanes * g, width + lanes * (g + 1))
            valued = dot(mixed.astype(BF16), keyval_ref[:, value_at])
            attended = valued[:tokens] * masks32[0]
            for h in range(1, GROUP):
                attended = attended + valued[tokens * h : tokens * (h + 1)] * masks32[h]
            att_ref[tokens * s : tokens * (s + 1), columns] = attended.astype(BF16)

    merged = dot(att_ref[...], output_ref[...])
    token_act = tokact_ref[...].reshape(samples * tokens, width).astype(F32)
    token_mid = (token_act + merged).astype(BF16).astype(F32)
    trans = layer_norm(token_mid, one_row(gain_ref[...]))
    hidden_width = down_ref.shape[0]
    gate = dot(trans, gate_ref[:, :hidden_width])
    up = dot(trans, gate_ref[:, hidden_width:])
    hidden = (gate / (1.0 + jnp.exp(-gate)) * up).astype(BF16)
    token_out = (token_mid + dot(hidden, down_ref[...])).astype(BF16)
    token_out_ref[...] = token_out.reshape(samples, tokens, width)
    back_rows = dot(token_out, back_ref[...]).astype(BF16)
    back_rows_ref[...] = back_rows.reshape(samples, tokens, -1)
    atoms = mid_ref.shape[1]
    slot = one_row(token_ref[...]) - device * tokens
    table = (lax.broadcasted_iota(jnp.int32, (tokens, atoms), 0) == slot).astype(BF16)
    for s in range(samples):
        gathered = dot_tn(table, back_rows[tokens * s : tokens * (s + 1)])
        atom_out_ref[s] = (mid_ref[s].astype(F32) + gathered).astype(BF16)


def run_late(absorbed, bias0, bias1, far, early, tokact, mid, token, gain, weights):
    samples, tokens, width = tokact.shape
    return pl.pallas_call(
        late_kernel,
        out_shape=(
            jax.ShapeDtypeStruct(mid.shape, BF16),
            jax.ShapeDtypeStruct(tokact.shape, BF16),
            jax.ShapeDtypeStruct((samples, tokens, mid.shape[2]), BF16),
        ),
        in_specs=[vmem()] * 17,
        out_specs=(vmem(),) * 3,
        scratch_shapes=[pltpu.VMEM((samples * tokens, width), BF16)],
        compiler_params=pltpu.CompilerParams(vmem_limit_bytes=18 * 2**20),
        cost_estimate=cost(5_000_000_000),
        name="late",
    )(absorbed, bias0, bias1, *far, *early, tokact, mid, token, gain, *weights)


def shifted(value, dx, dy):
    pairs = []
    for t in range(32):
        x, y, z = t // 8, (t // 2) % 4, t % 2
        pairs.append((t, ((x + dx) % 4) * 8 + ((y + dy) % 4) * 2 + z))
    return lax.ppermute(value, "seq", pairs)


def exchanged(value, axis, bit):
    return lax.ppermute(value, axis, [(t, t ^ (1 << bit)) for t in range(lax.axis_size(axis))])


def join_kernel(axis, bits, *refs):
    count = len(bits)
    device = lax.axis_index(axis)
    for own, other, joined, bit in zip(refs, refs[count:], refs[-count:], bits):
        rows = joined.shape[0] // 2
        where = (device // (1 << bit)) % 2
        joined[pl.ds(pl.multiple_of(where * rows, 16), rows)] = own[...]
        joined[pl.ds(pl.multiple_of((1 - where) * rows, 16), rows)] = other[...]


def joined(own, other, axis, bits, after=()):
    rows, width = own[0].shape
    shape = jax.ShapeDtypeStruct((2 * rows, width), BF16)
    return pl.pallas_call(
        functools.partial(join_kernel, axis, bits),
        out_shape=(shape,) * len(bits),
        in_specs=[vmem()] * (2 * len(bits)) + [anywhere()] * len(after),
        out_specs=(vmem(),) * len(bits),
        compiler_params=pltpu.CompilerParams(vmem_limit_bytes=16 * 2**20),
        cost_estimate=cost(1_000_000),
        name="join",
    )(*own, *other, *after)


STEPS = (0, 3, 1, 2)


def line_kernel(*refs):
    count = 2 * len(STEPS)
    device = lax.axis_index("seq")
    for s, line in enumerate(refs[count:]):
        at = place(device, s + 1)
        for step, piece in zip(STEPS, refs[len(STEPS) * s :]):
            rows = piece.shape[0]
            start = pl.multiple_of((at + step) % 4 * rows, 16)
            line[pl.ds(start, rows)] = piece[...]


def lines_of(first, second):
    rows, width = first[0].shape
    shape = jax.ShapeDtypeStruct((4 * rows, width), BF16)
    return pl.pallas_call(
        line_kernel,
        out_shape=(shape, shape),
        in_specs=[vmem()] * 8,
        out_specs=(vmem(),) * 2,
        compiler_params=pltpu.CompilerParams(vmem_limit_bytes=16 * 2**20),
        cost_estimate=cost(1_000_000),
        name="lines",
    )(*first, *second)


def pair_kernel(own_ref, other_ref, first_ref, second_ref):
    rows = own_ref.shape[1]
    where = lax.axis_index("seq") % 2
    for s, pair in enumerate((first_ref, second_ref)):
        pair[pl.ds(pl.multiple_of(where * rows, 16), rows)] = own_ref[s]
        pair[pl.ds(pl.multiple_of((1 - where) * rows, 16), rows)] = other_ref[s]


def pairs_of(own, other):
    _, rows, width = own.shape
    shape = jax.ShapeDtypeStruct((2 * rows, width), BF16)
    return pl.pallas_call(
        pair_kernel,
        out_shape=(shape, shape),
        in_specs=[vmem()] * 2,
        out_specs=(vmem(),) * 2,
        compiler_params=pltpu.CompilerParams(vmem_limit_bytes=16 * 2**20),
        cost_estimate=cost(1_000_000),
        name="pairs",
    )(own, other)


def spread(norm):
    other = exchanged(norm, "seq", 0)
    pairs = pairs_of(norm, other)
    around = []
    for value, dx, dy in ((pairs[0], 0, 1), (pairs[1], 1, 0)):
        around.append(
            [value]
            + [shifted(value, by * dx, by * dy) for by in (1, -1, 2)]
        )
    lines = lines_of(*around)
    near, far = [], []
    for value, dx, dy in ((lines[0], 1, 0), (lines[1], 0, 1)):
        low = shifted(value, dx, dy)
        near.append((value, low, shifted(value, -dx, -dy)))
        far.append(shifted(low, dx, dy))
    return near, far, other


def all_heads(bias, steps):
    heads, tokens, keys = bias.shape
    rows = bias.reshape(heads * tokens, keys)
    for bit, after in zip((1, 2), steps):
        (rows,) = joined([rows], [exchanged(rows, "samp", bit)], "samp", (bit,), (after,))
    shape = (lax.axis_size("samp") // 2, heads, tokens, keys)
    return rows.reshape(shape), exchanged(rows, "samp", 0).reshape(shape)


def per_device(
    atom_act,
    atom_gain,
    atom_query,
    atom_keyval,
    atom_output,
    atom_bias,
    key_range,
    atom_token,
    token_counts,
    gather_weight,
    token_gain,
    token_query,
    token_keyval,
    token_output,
    pair_bias,
    trans_gain,
    trans_gate_up,
    trans_down,
    back_weight,
):
    samples, atoms, channels = atom_act.shape
    tokens = token_counts.shape[0]
    device = lax.axis_index("seq")
    count = lax.axis_size("seq")
    to_next = [(i, i + 1) for i in range(count - 1)]
    to_previous = [(i + 1, i) for i in range(count - 1)]

    ranges = key_range.T
    first, last = run_pack(ranges, atom_act, atom_bias)
    after = lax.ppermute(first, "seq", to_previous)
    before = lax.ppermute(last, "seq", to_next)
    token_row = atom_token.reshape(-1, 128)
    atom_mid, token_act, token_norm = run_atoms(
        ranges,
        token_counts,
        before,
        after,
        atom_gain.reshape(1, -1),
        token_row,
        token_gain.reshape(-1, 128),
        atom_act,
        atom_query,
        atom_keyval,
        atom_bias,
        atom_output,
        gather_weight,
    )
    absorbed = run_queries(token_norm, token_query, token_keyval)
    near, far, ready = spread(token_norm)
    bias, turned = run_reorder(*all_heads(pair_bias, (ready, near[1][0])))
    early = run_early(absorbed, bias, turned, near[0] + near[1])
    atom_out, token_out, back_rows = run_late(
        absorbed,
        bias,
        turned,
        far,
        early,
        token_act,
        atom_mid,
        token_row,
        trans_gain.reshape(-1, 128),
        [token_keyval, token_output, trans_gate_up, trans_down, back_weight],
    )
    previous = lax.ppermute(back_rows[:, tokens - 1], "seq", to_next)
    earlier = (atom_token[:APT] < device * tokens)[None, :, None]
    extra = jnp.where(earlier, previous[:, None, :].astype(F32), 0.0)
    head = (atom_out[:, :APT].astype(F32) + extra).astype(BF16)
    atom_out = lax.dynamic_update_slice(atom_out, head, (0, 0, 0))
    return (atom_out, token_out)


def solution(mesh):
    placed = (
        P("samp", "seq", None),
        P(),
        P(),
        P(),
        P(),
        P(None, "seq", None, None),
        P("seq", None),
        P("seq"),
        P("seq"),
        P(),
        P(),
        P(),
        P(),
        P(),
        P("samp", "seq", None),
        P(),
        P(),
        P(),
        P(),
    )
    return jax.shard_map(
        per_device,
        mesh=mesh,
        in_specs=placed,
        out_specs=(P("samp", "seq", None), P("samp", "seq", None)),
        check_vma=False,
    )
```

```python
import functools
import math

import jax
import jax.numpy as jnp
from jax import lax
from jax.experimental import pallas as pl
from jax.experimental.pallas import tpu as pltpu
from jax.sharding import PartitionSpec as P

AH = 4
HEADS = 16
WQ = 32
WK = 128
EDGE = 48
APT = 8
BEFORE = EDGE
AFTER = WQ + EDGE
META = 16
GROUP = 8

EPSILON = 1e-05
NEGATIVE = -1e30
F32 = jnp.float32
BF16 = jnp.bfloat16


def cost(flops):
    return pl.CostEstimate(flops=flops, bytes_accessed=1000, transcendentals=0)


NT = (((1,), (1,)), ((), ()))
TN = (((0,), (0,)), ((), ()))


def dot(a, b):
    return jnp.dot(a, b, preferred_element_type=F32)


def dot_nt(a, b):
    return lax.dot_general(a, b, NT, preferred_element_type=F32)


def dot_tn(a, b):
    return lax.dot_general(a, b, TN, preferred_element_type=F32)


def layer_norm(widened, gain):
    centred = widened - jnp.mean(widened, axis=-1, keepdims=True)
    variance = jnp.mean(centred * centred, axis=-1, keepdims=True)
    return (centred * lax.rsqrt(variance + EPSILON) * gain).astype(BF16)


def one_row(flat):
    return jnp.concatenate([flat[i : i + 1] for i in range(flat.shape[0])], axis=1)


def lane_group(rows, lanes, width):
    return lax.broadcasted_iota(jnp.int32, (rows, lanes), 1) // width


def pack_kernel(range_ref, act_hbm, bias_hbm, first_ref, last_ref, sems):
    samples, atoms, _ = act_hbm.shape
    bias_at = samples * AFTER
    meta_at = bias_at + AH * WQ
    copies = []
    for s in range(samples):
        copies.append((act_hbm.at[s, :AFTER], first_ref.at[AFTER * s : AFTER * (s + 1)]))
        copies.append((act_hbm.at[s, atoms - BEFORE :], last_ref.at[BEFORE * s : BEFORE * (s + 1)]))
    for h in range(AH):
        copies.append((bias_hbm.at[h, 0], first_ref.at[bias_at + WQ * h : bias_at + WQ * (h + 1)]))
    started = []
    for i, (source, target) in enumerate(copies):
        copy = pltpu.make_async_copy(source, target, sems.at[i])
        copy.start()
        started.append(copy)
    start = lax.axis_index("seq") * atoms - EDGE
    row = lax.broadcasted_iota(jnp.int32, (META, WK), 0)
    meta = jnp.where(row == 0, range_ref[0, 0] - start, range_ref[1, 0] - start)
    first_ref[meta_at : meta_at + META, :] = meta.astype(F32).astype(BF16)
    for copy in started:
        copy.wait()


def run_pack(key_range, act, bias):
    samples, _, channels = act.shape
    return pl.pallas_call(
        pack_kernel,
        out_shape=(
            jax.ShapeDtypeStruct((samples * AFTER + AH * WQ + META, channels), BF16),
            jax.ShapeDtypeStruct((samples * BEFORE, channels), BF16),
        ),
        in_specs=[smem(), anywhere(), anywhere()],
        out_specs=(vmem(), vmem()),
        scratch_shapes=[pltpu.SemaphoreType.DMA((2 * samples + AH,))],
        compiler_params=pltpu.CompilerParams(vmem_limit_bytes=60 * 2**20),
        name="pack",
    )(key_range, act, bias)


def atom_kernel(
    range_ref,
    count_ref,
    before_ref,
    after_ref,
    gain_ref,
    token_ref,
    token_gain_ref,
    act_hbm,
    query_hbm,
    keyval_hbm,
    bias_hbm,
    output_hbm,
    gather_hbm,
    mid_ref,
    tokact_ref,
    norm_ref,
    act_ref,
    query_ref,
    keyval_ref,
    bias_ref,
    output_ref,
    gather_ref,
    att_ref,
    sems,
):
    copies = []
    for i, (source, target) in enumerate(
        (
            (act_hbm, act_ref),
            (query_hbm, query_ref),
            (keyval_hbm, keyval_ref),
            (bias_hbm, bias_ref),
            (output_hbm, output_ref),
            (gather_hbm, gather_ref),
        )
    ):
        copy = pltpu.make_async_copy(source, target, sems.at[i])
        copy.start()
        copies.append(copy)
    samples, atoms, channels = act_ref.shape
    windows = atoms // WQ
    tokens = norm_ref.shape[1]
    head_width = channels // AH
    scale = 1.0 / math.sqrt(head_width)
    device = lax.axis_index("seq")
    gain = gain_ref[...]
    token_gain = one_row(token_gain_ref[...])
    bias_at = samples * AFTER
    meta_at = bias_at + AH * WQ

    head_of = lane_group(WQ, channels, head_width)
    masks = [(head_of == h).astype(BF16) for h in range(AH)]
    masks32 = [(head_of == h).astype(F32) for h in range(AH)]
    index = lax.broadcasted_iota(jnp.int32, (1, WK), 1)

    meta = after_ref[meta_at : meta_at + META, :].astype(F32)
    indexf = index.astype(F32)
    valid_after = (indexf >= meta[0:1, :]) & (indexf < meta[1:2, :])

    slot = one_row(token_ref[...]) - device * tokens
    own_table = (lax.broadcasted_iota(jnp.int32, (tokens, atoms), 0) == slot).astype(F32)
    own_counts = jnp.sum(own_table, axis=1, keepdims=True)
    own_table = own_table.astype(BF16)
    row = lax.broadcasted_iota(jnp.int32, (tokens, 1), 0)
    remaining = jnp.where(
        row == tokens - 1, count_ref[tokens - 1].astype(F32) - own_counts, jnp.zeros_like(own_counts)
    )
    lane = lax.broadcasted_iota(jnp.int32, (tokens, WQ), 1).astype(F32)
    after_table = (lane < remaining).astype(BF16)
    counts = jnp.maximum(own_counts + remaining, 1.0)

    for copy in copies[:4]:
        copy.wait()
    for s in range(samples):
        extended = jnp.concatenate(
            [
                before_ref[s * BEFORE : (s + 1) * BEFORE, :],
                act_ref[s],
                after_ref[s * AFTER : (s + 1) * AFTER, :],
            ],
            axis=0,
        ).astype(F32)
        normed = layer_norm(extended, gain)
        queries = dot(normed, query_ref[...]).astype(BF16)
        keyvals = dot(normed, keyval_ref[...]).astype(BF16)
        values_ones = jnp.concatenate(
            [keyvals[:, channels:], jnp.ones((keyvals.shape[0], channels), BF16)], axis=1
        )
        for w in range(windows + 1):
            q = queries[BEFORE + WQ * w : BEFORE + WQ * (w + 1), :]
            keys = keyvals[WQ * w : WQ * w + WK, :channels]
            stacked = jnp.concatenate([q * m for m in masks], axis=0)
            scores = dot_nt(stacked, keys) * scale
            if w < windows:
                bias = bias_ref[:, w].reshape(AH * WQ, WK)
                start = (device * windows + w) * WQ - EDGE
                valid = (index >= range_ref[0, w] - start) & (index < range_ref[1, w] - start)
            else:
                bias = after_ref[bias_at : bias_at + AH * WQ, :]
                valid = valid_after
            scores = jnp.where(valid, scores + bias.astype(F32), NEGATIVE)
            exponent = jnp.exp(scores - jnp.max(scores, axis=-1, keepdims=True))
            sums = dot(exponent.astype(BF16), values_ones[WQ * w : WQ * w + WK])
            mixed = sums[:, :channels] / sums[:, channels:]
            attended = mixed[:WQ] * masks32[0]
            for h in range(1, AH):
                attended = attended + mixed[WQ * h : WQ * (h + 1)] * masks32[h]
            att_ref[s, WQ * w : WQ * (w + 1), :] = attended.astype(BF16)
        if s == 0:
            copies[4].wait()
            copies[5].wait()
        merged = dot(att_ref[s], output_ref[...])
        mid = (extended[BEFORE : BEFORE + atoms + WQ, :] + merged).astype(BF16)
        mid_ref[s] = mid[:atoms]
        hidden = jnp.maximum(dot(mid, gather_ref[...]), 0.0).astype(BF16)
        sums = dot(own_table, hidden[:atoms]) + dot(after_table, hidden[atoms:])
        token_act = (sums / counts).astype(BF16)
        tokact_ref[s] = token_act
        norm_ref[s] = layer_norm(token_act.astype(F32), token_gain)


def vmem():
    return pl.BlockSpec(memory_space=pltpu.VMEM)


def smem():
    return pl.BlockSpec(memory_space=pltpu.SMEM)


def anywhere():
    return pl.BlockSpec(memory_space=pl.ANY)


def run_atoms(key_range, counts, before, after, gain, token, token_gain, *arrays):
    samples, atoms, channels = arrays[0].shape
    width = arrays[-1].shape[1]
    tokens = atoms // APT
    return pl.pallas_call(
        atom_kernel,
        out_shape=(
            jax.ShapeDtypeStruct((samples, atoms, channels), BF16),
            jax.ShapeDtypeStruct((samples, tokens, width), BF16),
            jax.ShapeDtypeStruct((samples, tokens, width), BF16),
        ),
        in_specs=[smem()] * 2 + [vmem()] * 5 + [anywhere()] * len(arrays),
        out_specs=(vmem(),) * 3,
        scratch_shapes=[pltpu.VMEM(a.shape, a.dtype) for a in arrays]
        + [
            pltpu.VMEM((samples, atoms + WQ, channels), BF16),
            pltpu.SemaphoreType.DMA((len(arrays),)),
        ],
        compiler_params=pltpu.CompilerParams(vmem_limit_bytes=60 * 2**20),
        cost_estimate=cost(1_000_000),
        name="atoms",
    )(key_range, counts, before, after, gain, token, token_gain, *arrays)


def query_kernel(norm_ref, query_ref, keyval_ref, after_hbm, absorbed_ref):
    samples, tokens, width = norm_ref.shape
    head_size = width // HEADS
    scale = 1.0 / math.sqrt(head_size)
    lanes = GROUP * head_size
    head_of = lane_group(tokens, lanes, head_size)
    masks = [(head_of == h).astype(BF16) for h in range(GROUP)]
    queries = dot(norm_ref[...].reshape(samples * tokens, width), query_ref[...]).astype(BF16)
    for s in range(samples):
        for g in range(HEADS // GROUP):
            columns = slice(lanes * g, lanes * (g + 1))
            q = queries[tokens * s : tokens * (s + 1), columns]
            stacked = jnp.concatenate([q * m for m in masks], axis=0)
            absorbed = dot_nt(stacked, keyval_ref[:, columns]) * scale
            absorbed_ref[s, lanes * g : lanes * (g + 1)] = absorbed.astype(BF16)


def run_queries(norm, token_query, token_keyval, after):
    samples, tokens, width = norm.shape
    return pl.pallas_call(
        query_kernel,
        out_shape=jax.ShapeDtypeStruct((samples, HEADS * tokens, width), BF16),
        in_specs=[vmem()] * 3 + [anywhere()],
        out_specs=vmem(),
        compiler_params=pltpu.CompilerParams(vmem_limit_bytes=16 * 2**20),
        cost_estimate=cost(1000000),
        name="queries",
    )(norm, token_query, token_keyval, after)


def reorder_kernel(near_ref, near_far_ref, other_ref, other_far_ref, bias_ref, turned_ref):
    columns, heads, _, keys = near_ref.shape
    line = keys // 4
    part = line // 4
    place_of = lax.axis_index("samp")
    core, upper = place_of % 2, place_of // (2 * columns)
    for source, which, half in (
        (near_ref, core, upper),
        (near_far_ref, core, 1 - upper),
        (other_ref, 1 - core, upper),
        (other_far_ref, 1 - core, 1 - upper),
    ):
        for column in range(columns):
            for head in range(heads):
                at = (2 * (columns * half + column) + which) * heads + head
                rows = source[column, head]
                bias_ref[at] = rows
                blocks = [
                    rows[:, line * x + part * y : line * x + part * (y + 1)]
                    for y in range(4)
                    for x in range(4)
                ]
                turned_ref[at] = jnp.concatenate(blocks, axis=1)


def run_reorder(parts):
    columns, heads, tokens, keys = parts[0].shape
    shape = jax.ShapeDtypeStruct((4 * columns * heads, tokens, keys), BF16)
    return pl.pallas_call(
        reorder_kernel,
        out_shape=(shape, shape),
        in_specs=[vmem()] * 4,
        out_specs=(vmem(), vmem()),
        compiler_params=pltpu.CompilerParams(vmem_limit_bytes=24 * 2**20),
        cost_estimate=cost(4000000000),
        name="reorder",
    )(*parts)


def place(device, sample):
    x, y = device // 8, (device // 2) % 4
    return x if sample % 2 == 0 else y


def piece_scores(q, piece, bias_ref, group, chunk):
    size = piece.shape[0]
    start = pl.multiple_of(chunk * size, 128)
    bias = bias_ref[GROUP * group : GROUP * (group + 1), :, pl.ds(start, size)]
    return dot_nt(q, piece) + bias.reshape(q.shape[0], size).astype(F32)


def early_kernel(
    absorbed_ref,
    bias0_ref,
    bias1_ref,
    own0_ref,
    low0_ref,
    high0_ref,
    own1_ref,
    low1_ref,
    high1_ref,
    mixed_ref,
    best_ref,
    total_ref,
):
    device = lax.axis_index("seq")
    samples = absorbed_ref.shape[0]
    rows_of = absorbed_ref.shape[1] * GROUP // HEADS
    pieces = ((own0_ref, low0_ref, high0_ref), (own1_ref, low1_ref, high1_ref))
    for s in range(samples):
        here = place(device, s)
        for g in range(HEADS // GROUP):
            rows = slice(rows_of * g, rows_of * (g + 1))
            q = absorbed_ref[s, rows]
            scores = [
                piece_scores(q, piece[...], (bias0_ref, bias1_ref)[s], g, (here + step) % 4)
                for piece, step in zip(pieces[s], (0, 3, 1))
            ]
            best = functools.reduce(
                jnp.maximum, [jnp.max(c, axis=-1, keepdims=True) for c in scores]
            )
            total, mixed = 0.0, 0.0
            for piece, c in zip(pieces[s], scores):
                exponent = jnp.exp(c - best)
                total = total + jnp.sum(exponent, axis=-1, keepdims=True)
                mixed = mixed + dot(exponent.astype(BF16), piece[...])
            mixed_ref[s, rows] = mixed
            best_ref[s, rows] = jnp.broadcast_to(best, (rows_of, 128))
            total_ref[s, rows] = jnp.broadcast_to(total, (rows_of, 128))


def run_early(absorbed, bias0, bias1, pieces):
    samples, rows, width = absorbed.shape
    return pl.pallas_call(
        early_kernel,
        out_shape=(
            jax.ShapeDtypeStruct((samples, rows, width), F32),
            jax.ShapeDtypeStruct((samples, rows, 128), F32),
            jax.ShapeDtypeStruct((samples, rows, 128), F32),
        ),
        in_specs=[vmem()] * (3 + len(pieces)),
        out_specs=(vmem(),) * 3,
        compiler_params=pltpu.CompilerParams(vmem_limit_bytes=18 * 2**20),
        cost_estimate=cost(8000000000),
        name="early",
    )(absorbed, bias0, bias1, *pieces)


def late_kernel(
    absorbed_ref,
    bias0_ref,
    bias1_ref,
    far0_ref,
    far1_ref,
    mixed_ref,
    best_ref,
    total_ref,
    tokact_ref,
    mid_ref,
    token_ref,
    gain_ref,
    keyval_ref,
    output_ref,
    gate_ref,
    down_ref,
    back_ref,
    atom_out_ref,
    token_out_ref,
    back_rows_ref,
    att_ref,
):
    samples, tokens, width = tokact_ref.shape
    head_size = width // HEADS
    device = lax.axis_index("seq")
    lanes = GROUP * head_size
    head_of = lane_group(tokens, lanes, head_size)
    masks32 = [(head_of == h).astype(F32) for h in range(GROUP)]
    for s in range(samples):
        far = (place(device, s) + 2) % 4
        piece = (far0_ref, far1_ref)[s][...]
        for g in range(HEADS // GROUP):
            columns = slice(lanes * g, lanes * (g + 1))
            scores = piece_scores(absorbed_ref[s, columns], piece, (bias0_ref, bias1_ref)[s], g, far)
            before = best_ref[s, columns][:, :1]
            best = jnp.maximum(before, jnp.max(scores, axis=-1, keepdims=True))
            exponent = jnp.exp(scores - best)
            shrink = jnp.exp(before - best)
            total = total_ref[s, columns][:, :1] * shrink + jnp.sum(
                exponent, axis=-1, keepdims=True
            )
            mixed = mixed_ref[s, columns] * shrink + dot(exponent.astype(BF16), piece)
            mixed = mixed / total
            value_at = slice(width + lanes * g, width + lanes * (g + 1))
            valued = dot(mixed.astype(BF16), keyval_ref[:, value_at])
            attended = valued[:tokens] * masks32[0]
            for h in range(1, GROUP):
                attended = attended + valued[tokens * h : tokens * (h + 1)] * masks32[h]
            att_ref[tokens * s : tokens * (s + 1), columns] = attended.astype(BF16)

    merged = dot(att_ref[...], output_ref[...])
    token_act = tokact_ref[...].reshape(samples * tokens, width).astype(F32)
    token_mid = (token_act + merged).astype(BF16).astype(F32)
    trans = layer_norm(token_mid, one_row(gain_ref[...]))
    hidden_width = down_ref.shape[0]
    gate = dot(trans, gate_ref[:, :hidden_width])
    up = dot(trans, gate_ref[:, hidden_width:])
    hidden = (gate / (1.0 + jnp.exp(-gate)) * up).astype(BF16)
    token_out = (token_mid + dot(hidden, down_ref[...])).astype(BF16)
    token_out_ref[...] = token_out.reshape(samples, tokens, width)
    back_rows = dot(token_out, back_ref[...]).astype(BF16)
    back_rows_ref[...] = back_rows.reshape(samples, tokens, -1)
    atoms = mid_ref.shape[1]
    slot = one_row(token_ref[...]) - device * tokens
    table = (lax.broadcasted_iota(jnp.int32, (tokens, atoms), 0) == slot).astype(BF16)
    for s in range(samples):
        gathered = dot_tn(table, back_rows[tokens * s : tokens * (s + 1)])
        atom_out_ref[s] = (mid_ref[s].astype(F32) + gathered).astype(BF16)


def run_late(absorbed, bias0, bias1, far, early, tokact, mid, token, gain, weights):
    samples, tokens, width = tokact.shape
    return pl.pallas_call(
        late_kernel,
        out_shape=(
            jax.ShapeDtypeStruct(mid.shape, BF16),
            jax.ShapeDtypeStruct(tokact.shape, BF16),
            jax.ShapeDtypeStruct((samples, tokens, mid.shape[2]), BF16),
        ),
        in_specs=[vmem()] * 17,
        out_specs=(vmem(),) * 3,
        scratch_shapes=[pltpu.VMEM((samples * tokens, width), BF16)],
        compiler_params=pltpu.CompilerParams(vmem_limit_bytes=18 * 2**20),
        cost_estimate=cost(5_000_000_000),
        name="late",
    )(absorbed, bias0, bias1, *far, *early, tokact, mid, token, gain, *weights)


def shifted(value, dx, dy):
    pairs = []
    for t in range(32):
        x, y, z = t // 8, (t // 2) % 4, t % 2
        pairs.append((t, ((x + dx) % 4) * 8 + ((y + dy) % 4) * 2 + z))
    return lax.ppermute(value, "seq", pairs)


def exchanged(value, axis, bit):
    return lax.ppermute(value, axis, [(t, t ^ (1 << bit)) for t in range(lax.axis_size(axis))])


def join_kernel(axis, bits, *refs):
    count = len(bits)
    device = lax.axis_index(axis)
    for own, other, joined, bit in zip(refs, refs[count:], refs[-count:], bits):
        rows = joined.shape[0] // 2
        where = (device // (1 << bit)) % 2
        joined[pl.ds(pl.multiple_of(where * rows, 16), rows)] = own[...]
        joined[pl.ds(pl.multiple_of((1 - where) * rows, 16), rows)] = other[...]


def joined(own, other, axis, bits, after=()):
    rows, width = own[0].shape
    shape = jax.ShapeDtypeStruct((2 * rows, width), BF16)
    return pl.pallas_call(
        functools.partial(join_kernel, axis, bits),
        out_shape=(shape,) * len(bits),
        in_specs=[vmem()] * (2 * len(bits)) + [anywhere()] * len(after),
        out_specs=(vmem(),) * len(bits),
        compiler_params=pltpu.CompilerParams(vmem_limit_bytes=16 * 2**20),
        cost_estimate=cost(1_000_000),
        name="join",
    )(*own, *other, *after)


def spread(norm):
    other = exchanged(norm, "seq", 0)
    lines = joined([norm[0], norm[1]], [other[0], other[1]], "seq", (0, 0))
    for bits in ((1, 3), (2, 4)):
        lines = joined(lines, [exchanged(v, "seq", b) for v, b in zip(lines, bits)], "seq", bits)
    near, far = [], []
    for value, dx, dy in ((lines[0], 1, 0), (lines[1], 0, 1)):
        low = shifted(value, dx, dy)
        near.append((value, low, shifted(value, -dx, -dy)))
        far.append(shifted(low, dx, dy))
    return near, far, other


def all_heads(bias, ready):
    heads, tokens, keys = bias.shape
    rows = bias.reshape(heads * tokens, keys)
    (pair,) = joined([rows], [exchanged(rows, "samp", 1)], "samp", (1,), (ready,))
    other_pair = exchanged(pair, "samp", 0)
    beyond = exchanged(pair, "samp", 2)
    parts = (pair, beyond, other_pair, exchanged(beyond, "samp", 0))
    return [part.reshape(2, heads, tokens, keys) for part in parts]


def per_device(
    atom_act,
    atom_gain,
    atom_query,
    atom_keyval,
    atom_output,
    atom_bias,
    key_range,
    atom_token,
    token_counts,
    gather_weight,
    token_gain,
    token_query,
    token_keyval,
    token_output,
    pair_bias,
    trans_gain,
    trans_gate_up,
    trans_down,
    back_weight,
):
    samples, atoms, channels = atom_act.shape
    tokens = token_counts.shape[0]
    device = lax.axis_index("seq")
    count = lax.axis_size("seq")
    to_next = [(i, i + 1) for i in range(count - 1)]
    to_previous = [(i + 1, i) for i in range(count - 1)]

    ranges = key_range.T
    first, last = run_pack(ranges, atom_act, atom_bias)
    after = lax.ppermute(first, "seq", to_previous)
    before = lax.ppermute(last, "seq", to_next)
    token_row = atom_token.reshape(-1, 128)
    atom_mid, token_act, token_norm = run_atoms(
        ranges,
        token_counts,
        before,
        after,
        atom_gain.reshape(1, -1),
        token_row,
        token_gain.reshape(-1, 128),
        atom_act,
        atom_query,
        atom_keyval,
        atom_bias,
        atom_output,
        gather_weight,
    )
    near, far, ready = spread(token_norm)
    absorbed = run_queries(token_norm, token_query, token_keyval, token_norm)
    bias, turned = run_reorder(all_heads(pair_bias, ready))
    early = run_early(absorbed, bias, turned, near[0] + near[1])
    atom_out, token_out, back_rows = run_late(
        absorbed,
        bias,
        turned,
        far,
        early,
        token_act,
        atom_mid,
        token_row,
        trans_gain.reshape(-1, 128),
        [token_keyval, token_output, trans_gate_up, trans_down, back_weight],
    )
    previous = lax.ppermute(back_rows[:, tokens - 1], "seq", to_next)
    earlier = (atom_token[:APT] < device * tokens)[None, :, None]
    extra = jnp.where(earlier, previous[:, None, :].astype(F32), 0.0)
    head = (atom_out[:, :APT].astype(F32) + extra).astype(BF16)
    atom_out = lax.dynamic_update_slice(atom_out, head, (0, 0, 0))
    return (atom_out, token_out)


def solution(mesh):
    placed = (
        P("samp", "seq", None),
        P(),
        P(),
        P(),
        P(),
        P(None, "seq", None, None),
        P("seq", None),
        P("seq"),
        P("seq"),
        P(),
        P(),
        P(),
        P(),
        P(),
        P("samp", "seq", None),
        P(),
        P(),
        P(),
        P(),
    )
    return jax.shard_map(
        per_device,
        mesh=mesh,
        in_specs=placed,
        out_specs=(P("samp", "seq", None), P("samp", "seq", None)),
        check_vma=False,
    )
```

```python
import functools
import math

import jax
import jax.numpy as jnp
from jax import lax
from jax.experimental import pallas as pl
from jax.experimental.pallas import tpu as pltpu
from jax.sharding import PartitionSpec as P

AH = 4
HEADS = 16
WQ = 32
WK = 128
EDGE = 48
APT = 8
BEFORE = EDGE
AFTER = WQ + EDGE
META = 16
GROUP = 8

EPSILON = 1e-05
NEGATIVE = -1e30
F32 = jnp.float32
BF16 = jnp.bfloat16


def cost(flops):
    return pl.CostEstimate(flops=flops, bytes_accessed=1000, transcendentals=0)


NT = (((1,), (1,)), ((), ()))
TN = (((0,), (0,)), ((), ()))


def dot(a, b):
    return jnp.dot(a, b, preferred_element_type=F32)


def dot_nt(a, b):
    return lax.dot_general(a, b, NT, preferred_element_type=F32)


def dot_tn(a, b):
    return lax.dot_general(a, b, TN, preferred_element_type=F32)


def layer_norm(widened, gain):
    centred = widened - jnp.mean(widened, axis=-1, keepdims=True)
    variance = jnp.mean(centred * centred, axis=-1, keepdims=True)
    return (centred * lax.rsqrt(variance + EPSILON) * gain).astype(BF16)


def one_row(flat):
    return jnp.concatenate([flat[i : i + 1] for i in range(flat.shape[0])], axis=1)


def lane_group(rows, lanes, width):
    return lax.broadcasted_iota(jnp.int32, (rows, lanes), 1) // width


def pack_kernel(range_ref, act_hbm, bias_hbm, first_ref, last_ref, sems):
    samples, atoms, _ = act_hbm.shape
    bias_at = samples * AFTER
    meta_at = bias_at + AH * WQ
    copies = []
    for s in range(samples):
        copies.append((act_hbm.at[s, :AFTER], first_ref.at[AFTER * s : AFTER * (s + 1)]))
        copies.append((act_hbm.at[s, atoms - BEFORE :], last_ref.at[BEFORE * s : BEFORE * (s + 1)]))
    for h in range(AH):
        copies.append((bias_hbm.at[h, 0], first_ref.at[bias_at + WQ * h : bias_at + WQ * (h + 1)]))
    started = []
    for i, (source, target) in enumerate(copies):
        copy = pltpu.make_async_copy(source, target, sems.at[i])
        copy.start()
        started.append(copy)
    start = lax.axis_index("seq") * atoms - EDGE
    row = lax.broadcasted_iota(jnp.int32, (META, WK), 0)
    meta = jnp.where(row == 0, range_ref[0, 0] - start, range_ref[1, 0] - start)
    first_ref[meta_at : meta_at + META, :] = meta.astype(F32).astype(BF16)
    for copy in started:
        copy.wait()


def run_pack(key_range, act, bias):
    samples, _, channels = act.shape
    return pl.pallas_call(
        pack_kernel,
        out_shape=(
            jax.ShapeDtypeStruct((samples * AFTER + AH * WQ + META, channels), BF16),
            jax.ShapeDtypeStruct((samples * BEFORE, channels), BF16),
        ),
        in_specs=[smem(), anywhere(), anywhere()],
        out_specs=(vmem(), vmem()),
        scratch_shapes=[pltpu.SemaphoreType.DMA((2 * samples + AH,))],
        compiler_params=pltpu.CompilerParams(vmem_limit_bytes=60 * 2**20),
        name="pack",
    )(key_range, act, bias)


def atom_kernel(
    range_ref,
    count_ref,
    before_ref,
    after_ref,
    gain_ref,
    token_ref,
    token_gain_ref,
    act_hbm,
    query_hbm,
    keyval_hbm,
    bias_hbm,
    output_hbm,
    gather_hbm,
    mid_ref,
    tokact_ref,
    norm_ref,
    act_ref,
    query_ref,
    keyval_ref,
    bias_ref,
    output_ref,
    gather_ref,
    att_ref,
    sems,
):
    copies = []
    for i, (source, target) in enumerate(
        (
            (act_hbm, act_ref),
            (query_hbm, query_ref),
            (keyval_hbm, keyval_ref),
            (bias_hbm, bias_ref),
            (output_hbm, output_ref),
            (gather_hbm, gather_ref),
        )
    ):
        copy = pltpu.make_async_copy(source, target, sems.at[i])
        copy.start()
        copies.append(copy)
    samples, atoms, channels = act_ref.shape
    windows = atoms // WQ
    tokens = norm_ref.shape[1]
    head_width = channels // AH
    scale = 1.0 / math.sqrt(head_width)
    device = lax.axis_index("seq")
    gain = gain_ref[...]
    token_gain = one_row(token_gain_ref[...])
    bias_at = samples * AFTER
    meta_at = bias_at + AH * WQ

    head_of = lane_group(WQ, channels, head_width)
    masks = [(head_of == h).astype(BF16) for h in range(AH)]
    masks32 = [(head_of == h).astype(F32) for h in range(AH)]
    index = lax.broadcasted_iota(jnp.int32, (1, WK), 1)

    meta = after_ref[meta_at : meta_at + META, :].astype(F32)
    indexf = index.astype(F32)
    valid_after = (indexf >= meta[0:1, :]) & (indexf < meta[1:2, :])

    slot = one_row(token_ref[...]) - device * tokens
    own_table = (lax.broadcasted_iota(jnp.int32, (tokens, atoms), 0) == slot).astype(F32)
    own_counts = jnp.sum(own_table, axis=1, keepdims=True)
    own_table = own_table.astype(BF16)
    row = lax.broadcasted_iota(jnp.int32, (tokens, 1), 0)
    remaining = jnp.where(
        row == tokens - 1, count_ref[tokens - 1].astype(F32) - own_counts, jnp.zeros_like(own_counts)
    )
    lane = lax.broadcasted_iota(jnp.int32, (tokens, WQ), 1).astype(F32)
    after_table = (lane < remaining).astype(BF16)
    counts = jnp.maximum(own_counts + remaining, 1.0)

    for copy in copies[:4]:
        copy.wait()
    for s in range(samples):
        extended = jnp.concatenate(
            [
                before_ref[s * BEFORE : (s + 1) * BEFORE, :],
                act_ref[s],
                after_ref[s * AFTER : (s + 1) * AFTER, :],
            ],
            axis=0,
        ).astype(F32)
        normed = layer_norm(extended, gain)
        queries = dot(normed, query_ref[...]).astype(BF16)
        keyvals = dot(normed, keyval_ref[...]).astype(BF16)
        values_ones = jnp.concatenate(
            [keyvals[:, channels:], jnp.ones((keyvals.shape[0], channels), BF16)], axis=1
        )
        for w in range(windows + 1):
            q = queries[BEFORE + WQ * w : BEFORE + WQ * (w + 1), :]
            keys = keyvals[WQ * w : WQ * w + WK, :channels]
            stacked = jnp.concatenate([q * m for m in masks], axis=0)
            scores = dot_nt(stacked, keys) * scale
            if w < windows:
                bias = bias_ref[:, w].reshape(AH * WQ, WK)
                start = (device * windows + w) * WQ - EDGE
                valid = (index >= range_ref[0, w] - start) & (index < range_ref[1, w] - start)
            else:
                bias = after_ref[bias_at : bias_at + AH * WQ, :]
                valid = valid_after
            scores = jnp.where(valid, scores + bias.astype(F32), NEGATIVE)
            exponent = jnp.exp(scores - jnp.max(scores, axis=-1, keepdims=True))
            sums = dot(exponent.astype(BF16), values_ones[WQ * w : WQ * w + WK])
            mixed = sums[:, :channels] / sums[:, channels:]
            attended = mixed[:WQ] * masks32[0]
            for h in range(1, AH):
                attended = attended + mixed[WQ * h : WQ * (h + 1)] * masks32[h]
            att_ref[s, WQ * w : WQ * (w + 1), :] = attended.astype(BF16)
        if s == 0:
            copies[4].wait()
            copies[5].wait()
        merged = dot(att_ref[s], output_ref[...])
        mid = (extended[BEFORE : BEFORE + atoms + WQ, :] + merged).astype(BF16)
        mid_ref[s] = mid[:atoms]
        hidden = jnp.maximum(dot(mid, gather_ref[...]), 0.0).astype(BF16)
        sums = dot(own_table, hidden[:atoms]) + dot(after_table, hidden[atoms:])
        token_act = (sums / counts).astype(BF16)
        tokact_ref[s] = token_act
        norm_ref[s] = layer_norm(token_act.astype(F32), token_gain)


def vmem():
    return pl.BlockSpec(memory_space=pltpu.VMEM)


def smem():
    return pl.BlockSpec(memory_space=pltpu.SMEM)


def anywhere():
    return pl.BlockSpec(memory_space=pl.ANY)


def run_atoms(key_range, counts, before, after, gain, token, token_gain, *arrays):
    samples, atoms, channels = arrays[0].shape
    width = arrays[-1].shape[1]
    tokens = atoms // APT
    return pl.pallas_call(
        atom_kernel,
        out_shape=(
            jax.ShapeDtypeStruct((samples, atoms, channels), BF16),
            jax.ShapeDtypeStruct((samples, tokens, width), BF16),
            jax.ShapeDtypeStruct((samples, tokens, width), BF16),
        ),
        in_specs=[smem()] * 2 + [vmem()] * 5 + [anywhere()] * len(arrays),
        out_specs=(vmem(),) * 3,
        scratch_shapes=[pltpu.VMEM(a.shape, a.dtype) for a in arrays]
        + [
            pltpu.VMEM((samples, atoms + WQ, channels), BF16),
            pltpu.SemaphoreType.DMA((len(arrays),)),
        ],
        compiler_params=pltpu.CompilerParams(vmem_limit_bytes=60 * 2**20),
        cost_estimate=cost(1_000_000),
        name="atoms",
    )(key_range, counts, before, after, gain, token, token_gain, *arrays)


def query_kernel(norm_ref, query_ref, keyval_ref, after_hbm, absorbed_ref):
    samples, tokens, width = norm_ref.shape
    head_size = width // HEADS
    scale = 1.0 / math.sqrt(head_size)
    lanes = GROUP * head_size
    head_of = lane_group(tokens, lanes, head_size)
    masks = [(head_of == h).astype(BF16) for h in range(GROUP)]
    queries = dot(norm_ref[...].reshape(samples * tokens, width), query_ref[...]).astype(BF16)
    for s in range(samples):
        for g in range(HEADS // GROUP):
            columns = slice(lanes * g, lanes * (g + 1))
            q = queries[tokens * s : tokens * (s + 1), columns]
            stacked = jnp.concatenate([q * m for m in masks], axis=0)
            absorbed = dot_nt(stacked, keyval_ref[:, columns]) * scale
            absorbed_ref[s, lanes * g : lanes * (g + 1)] = absorbed.astype(BF16)


def run_queries(norm, token_query, token_keyval, after):
    samples, tokens, width = norm.shape
    return pl.pallas_call(
        query_kernel,
        out_shape=jax.ShapeDtypeStruct((samples, HEADS * tokens, width), BF16),
        in_specs=[vmem()] * 3 + [anywhere()],
        out_specs=vmem(),
        compiler_params=pltpu.CompilerParams(vmem_limit_bytes=16 * 2**20),
        cost_estimate=cost(1000000),
        name="queries",
    )(norm, token_query, token_keyval, after)


def reorder_kernel(near_ref, near_far_ref, other_ref, other_far_ref, bias_ref, turned_ref):
    columns, heads, _, keys = near_ref.shape
    line = keys // 4
    part = line // 4
    place_of = lax.axis_index("samp")
    core, upper = place_of % 2, place_of // (2 * columns)
    for source, which, half in (
        (near_ref, core, upper),
        (near_far_ref, core, 1 - upper),
        (other_ref, 1 - core, upper),
        (other_far_ref, 1 - core, 1 - upper),
    ):
        for column in range(columns):
            for head in range(heads):
                at = (2 * (columns * half + column) + which) * heads + head
                rows = source[column, head]
                bias_ref[at] = rows
                blocks = [
                    rows[:, line * x + part * y : line * x + part * (y + 1)]
                    for y in range(4)
                    for x in range(4)
                ]
                turned_ref[at] = jnp.concatenate(blocks, axis=1)


def run_reorder(parts):
    columns, heads, tokens, keys = parts[0].shape
    shape = jax.ShapeDtypeStruct((4 * columns * heads, tokens, keys), BF16)
    return pl.pallas_call(
        reorder_kernel,
        out_shape=(shape, shape),
        in_specs=[vmem()] * 4,
        out_specs=(vmem(), vmem()),
        compiler_params=pltpu.CompilerParams(vmem_limit_bytes=24 * 2**20),
        cost_estimate=cost(4000000000),
        name="reorder",
    )(*parts)


def place(device, sample):
    x, y = device // 8, (device // 2) % 4
    return x if sample % 2 == 0 else y


def piece_scores(q, piece, bias_ref, group, chunk):
    size = piece.shape[0]
    start = pl.multiple_of(chunk * size, 128)
    bias = bias_ref[GROUP * group : GROUP * (group + 1), :, pl.ds(start, size)]
    return dot_nt(q, piece) + bias.reshape(q.shape[0], size).astype(F32)


def early_kernel(
    absorbed_ref,
    bias0_ref,
    bias1_ref,
    own0_ref,
    low0_ref,
    high0_ref,
    own1_ref,
    low1_ref,
    high1_ref,
    mixed_ref,
    best_ref,
    total_ref,
):
    device = lax.axis_index("seq")
    samples = absorbed_ref.shape[0]
    rows_of = absorbed_ref.shape[1] * GROUP // HEADS
    pieces = ((own0_ref, low0_ref, high0_ref), (own1_ref, low1_ref, high1_ref))
    for s in range(samples):
        here = place(device, s)
        for g in range(HEADS // GROUP):
            rows = slice(rows_of * g, rows_of * (g + 1))
            q = absorbed_ref[s, rows]
            scores = [
                piece_scores(q, piece[...], (bias0_ref, bias1_ref)[s], g, (here + step) % 4)
                for piece, step in zip(pieces[s], (0, 3, 1))
            ]
            best = functools.reduce(
                jnp.maximum, [jnp.max(c, axis=-1, keepdims=True) for c in scores]
            )
            total, mixed = 0.0, 0.0
            for piece, c in zip(pieces[s], scores):
                exponent = jnp.exp(c - best)
                total = total + jnp.sum(exponent, axis=-1, keepdims=True)
                mixed = mixed + dot(exponent.astype(BF16), piece[...])
            mixed_ref[s, rows] = mixed
            best_ref[s, rows] = jnp.broadcast_to(best, (rows_of, 128))
            total_ref[s, rows] = jnp.broadcast_to(total, (rows_of, 128))


def run_early(absorbed, bias0, bias1, pieces):
    samples, rows, width = absorbed.shape
    return pl.pallas_call(
        early_kernel,
        out_shape=(
            jax.ShapeDtypeStruct((samples, rows, width), F32),
            jax.ShapeDtypeStruct((samples, rows, 128), F32),
            jax.ShapeDtypeStruct((samples, rows, 128), F32),
        ),
        in_specs=[vmem()] * (3 + len(pieces)),
        out_specs=(vmem(),) * 3,
        compiler_params=pltpu.CompilerParams(vmem_limit_bytes=18 * 2**20),
        cost_estimate=cost(8000000000),
        name="early",
    )(absorbed, bias0, bias1, *pieces)


def late_kernel(
    absorbed_ref,
    bias0_ref,
    bias1_ref,
    far0_ref,
    far1_ref,
    mixed_ref,
    best_ref,
    total_ref,
    tokact_ref,
    mid_ref,
    token_ref,
    gain_ref,
    keyval_ref,
    output_ref,
    gate_ref,
    down_ref,
    back_ref,
    atom_out_ref,
    token_out_ref,
    back_rows_ref,
    att_ref,
):
    samples, tokens, width = tokact_ref.shape
    head_size = width // HEADS
    device = lax.axis_index("seq")
    lanes = GROUP * head_size
    head_of = lane_group(tokens, lanes, head_size)
    masks32 = [(head_of == h).astype(F32) for h in range(GROUP)]
    for s in range(samples):
        far = (place(device, s) + 2) % 4
        piece = (far0_ref, far1_ref)[s][...]
        for g in range(HEADS // GROUP):
            columns = slice(lanes * g, lanes * (g + 1))
            scores = piece_scores(absorbed_ref[s, columns], piece, (bias0_ref, bias1_ref)[s], g, far)
            before = best_ref[s, columns][:, :1]
            best = jnp.maximum(before, jnp.max(scores, axis=-1, keepdims=True))
            exponent = jnp.exp(scores - best)
            shrink = jnp.exp(before - best)
            total = total_ref[s, columns][:, :1] * shrink + jnp.sum(
                exponent, axis=-1, keepdims=True
            )
            mixed = mixed_ref[s, columns] * shrink + dot(exponent.astype(BF16), piece)
            mixed = mixed / total
            value_at = slice(width + lanes * g, width + lanes * (g + 1))
            valued = dot(mixed.astype(BF16), keyval_ref[:, value_at])
            attended = valued[:tokens] * masks32[0]
            for h in range(1, GROUP):
                attended = attended + valued[tokens * h : tokens * (h + 1)] * masks32[h]
            att_ref[tokens * s : tokens * (s + 1), columns] = attended.astype(BF16)

    merged = dot(att_ref[...], output_ref[...])
    token_act = tokact_ref[...].reshape(samples * tokens, width).astype(F32)
    token_mid = (token_act + merged).astype(BF16).astype(F32)
    trans = layer_norm(token_mid, one_row(gain_ref[...]))
    hidden_width = down_ref.shape[0]
    gate = dot(trans, gate_ref[:, :hidden_width])
    up = dot(trans, gate_ref[:, hidden_width:])
    hidden = (gate / (1.0 + jnp.exp(-gate)) * up).astype(BF16)
    token_out = (token_mid + dot(hidden, down_ref[...])).astype(BF16)
    token_out_ref[...] = token_out.reshape(samples, tokens, width)
    back_rows = dot(token_out, back_ref[...]).astype(BF16)
    back_rows_ref[...] = back_rows.reshape(samples, tokens, -1)
    atoms = mid_ref.shape[1]
    slot = one_row(token_ref[...]) - device * tokens
    table = (lax.broadcasted_iota(jnp.int32, (tokens, atoms), 0) == slot).astype(BF16)
    for s in range(samples):
        gathered = dot_tn(table, back_rows[tokens * s : tokens * (s + 1)])
        atom_out_ref[s] = (mid_ref[s].astype(F32) + gathered).astype(BF16)


def run_late(absorbed, bias0, bias1, far, early, tokact, mid, token, gain, weights):
    samples, tokens, width = tokact.shape
    return pl.pallas_call(
        late_kernel,
        out_shape=(
            jax.ShapeDtypeStruct(mid.shape, BF16),
            jax.ShapeDtypeStruct(tokact.shape, BF16),
            jax.ShapeDtypeStruct((samples, tokens, mid.shape[2]), BF16),
        ),
        in_specs=[vmem()] * 17,
        out_specs=(vmem(),) * 3,
        scratch_shapes=[pltpu.VMEM((samples * tokens, width), BF16)],
        compiler_params=pltpu.CompilerParams(vmem_limit_bytes=18 * 2**20),
        cost_estimate=cost(5_000_000_000),
        name="late",
    )(absorbed, bias0, bias1, *far, *early, tokact, mid, token, gain, *weights)


def shifted(value, dx, dy):
    pairs = []
    for t in range(32):
        x, y, z = t // 8, (t // 2) % 4, t % 2
        pairs.append((t, ((x + dx) % 4) * 8 + ((y + dy) % 4) * 2 + z))
    return lax.ppermute(value, "seq", pairs)


def exchanged(value, axis, bit):
    return lax.ppermute(value, axis, [(t, t ^ (1 << bit)) for t in range(lax.axis_size(axis))])


def join_kernel(axis, bits, *refs):
    count = len(bits)
    device = lax.axis_index(axis)
    for own, other, joined, bit in zip(refs, refs[count:], refs[-count:], bits):
        rows = joined.shape[0] // 2
        where = (device // (1 << bit)) % 2
        joined[pl.ds(pl.multiple_of(where * rows, 16), rows)] = own[...]
        joined[pl.ds(pl.multiple_of((1 - where) * rows, 16), rows)] = other[...]


def joined(own, other, axis, bits, after=()):
    rows, width = own[0].shape
    shape = jax.ShapeDtypeStruct((2 * rows, width), BF16)
    return pl.pallas_call(
        functools.partial(join_kernel, axis, bits),
        out_shape=(shape,) * len(bits),
        in_specs=[vmem()] * (2 * len(bits)) + [anywhere()] * len(after),
        out_specs=(vmem(),) * len(bits),
        compiler_params=pltpu.CompilerParams(vmem_limit_bytes=16 * 2**20),
        cost_estimate=cost(1_000_000),
        name="join",
    )(*own, *other, *after)


def spread(norm, bias):
    other = exchanged(norm, "seq", 0)
    heads = all_heads(bias, other)
    lines = joined([norm[0], norm[1]], [other[0], other[1]], "seq", (0, 0))
    for bits, after in (((1, 3), ()), ((2, 4), (heads[2],))):
        turned = [exchanged(v, "seq", b) for v, b in zip(lines, bits)]
        lines = joined(lines, turned, "seq", bits, after)
    near, far = [], []
    for value, dx, dy in ((lines[0], 1, 0), (lines[1], 0, 1)):
        low = shifted(value, dx, dy)
        near.append((value, low, shifted(value, -dx, -dy)))
        far.append(shifted(low, dx, dy))
    return near, far, heads


def all_heads(bias, ready):
    heads, tokens, keys = bias.shape
    rows = bias.reshape(heads * tokens, keys)
    (pair,) = joined([rows], [exchanged(rows, "samp", 1)], "samp", (1,), (ready,))
    other_pair = exchanged(pair, "samp", 0)
    beyond = exchanged(pair, "samp", 2)
    parts = (pair, beyond, other_pair, exchanged(beyond, "samp", 0))
    return [part.reshape(2, heads, tokens, keys) for part in parts]


def per_device(
    atom_act,
    atom_gain,
    atom_query,
    atom_keyval,
    atom_output,
    atom_bias,
    key_range,
    atom_token,
    token_counts,
    gather_weight,
    token_gain,
    token_query,
    token_keyval,
    token_output,
    pair_bias,
    trans_gain,
    trans_gate_up,
    trans_down,
    back_weight,
):
    samples, atoms, channels = atom_act.shape
    tokens = token_counts.shape[0]
    device = lax.axis_index("seq")
    count = lax.axis_size("seq")
    to_next = [(i, i + 1) for i in range(count - 1)]
    to_previous = [(i + 1, i) for i in range(count - 1)]

    ranges = key_range.T
    first, last = run_pack(ranges, atom_act, atom_bias)
    after = lax.ppermute(first, "seq", to_previous)
    before = lax.ppermute(last, "seq", to_next)
    token_row = atom_token.reshape(-1, 128)
    atom_mid, token_act, token_norm = run_atoms(
        ranges,
        token_counts,
        before,
        after,
        atom_gain.reshape(1, -1),
        token_row,
        token_gain.reshape(-1, 128),
        atom_act,
        atom_query,
        atom_keyval,
        atom_bias,
        atom_output,
        gather_weight,
    )
    near, far, heads = spread(token_norm, pair_bias)
    absorbed = run_queries(token_norm, token_query, token_keyval, token_norm)
    bias, turned = run_reorder(heads)
    early = run_early(absorbed, bias, turned, near[0] + near[1])
    atom_out, token_out, back_rows = run_late(
        absorbed,
        bias,
        turned,
        far,
        early,
        token_act,
        atom_mid,
        token_row,
        trans_gain.reshape(-1, 128),
        [token_keyval, token_output, trans_gate_up, trans_down, back_weight],
    )
    previous = lax.ppermute(back_rows[:, tokens - 1], "seq", to_next)
    earlier = (atom_token[:APT] < device * tokens)[None, :, None]
    extra = jnp.where(earlier, previous[:, None, :].astype(F32), 0.0)
    head = (atom_out[:, :APT].astype(F32) + extra).astype(BF16)
    atom_out = lax.dynamic_update_slice(atom_out, head, (0, 0, 0))
    return (atom_out, token_out)


def solution(mesh):
    placed = (
        P("samp", "seq", None),
        P(),
        P(),
        P(),
        P(),
        P(None, "seq", None, None),
        P("seq", None),
        P("seq"),
        P("seq"),
        P(),
        P(),
        P(),
        P(),
        P(),
        P("samp", "seq", None),
        P(),
        P(),
        P(),
        P(),
    )
    return jax.shard_map(
        per_device,
        mesh=mesh,
        in_specs=placed,
        out_specs=(P("samp", "seq", None), P("samp", "seq", None)),
        check_vma=False,
    )
```
